256 devices in a mesh: lat: 8 (over y_lo, x), lon: 32 (over z, y_hi, core).
Axes of the slice: x: 4, y: 4 (y_hi: 2, y_lo: 2; y = y_hi * 2 + y_lo), z: 8, core: 2. Of those that a mesh axis runs over, the one named last changes fastest.
Arguments:
- background: bfloat16 [69, 64, 32, 8, 128], P(None, None, 'lon', 'lat'), may hold values from -6 to 6
- obs_ens: bfloat16 [4, 8, 32, 32, 64, 128], P(None, 'lat', 'lon'), may hold values from -6 to 6
- obs_value: bfloat16 [4, 8, 32, 32, 128], P(None, 'lat', 'lon'), may hold values from -10 to 10
- obs_prec: bfloat16 [4, 8, 32, 32, 128], P(None, 'lat', 'lon'), may hold values from 0.019897461 to 0.5
- obs_count: int32 [4, 8, 32], P(None, 'lat', 'lon'), may hold values from 32 to 128, as said below
- slot_owner: int32 [4], replicated, may hold values from 0 to 31
- region_slots: int32 [64, 128, 2], P('lon', 'lat'), may hold values from 0 to 3, as said below
Outputs:
- analysis: bfloat16 [69, 64, 32, 8, 128], P(None, None, 'lon', 'lat')
The draws below stay inside these ranges and needn't reach their ends.
Inputs may be any that keep to these rules, and one draw needn't show every extreme that they name: The first obs_count entries of a patch's block in a slot are live; the largest value 128 occurs in every draw. `region_slots`: the 2 slots of a region are distinct.
All inputs are finite; a program needn't handle non-finite values.
Results may differ from the reference program's by a relative error of at most 0.0095.
Values may be sent and summed in bfloat16 or wider, within the bound.
No kernel may reach another device: no remote copies, remote signals or barrier semaphores. Data moves between devices by JAX's collectives and lax.ppermute only.
A program may use at most 64 MiB of HBM per device.

```python
import math
import jax
import jax.numpy as jnp
from jax import lax

MEMBERS = 64
FIELDS = 69
CELLS_LAT = 32
CELLS_LON = 4
OBS_BLOCK = 128
SLOTS = 4
SLOTS_USED = 2
NEWTON_STEPS = 3
GRID_LAT = 256
GRID_LON = 128
REG_LAT = 128
REG_LON = 64
PATCH_CELLS = 128
N_LAT = 8
N_LON = 32


def draw_obs_count(key, part):
    key = jax.random.fold_in(key, 11)
    count_key, place_key = jax.random.split(key)
    counts = jax.random.randint(count_key, (SLOTS, N_LAT, N_LON), OBS_BLOCK // 4, OBS_BLOCK + 1)
    flattened = counts.reshape(-1)
    location = jax.random.randint(place_key, (), 0, flattened.shape[0])
    flattened = flattened.at[location].set(OBS_BLOCK)
    return flattened.reshape(SLOTS, N_LAT, N_LON).astype(jnp.int32)


def draw_region_slots(key, part):
    key = jax.random.fold_in(key, 23)
    scores = jax.random.randint(key, (REG_LON, REG_LAT, SLOTS), 0, 4096)
    distinct = scores * SLOTS + lax.broadcasted_iota(jnp.int32, (REG_LON, REG_LAT, SLOTS), 2)
    ranking = jnp.argsort(distinct, axis=-1, stable=True)
    return ranking[..., :SLOTS_USED].astype(jnp.int32)


def plant(drawn, rng, least, high):
    extent = drawn.shape
    index_at = [jax.random.randint(jax.random.fold_in(rng, axis), (), 0, extent[axis]) for axis in range(len(extent))]
    drawn = drawn.at[tuple(index_at)].set(least)
    longest = extent.index(max(extent))
    index_at[longest] = (index_at[longest] + 1) % extent[longest]
    return drawn.at[tuple(index_at)].set(high)


def block_levels(key, dims, cuts, least, top_value):
    loudness = 1.0
    for dim, blocks in cuts:
        heights = jax.random.uniform(jax.random.fold_in(jax.random.fold_in(key, 6), dim), (blocks,), jnp.float32, least / len(cuts), top_value / len(cuts))
        loudness = loudness * jnp.repeat(jnp.exp(heights), dims[dim] // blocks).reshape((-1,) + (1,) * (len(dims) - 1 - dim))
    return loudness


def noise(own_key, extent, spread, bound, shards=(), kind=jnp.bfloat16):
    entries = jax.random.normal(own_key, extent, jnp.float32) * spread
    if len(shards) > 0:
        entries = block_levels(own_key, extent, shards, -0.22, 0.18) * entries
    return jnp.clip(entries, min=-bound, max=bound).astype(kind)


def setup_inputs(seed: int = 0) -> dict:
    splits = jax.random.split(jax.random.key(seed), 8)
    return {
        "background": noise(splits[0], (FIELDS, MEMBERS, N_LON, N_LAT, PATCH_CELLS), 1.0, 6.0, ((2, 32), (3, 8))),
        "obs_ens": noise(splits[1], (SLOTS, N_LAT, N_LON, N_LON, MEMBERS, OBS_BLOCK), 1.0, 6.0, ((1, 8), (2, 32))),
        "obs_value": noise(splits[2], (SLOTS, N_LAT, N_LON, N_LON, OBS_BLOCK), 2.0, 10.0, ((1, 8), (2, 32))),
        "obs_prec": jnp.clip(jnp.exp(math.log(0.5) - 3.224016 * jax.random.uniform(splits[3], (SLOTS, N_LAT, N_LON, N_LON, OBS_BLOCK), jnp.float32) ** block_levels(splits[3], (SLOTS, N_LAT, N_LON, N_LON, OBS_BLOCK), ((1, 8), (2, 32)), -0.2, 0.2)), 0.019897461, 0.5).astype(jnp.bfloat16),
        "obs_count": draw_obs_count(jax.random.fold_in(splits[7], 71), 0),
        "slot_owner": plant(jax.random.randint(splits[5], (SLOTS,), 0, N_LON), jax.random.fold_in(splits[5], 1), 0, N_LON - 1).astype(jnp.int32),
        "region_slots": draw_region_slots(jax.random.fold_in(splits[7], 71), 0),
    }


exact_mode = lax.Precision.HIGHEST
TABLE_OWN = (((1, 0.75), (0, 0.25)), ((2, 0.25), (1, 0.75)))

def slot_grams(ens_block, value_block, prec_block, live_count):
    ens_float = ens_block.astype(jnp.float32)
    obs_mean = lax.optimization_barrier(jnp.mean(ens_float, axis=-2))
    obs_pert = (ens_float - obs_mean[..., None, :]).astype(jnp.bfloat16)
    position = lax.broadcasted_iota(jnp.int32, value_block.shape, value_block.ndim - 1)
    weight = jnp.where(position < live_count[..., None], prec_block.astype(jnp.float32), 0.0)
    weighted = (obs_pert.astype(jnp.float32) * weight[..., None, :]).astype(jnp.bfloat16)
    gram_slot = jnp.einsum('...ko,...jo->...kj', weighted.astype(jnp.float32), obs_pert.astype(jnp.float32), precision=exact_mode)
    innovation = value_block.astype(jnp.float32) - obs_mean
    projected = lax.optimization_barrier(jnp.sum(weighted.astype(jnp.float32) * innovation[..., None, :], axis=-1))
    return (gram_slot, projected)

def region_transform(gram_sum, proj_sum, newton_steps):
    members = gram_sum.shape[-1]
    identity = jnp.eye(members, dtype=jnp.float32)
    matrix = gram_sum + (members - 1.0) * identity
    scaling = jnp.trace(matrix, axis1=-2, axis2=-1) / members
    iterate = matrix / scaling[..., None, None]
    inverse = jnp.broadcast_to(identity, matrix.shape)
    for step_index in range(newton_steps):
        factor = 1.5 * identity - 0.5 * jnp.einsum('...ij,...jk->...ik', inverse, iterate, precision=exact_mode)
        iterate = jnp.einsum('...ij,...jk->...ik', iterate, factor, precision=exact_mode)
        inverse = jnp.einsum('...ij,...jk->...ik', factor, inverse, precision=exact_mode)
    root_inv = inverse / jnp.sqrt(scaling)[..., None, None]
    inner_part = jnp.einsum('...ij,...j->...i', root_inv, proj_sum, precision=exact_mode)
    mean_weight = jnp.einsum('...ij,...j->...i', root_inv, inner_part, precision=exact_mode)
    transform = math.sqrt(members - 1.0) * root_inv + mean_weight[..., :, None]
    return transform.astype(jnp.bfloat16)

def interpolate(pert_cells, padded, tapers):
    lon_len = pert_cells.shape[2]
    lat_len = pert_cells.shape[4]
    lon_parts = []
    for lon_par in range(2):
        lat_parts = []
        for lat_par in range(2):
            quarter = pert_cells[:, :, :, lon_par, :, lat_par].astype(jnp.float32)
            summed = jnp.zeros(quarter.shape, jnp.float32)
            for lon_off, lon_w in tapers[lon_par]:
                for lat_off, lat_w in tapers[lat_par]:
                    window = padded[lon_off:lon_off + lon_len, lat_off:lat_off + lat_len].astype(jnp.float32)
                    product = jnp.einsum('vklm,lmkj->vjlm', quarter, window)
                    summed = summed + lon_w * lat_w * product
            lat_parts.append(summed)
        lon_parts.append(jnp.stack(lat_parts, axis=-1))
    return jnp.stack(lon_parts, axis=3)

def to_grid(patches):
    fields_n = patches.shape[0]
    members_n = patches.shape[1]
    shaped = patches.reshape(fields_n, members_n, N_LON, N_LAT, CELLS_LON, CELLS_LAT)
    return jnp.transpose(shaped, (0, 1, 2, 4, 3, 5)).reshape(fields_n, members_n, GRID_LON, GRID_LAT)

def to_patches(grid):
    fields_n = grid.shape[0]
    members_n = grid.shape[1]
    shaped = grid.reshape(fields_n, members_n, N_LON, CELLS_LON, N_LAT, CELLS_LAT)
    return jnp.transpose(shaped, (0, 1, 2, 4, 3, 5)).reshape(fields_n, members_n, N_LON, N_LAT, CELLS_LON * CELLS_LAT)

def reference(background, obs_ens, obs_value, obs_prec, obs_count, slot_owner, region_slots):
    state = to_grid(background)
    picked_ens = []
    picked_value = []
    picked_prec = []
    for slot_index in range(SLOTS):
        slot_root = slot_owner[slot_index]
        picked_ens.append(lax.dynamic_index_in_dim(obs_ens[slot_index], slot_root, axis=1, keepdims=False))
        picked_value.append(lax.dynamic_index_in_dim(obs_value[slot_index], slot_root, axis=1, keepdims=False))
        picked_prec.append(lax.dynamic_index_in_dim(obs_prec[slot_index], slot_root, axis=1, keepdims=False))
    gram_all, proj_all = slot_grams(jnp.stack(picked_ens), jnp.stack(picked_value), jnp.stack(picked_prec), obs_count)
    lon_pairs = CELLS_LON // 2
    lat_pairs = CELLS_LAT // 2

    def column(region_lon):
        patch_lon = region_lon // lon_pairs
        gram_col = jnp.repeat(lax.dynamic_index_in_dim(gram_all, patch_lon, axis=2, keepdims=False), lat_pairs, axis=1)
        proj_col = jnp.repeat(lax.dynamic_index_in_dim(proj_all, patch_lon, axis=2, keepdims=False), lat_pairs, axis=1)
        chosen = lax.dynamic_index_in_dim(region_slots, region_lon, axis=0, keepdims=False)
        gram_sum = jnp.zeros(gram_col.shape[1:], jnp.float32)
        proj_sum = jnp.zeros(proj_col.shape[1:], jnp.float32)
        for slot_index in range(SLOTS):
            member = lax.optimization_barrier(jnp.sum((chosen == slot_index).astype(jnp.float32), axis=-1))
            gram_sum = gram_sum + member[:, None, None] * gram_col[slot_index]
            proj_sum = proj_sum + member[:, None] * proj_col[slot_index]
        return region_transform(gram_sum, proj_sum, NEWTON_STEPS)
    transforms = lax.map(column, jnp.arange(REG_LON, dtype=jnp.int32))
    back_float = state.astype(jnp.float32)
    back_mean = lax.optimization_barrier(jnp.mean(back_float, axis=1, keepdims=True))
    pert = (back_float - back_mean).astype(jnp.bfloat16)
    wrapped = jnp.concatenate([transforms[-1:], transforms, transforms[:1]], axis=0)
    padded = jnp.pad(wrapped, ((0, 0), (1, 1), (0, 0), (0, 0)))
    pert_cells = pert.reshape(FIELDS, MEMBERS, REG_LON, 2, REG_LAT, 2)
    mean_cells = back_mean.reshape(FIELDS, 1, REG_LON, 2, REG_LAT, 2)

    def lon_band(region_lon):
        cell_block = lax.dynamic_slice_in_dim(pert_cells, region_lon, 1, axis=2)
        window = lax.dynamic_slice_in_dim(padded, region_lon, 3, axis=0)
        increment = interpolate(cell_block, window, TABLE_OWN)
        mean_block = lax.dynamic_slice_in_dim(mean_cells, region_lon, 1, axis=2)
        return (mean_block + increment).astype(jnp.bfloat16)
    bands = lax.map(lon_band, jnp.arange(REG_LON, dtype=jnp.int32))
    grid_out = jnp.moveaxis(bands[:, :, :, 0], 0, 2).reshape(FIELDS, MEMBERS, GRID_LON, GRID_LAT)
    return to_patches(grid_out)
```

```python
import math

import jax
import jax.numpy as jnp
import numpy as np
from jax import lax
from jax.experimental import pallas as pl
from jax.experimental.pallas import tpu as pltpu
from jax.sharding import PartitionSpec as P

MEMBERS = 64
FIELDS = 69
CELLS_LAT = 32
CELLS_LON = 4
PATCH_CELLS = 128
SLOTS = 4
OBS_BLOCK = 128
NEWTON_STEPS = 3
LON_PAIRS = 2
LAT_PAIRS = 16
PAIRS = ((0, 1), (0, 2), (0, 3), (1, 2), (1, 3), (2, 3))
BITS = (0, 1, 2, 3, 4)
ROWS = 66
PAIR_ROWS = 192
EDGE_ROWS = 64
COEF_ROWS = 16
MSG_ROWS = PAIR_ROWS + 2 * EDGE_ROWS + COEF_ROWS


def lon_weight(column, region):
    if column // 2 == region:
        return 0.75
    outer = column // 2 + (1 if column % 2 else -1)
    return 0.25 if outer == region else 0.0


def lat_weight(row, region):
    if row // 2 == region:
        return 0.75
    outer = row // 2 + (1 if row % 2 else -1)
    return 0.25 if outer == region else 0.0


def taper_tables():
    table = np.zeros((LON_PAIRS * LAT_PAIRS, 2 * PATCH_CELLS), np.float32)
    for a in range(LON_PAIRS):
        for b in range(LAT_PAIRS):
            for col in range(CELLS_LON):
                for row in range(CELLS_LAT):
                    cell = col * CELLS_LAT + row
                    lat_w = lat_weight(row, b)
                    table[a * LAT_PAIRS + b, cell] = lon_weight(col, a) * lat_w
                    if col == 0:
                        lon_w = lon_weight(col, a - LON_PAIRS)
                    elif col == CELLS_LON - 1:
                        lon_w = lon_weight(col, a + LON_PAIRS)
                    else:
                        lon_w = 0.0
                    table[a * LAT_PAIRS + b, PATCH_CELLS + cell] = lon_w * lat_w
    sides = np.zeros((2, 2, 3, COEF_ROWS, PATCH_CELLS), np.float32)
    for lat_par in range(2):
        for which in range(2):
            upper = (which == 0) == (lat_par == 0)
            row = CELLS_LAT - 1 if upper else 0
            for lon_par in range(2):
                for source in range(3):
                    if source == 0:
                        shift = 0
                    else:
                        right = (source == 1) == (lon_par == 0)
                        shift = LON_PAIRS if right else -LON_PAIRS
                    for a in range(LON_PAIRS):
                        for col in range(CELLS_LON):
                            sides[lat_par, lon_par, source, 6 + 2 * which + a, col * CELLS_LAT + row] = (
                                0.25 * lon_weight(col, a + shift)
                            )
    masks = np.zeros((2, 2, COEF_ROWS, PATCH_CELLS), np.float32)
    for lon_par in range(2):
        for source in range(2):
            right = (source == 0) == (lon_par == 0)
            first = (CELLS_LON - 1) * CELLS_LAT if right else 0
            masks[lon_par, source, :6, first : first + CELLS_LAT] = 1.0
    return table, sides, masks


TABLE, SIDES, MASKS = taper_tables()


def mm(left, right):
    return lax.dot_general(
        left,
        right,
        (((1,), (0,)), ((), ())),
        precision=lax.Precision.HIGHEST,
        preferred_element_type=jnp.float32,
    )


def transform_kernel(count_ref, edge_ref, block_ref, pair_ref, edges_ref, held_ref):
    f32 = jnp.float32
    members = MEMBERS
    row_id = lax.broadcasted_iota(jnp.int32, (members, members), 0)
    col_id = lax.broadcasted_iota(jnp.int32, (members, members), 1)
    identity = jnp.where(row_id == col_id, 1.0, 0.0).astype(f32)
    position = lax.broadcasted_iota(jnp.int32, (1, OBS_BLOCK), 1)
    grams = []
    projs = []
    for slot in range(SLOTS):
        block = block_ref[slot].astype(f32)
        ens = block[:members]
        value = block[members : members + 1]
        prec = block[members + 1 : members + 2]
        obs_mean = jnp.sum(ens, axis=0, keepdims=True) * (1.0 / members)
        pert = (ens - obs_mean).astype(jnp.bfloat16)
        weight = jnp.where(position < count_ref[slot], prec, 0.0)
        weighted = (pert.astype(f32) * weight).astype(jnp.bfloat16)
        grams.append(
            lax.dot_general(
                weighted, pert, (((1,), (1,)), ((), ())), preferred_element_type=f32
            )
        )
        innovation = value - obs_mean
        projs.append(jnp.sum(weighted.astype(f32) * innovation, axis=1, keepdims=True))
    inverses = []
    iterates = []
    scalings = []
    for first, second in PAIRS:
        matrix = grams[first] + grams[second] + (members - 1.0) * identity
        trace = jnp.sum(jnp.sum(matrix * identity, axis=1, keepdims=True), axis=0, keepdims=True)
        scaling = trace * (1.0 / members)
        scalings.append(scaling)
        iterate = matrix / scaling
        inverses.append(1.5 * identity - 0.5 * iterate)
        iterates.append(iterate)
    iterates = [mm(x, y) for x, y in zip(iterates, inverses)]
    for step in range(1, NEWTON_STEPS):
        factors = [1.5 * identity - 0.5 * mm(y, x) for x, y in zip(iterates, inverses)]
        if step < NEWTON_STEPS - 1:
            iterates = [mm(x, f) for x, f in zip(iterates, factors)]
        inverses = [mm(f, y) for f, y in zip(factors, inverses)]
    roots = [y / jnp.sqrt(s) for y, s in zip(inverses, scalings)]
    sums = [projs[first] + projs[second] for first, second in PAIRS]
    inner = [mm(r, jnp.broadcast_to(p, (members, members))) for r, p in zip(roots, sums)]
    means = [mm(r, p) for r, p in zip(roots, inner)]
    for pair in range(len(PAIRS)):
        transform = math.sqrt(members - 1.0) * roots[pair] + means[pair]
        turned = transform.T
        held_ref[pair] = turned
        half = pair % 2
        pair_ref[pair // 2, :, half * members : (half + 1) * members] = turned.astype(jnp.bfloat16)
    for which in range(2):
        for a in range(LON_PAIRS):
            chosen = held_ref[edge_ref[2 * which + a]]
            edges_ref[which, :, a * members : (a + 1) * members] = chosen.astype(jnp.bfloat16)


def transforms_of(counts, edge_ids, blocks):
    smem = pl.BlockSpec(memory_space=pltpu.SMEM)
    vmem = pl.BlockSpec(memory_space=pltpu.VMEM)
    return pl.pallas_call(
        transform_kernel,
        out_shape=(
            jax.ShapeDtypeStruct((3, MEMBERS, 2 * MEMBERS), jnp.bfloat16),
            jax.ShapeDtypeStruct((2, MEMBERS, 2 * MEMBERS), jnp.bfloat16),
        ),
        in_specs=[smem, smem, vmem],
        out_specs=(vmem, vmem),
        scratch_shapes=[pltpu.VMEM((len(PAIRS), MEMBERS, MEMBERS), jnp.float32)],
        compiler_params=pltpu.CompilerParams(vmem_limit_bytes=16 * 1024 * 1024),
        name="transforms",
    )(counts, edge_ids, blocks)


def analysis_kernel(own_ref, side_ref, other_ref, coef_ref, mask_ref, back_ref, out_ref, left_ref, weight_ref):
    f32 = jnp.float32
    bf16 = jnp.bfloat16
    tiles = (MSG_ROWS - COEF_ROWS) // MEMBERS
    coef_rows = MSG_ROWS - COEF_ROWS
    for source, ref in enumerate((own_ref, side_ref, other_ref)):
        for tile in range(tiles):
            at = (source * tiles + tile) * 2 * MEMBERS
            left_ref[:, at : at + 2 * MEMBERS] = ref[tile * MEMBERS : (tile + 1) * MEMBERS, :]
        if source == 0:
            weight_ref[source] = coef_ref[source].astype(f32)
        else:
            weight_ref[source] = coef_ref[source].astype(f32) + ref[coef_rows:, :].astype(f32) * mask_ref[
                source - 1
            ].astype(f32)

    def fields(first, count):
        perts = []
        means = []
        for f in range(count):
            state = back_ref[first + f].astype(f32)
            mean = jnp.sum(state, axis=0, keepdims=True) * (1.0 / MEMBERS)
            means.append(mean)
            perts.append((state - mean).astype(bf16))
        parts = []
        for source in range(3):
            for k in range(2 * tiles):
                weight = weight_ref[source, k : k + 1, :].astype(bf16)
                parts.append(jnp.concatenate([p * weight for p in perts], axis=1))
        right = jnp.concatenate(parts, axis=0)
        total = lax.dot_general(
            left_ref[...], right, (((1,), (0,)), ((), ())), preferred_element_type=f32
        )
        for f in range(count):
            piece = total[:, f * PATCH_CELLS : (f + 1) * PATCH_CELLS]
            out_ref[first + f] = (piece + means[f]).astype(bf16)

    def step(index, carry):
        fields(index * 2, 2)
        return carry

    lax.fori_loop(0, FIELDS // 2, step, 0)
    if FIELDS % 2:
        fields(FIELDS - 1, 1)


def analysis_of(own, side, other, coefs, masks, background):
    vmem = pl.BlockSpec(memory_space=pltpu.VMEM)
    depth = 3 * (MSG_ROWS - COEF_ROWS) // MEMBERS * 2 * MEMBERS
    return pl.pallas_call(
        analysis_kernel,
        out_shape=jax.ShapeDtypeStruct((FIELDS, MEMBERS, PATCH_CELLS), jnp.bfloat16),
        in_specs=[vmem] * 6,
        out_specs=vmem,
        scratch_shapes=[
            pltpu.VMEM((MEMBERS, depth), jnp.bfloat16),
            pltpu.VMEM((3, COEF_ROWS, PATCH_CELLS), jnp.float32),
        ],
        compiler_params=pltpu.CompilerParams(vmem_limit_bytes=32 * 1024 * 1024),
        name="analysis",
    )(own, side, other, coefs, masks, background)


def scatter_blocks(obs_ens, obs_value, obs_prec, slot_owner, lon_index):
    small = jnp.stack([obs_value[:, 0, 0], obs_prec[:, 0, 0]], axis=2)
    blocks = jnp.concatenate([obs_ens[:, 0, 0], small], axis=2)
    blocks = blocks.reshape((SLOTS, 2, 2, 2, 2, 2, ROWS, OBS_BLOCK))
    axes = {0: 5, 1: 4, 2: 3, 3: 2, 4: 1}
    for bit in BITS:
        axis = axes[bit]
        mine = (lon_index >> bit) & 1
        keep = lax.dynamic_index_in_dim(blocks, mine, axis, keepdims=False)
        send = lax.dynamic_index_in_dim(blocks, 1 - mine, axis, keepdims=False)
        got = lax.ppermute(send, "lon", [(i, i ^ (1 << bit)) for i in range(32)])
        held = ((slot_owner >> bit) & 1) == mine
        blocks = jnp.where(held.reshape((SLOTS,) + (1,) * (keep.ndim - 1)), keep, got)
        axes = {b: (d - 1 if d > axis else d) for b, d in axes.items()}
    return blocks.reshape(SLOTS, ROWS, OBS_BLOCK)


def shards(background, obs_ens, obs_value, obs_prec, obs_count, slot_owner, region_slots):
    lon_index = lax.axis_index("lon")
    lat_index = lax.axis_index("lat")
    lon_par = lon_index & 1
    lat_par = lat_index & 1

    low = jnp.min(region_slots, axis=-1)
    high = jnp.max(region_slots, axis=-1)
    ids = ((low * (7 - low)) >> 1) + (high - low - 1)
    edge_top = ids[:, 0]
    edge_bottom = ids[:, LAT_PAIRS - 1]
    even = lat_par == 0
    edge_ids = jnp.concatenate(
        [jnp.where(even, edge_bottom, edge_top), jnp.where(even, edge_top, edge_bottom)]
    )
    one_hot = (
        lax.broadcasted_iota(jnp.int32, (COEF_ROWS, LON_PAIRS * LAT_PAIRS), 0) == ids.reshape(1, -1)
    ).astype(jnp.bfloat16)
    tapers = lax.dot_general(
        one_hot,
        jnp.asarray(TABLE, jnp.bfloat16),
        (((1,), (0,)), ((), ())),
        preferred_element_type=jnp.float32,
    ).astype(jnp.bfloat16)
    own_taper = tapers[:, :PATCH_CELLS]
    next_taper = tapers[:, PATCH_CELLS:]
    sides = jnp.asarray(SIDES, jnp.bfloat16)[lat_par, lon_par]
    coefs = jnp.concatenate([(sides[0] + own_taper)[None], sides[1:]], axis=0)
    masks = jnp.asarray(MASKS, jnp.bfloat16)[lon_par]

    blocks = scatter_blocks(obs_ens, obs_value, obs_prec, slot_owner, lon_index)
    pair_tiles, edges = transforms_of(obs_count[:, 0, 0], edge_ids, blocks)

    pairs_a = [(i, i ^ 1) for i in range(8)]
    pairs_b = [(i, i + 1) for i in range(1, 7, 2)] + [(i + 1, i) for i in range(1, 7, 2)]
    lat_a = lax.ppermute(edges[0], "lat", pairs_a)
    lat_b = lax.ppermute(edges[1], "lat", pairs_b)
    message = jnp.concatenate(
        [pair_tiles.reshape(PAIR_ROWS, 2 * MEMBERS), lat_a, lat_b, next_taper], axis=0
    )
    swap = [(i, (i + 1) % 32) for i in range(1, 32, 2)] + [((i + 1) % 32, i) for i in range(1, 32, 2)]
    from_core = lax.ppermute(message, "lon", [(i, i ^ 1) for i in range(32)])
    from_next = lax.ppermute(message, "lon", swap)
    state = background.reshape(FIELDS, MEMBERS, PATCH_CELLS)
    result = analysis_of(message, from_core, from_next, coefs, masks, state)
    return result.reshape(FIELDS, MEMBERS, 1, 1, PATCH_CELLS)


def solution(mesh):
    in_specs = (
        P(None, None, "lon", "lat", None),
        P(None, "lat", "lon", None, None, None),
        P(None, "lat", "lon", None, None),
        P(None, "lat", "lon", None, None),
        P(None, "lat", "lon"),
        P(),
        P("lon", "lat", None),
    )
    out_specs = P(None, None, "lon", "lat", None)
    return jax.shard_map(shards, mesh=mesh, in_specs=in_specs, out_specs=out_specs, check_vma=False)
```

```python
import functools
import math

import jax
import jax.numpy as jnp
import numpy as np
from jax import lax
from jax.experimental import pallas as pl
from jax.experimental.pallas import tpu as pltpu
from jax.sharding import PartitionSpec as P

MEMBERS = 64
FIELDS = 69
CELLS_LAT = 32
CELLS_LON = 4
PATCH_CELLS = 128
SLOTS = 4
OBS_BLOCK = 128
NEWTON_STEPS = 3
LON_PAIRS = 2
LAT_PAIRS = 16
PAIRS = ((0, 1), (0, 2), (0, 3), (1, 2), (1, 3), (2, 3))
ROWS = 66
PAIR_ROWS = 192
COEF_ROWS = 16
MSG_ROWS = PAIR_ROWS + MEMBERS + COEF_ROWS
CHIPS = 16
SAME_CORE = [[j for j in range(32) if j % 2 == core] for core in range(2)]


def lon_weight(column, region):
    if column // 2 == region:
        return 0.75
    outer = column // 2 + (1 if column % 2 else -1)
    return 0.25 if outer == region else 0.0


def lat_weight(row, region):
    if row // 2 == region:
        return 0.75
    outer = row // 2 + (1 if row % 2 else -1)
    return 0.25 if outer == region else 0.0


def taper_tables():
    table = np.zeros((LON_PAIRS * LAT_PAIRS, 2 * PATCH_CELLS), np.float32)
    for a in range(LON_PAIRS):
        for b in range(LAT_PAIRS):
            for col in range(CELLS_LON):
                for row in range(CELLS_LAT):
                    cell = col * CELLS_LAT + row
                    lat_w = lat_weight(row, b)
                    table[a * LAT_PAIRS + b, cell] = lon_weight(col, a) * lat_w
                    if col == 0:
                        lon_w = lon_weight(col, a - LON_PAIRS)
                    elif col == CELLS_LON - 1:
                        lon_w = lon_weight(col, a + LON_PAIRS)
                    else:
                        lon_w = 0.0
                    table[a * LAT_PAIRS + b, PATCH_CELLS + cell] = lon_w * lat_w
    own_edges = np.zeros((2, COEF_ROWS, PATCH_CELLS), np.float32)
    side_edges = np.zeros((2, 2, 2, COEF_ROWS, PATCH_CELLS), np.float32)
    masks = np.zeros((2, 2, COEF_ROWS, PATCH_CELLS), np.float32)
    for lat_par in range(2):
        for which in range(2):
            upper = (which == 0) == (lat_par == 0)
            row = CELLS_LAT - 1 if upper else 0
            for col in range(CELLS_LON):
                cell = col * CELLS_LAT + row
                for a in range(LON_PAIRS):
                    own_edges[lat_par, 6 + 2 * which + a, cell] = 0.25 * lon_weight(col, a)
                for lon_par in range(2):
                    for source in range(2):
                        right = (source == 0) == (lon_par == 0)
                        region = LON_PAIRS if right else -1
                        weight = 0.25 * lon_weight(col, region)
                        side_edges[lat_par, lon_par, source, 6 + which, cell] = weight
    for lon_par in range(2):
        for source in range(2):
            right = (source == 0) == (lon_par == 0)
            first = (CELLS_LON - 1) * CELLS_LAT if right else 0
            masks[lon_par, source, :6, first : first + CELLS_LAT] = 1.0
    return table.reshape(LON_PAIRS, LAT_PAIRS, 2 * PATCH_CELLS), own_edges, side_edges, masks


TABLE, OWN_EDGES, SIDE_EDGES, MASKS = taper_tables()
SMEM = pl.BlockSpec(memory_space=pltpu.SMEM)
VMEM = pl.BlockSpec(memory_space=pltpu.VMEM)
MIB = 1024 * 1024


def mm(left, right):
    return lax.dot_general(
        left,
        right,
        (((1,), (0,)), ((), ())),
        precision=lax.Precision.HIGHEST,
        preferred_element_type=jnp.float32,
    )


def slot_ranks(owner_ref):
    owners = [owner_ref[s] for s in range(SLOTS)]
    ranks = []
    for s in range(SLOTS):
        rank = jnp.int32(0)
        for earlier in range(s):
            rank = rank + jnp.where((owners[earlier] >> 1) == (owners[s] >> 1), 1, 0)
        ranks.append(rank)
    return owners, ranks


def chosen_slot(owners, ranks, chip, q):
    slot = jnp.int32(0)
    owner = jnp.int32(0)
    for s in range(SLOTS):
        match = jnp.logical_and((owners[s] >> 1) == chip, ranks[s] == q)
        slot = jnp.where(match, s, slot)
        owner = jnp.where(match, owners[s], owner)
    return slot, owner


def split_kernel(depth, owner_ref, ens_ref, value_ref, prec_ref, send_ref, keep_ref, rows_ref, sems):
    f32 = jnp.float32
    me = lax.axis_index("lon")
    core = me & 1
    owners, ranks = slot_ranks(owner_ref)
    slots = [chosen_slot(owners, ranks, me >> 1, q)[0] for q in range(depth)]
    targets = ((send_ref, 1 - core), (keep_ref, core))
    copies = []
    for q in range(depth):
        for k, (ref, side) in enumerate(targets):
            copy = pltpu.make_async_copy(
                ens_ref.at[slots[q], :, side], ref.at[:, q, pl.ds(0, MEMBERS)], sems.at[2 * q + k]
            )
            copy.start()
            copies.append(copy)
    for q in range(depth):
        rows_ref[0] = value_ref[slots[q]].astype(f32)
        rows_ref[1] = prec_ref[slots[q]].astype(f32)
        for ref, side in targets:
            value = rows_ref[0, pl.ds(side, CHIPS, stride=2), :]
            prec = rows_ref[1, pl.ds(side, CHIPS, stride=2), :]
            for i in range(CHIPS):
                both = jnp.concatenate([value[i : i + 1], prec[i : i + 1]], axis=0)
                ref[i, q, MEMBERS:ROWS, :] = both.astype(jnp.bfloat16)
    for copy in copies:
        copy.wait()


def split_of(depth, slot_owner, obs_ens, obs_value, obs_prec):
    shape = jax.ShapeDtypeStruct((CHIPS, depth, ROWS, OBS_BLOCK), jnp.bfloat16)
    return pl.pallas_call(
        functools.partial(split_kernel, depth),
        out_shape=(shape, shape),
        in_specs=[SMEM, pl.BlockSpec(memory_space=pl.ANY), VMEM, VMEM],
        out_specs=(VMEM, VMEM),
        scratch_shapes=[
            pltpu.VMEM((2, 2 * CHIPS, OBS_BLOCK), jnp.float32),
            pltpu.SemaphoreType.DMA((2 * depth,)),
        ],
        compiler_params=pltpu.CompilerParams(vmem_limit_bytes=16 * MIB),
        name="split",
    )(
        slot_owner,
        obs_ens.reshape(SLOTS, CHIPS, 2, MEMBERS, OBS_BLOCK),
        obs_value.reshape(SLOTS, 2 * CHIPS, OBS_BLOCK),
        obs_prec.reshape(SLOTS, 2 * CHIPS, OBS_BLOCK),
    )


def merge_kernel(depth, owner_ref, keep_ref, got_ref, out_ref):
    me = lax.axis_index("lon")
    owners, ranks = slot_ranks(owner_ref)
    for q in range(depth):
        owner = chosen_slot(owners, ranks, me >> 1, q)[1]
        held = (owner & 1) == (me & 1)

        @pl.when(held)
        def _():
            out_ref[:, q] = keep_ref[:, q]

        @pl.when(jnp.logical_not(held))
        def _():
            out_ref[:, q] = got_ref[:, q]


def merge_of(depth, slot_owner, keep, got):
    return pl.pallas_call(
        functools.partial(merge_kernel, depth),
        out_shape=jax.ShapeDtypeStruct(keep.shape, keep.dtype),
        in_specs=[SMEM, VMEM, VMEM],
        out_specs=VMEM,
        compiler_params=pltpu.CompilerParams(vmem_limit_bytes=16 * MIB),
        name="merge",
    )(slot_owner, keep, got)


def transform_kernel(
    depth, owner_ref, count_ref, slots_ref, ids_ref, table_ref, sides_ref, block_ref,
    pair_ref, edge_a_ref, edge_b_ref, coef_ref, next_ref, held_ref,
):
    lat_par = lax.axis_index("lat") & 1
    owners, ranks = slot_ranks(owner_ref)
    places = [(owners[s] >> 1) * depth + ranks[s] for s in range(SLOTS)]
    f32 = jnp.float32
    members = MEMBERS
    row_id = lax.broadcasted_iota(jnp.int32, (members, members), 0)
    col_id = lax.broadcasted_iota(jnp.int32, (members, members), 1)
    identity = jnp.where(row_id == col_id, 1.0, 0.0).astype(f32)
    position = lax.broadcasted_iota(jnp.int32, (1, OBS_BLOCK), 1)
    grams = []
    projs = []
    for slot in range(SLOTS):
        block = block_ref[places[slot]].astype(f32)
        ens = block[:members]
        value = block[members : members + 1]
        prec = block[members + 1 : members + 2]
        obs_mean = jnp.sum(ens, axis=0, keepdims=True) * (1.0 / members)
        pert = (ens - obs_mean).astype(jnp.bfloat16)
        weight = jnp.where(position < count_ref[slot], prec, 0.0)
        weighted = (pert.astype(f32) * weight).astype(jnp.bfloat16)
        grams.append(
            lax.dot_general(
                weighted, pert, (((1,), (1,)), ((), ())), preferred_element_type=f32
            )
        )
        innovation = value - obs_mean
        projs.append(jnp.sum(weighted.astype(f32) * innovation, axis=1, keepdims=True))
    inverses = []
    iterates = []
    scalings = []
    for first, second in PAIRS:
        matrix = grams[first] + grams[second] + (members - 1.0) * identity
        trace = jnp.sum(jnp.sum(matrix * identity, axis=1, keepdims=True), axis=0, keepdims=True)
        scaling = trace * (1.0 / members)
        scalings.append(scaling)
        iterate = matrix / scaling
        inverses.append(1.5 * identity - 0.5 * iterate)
        iterates.append(iterate)
    iterates = [mm(x, y) for x, y in zip(iterates, inverses)]
    for step in range(1, NEWTON_STEPS):
        factors = [1.5 * identity - 0.5 * mm(y, x) for x, y in zip(iterates, inverses)]
        if step < NEWTON_STEPS - 1:
            iterates = [mm(x, f) for x, f in zip(iterates, factors)]
        inverses = [mm(f, y) for f, y in zip(factors, inverses)]
    roots = [y / jnp.sqrt(s) for y, s in zip(inverses, scalings)]
    sums = [projs[first] + projs[second] for first, second in PAIRS]
    inner = [mm(r, jnp.broadcast_to(p, (members, members))) for r, p in zip(roots, sums)]
    means = [mm(r, p) for r, p in zip(roots, inner)]
    for pair in range(len(PAIRS)):
        transform = math.sqrt(members - 1.0) * roots[pair] + means[pair]
        turned = transform.T
        held_ref[pair] = turned
        half = pair % 2
        pair_ref[pl.ds(pair // 2 * members, members), half * members : (half + 1) * members] = turned.astype(
            jnp.bfloat16
        )
    for which, ref in enumerate((edge_a_ref, edge_b_ref)):
        row = jnp.where(lat_par == which, LAT_PAIRS - 1, 0)
        for a in range(LON_PAIRS):
            one = slots_ref[a, 0, row]
            two = slots_ref[a, 1, row]
            low = jnp.minimum(one, two)
            high = jnp.maximum(one, two)
            chosen = held_ref[((low * (7 - low)) >> 1) + (high - low - 1)]
            ref[:, a * members : (a + 1) * members] = chosen.astype(jnp.bfloat16)
    tapers = jnp.zeros((COEF_ROWS, 2 * PATCH_CELLS), f32)
    pair_id = lax.broadcasted_iota(jnp.int32, (COEF_ROWS, LAT_PAIRS), 0)
    for a in range(LON_PAIRS):
        one = ids_ref[a, 0:1, :]
        two = ids_ref[a, 1:2, :]
        low = jnp.minimum(one, two)
        high = jnp.maximum(one, two)
        ids = ((low * (7 - low)) >> 1) + (high - low - 1)
        hot = jnp.where(pair_id == ids, 1.0, 0.0).astype(jnp.bfloat16)
        tapers = tapers + lax.dot_general(
            hot, table_ref[a], (((1,), (0,)), ((), ())), preferred_element_type=f32
        )
    coef_ref[...] = tapers[:, :PATCH_CELLS].astype(jnp.bfloat16) + sides_ref[lat_par]
    next_ref[...] = tapers[:, PATCH_CELLS:].astype(jnp.bfloat16)


def transforms_of(depth, slot_owner, counts, region_slots, blocks):
    bf16 = jnp.bfloat16
    wide = jax.ShapeDtypeStruct((MEMBERS, 2 * MEMBERS), bf16)
    coef = jax.ShapeDtypeStruct((COEF_ROWS, PATCH_CELLS), bf16)
    return pl.pallas_call(
        functools.partial(transform_kernel, depth),
        out_shape=(jax.ShapeDtypeStruct((PAIR_ROWS, 2 * MEMBERS), bf16), wide, wide, coef, coef),
        in_specs=[SMEM, SMEM, SMEM, VMEM, VMEM, VMEM, VMEM],
        out_specs=(VMEM,) * 5,
        scratch_shapes=[pltpu.VMEM((len(PAIRS), MEMBERS, MEMBERS), jnp.float32)],
        compiler_params=pltpu.CompilerParams(vmem_limit_bytes=16 * MIB),
        name="transforms",
    )(
        slot_owner, counts, region_slots, region_slots,
        jnp.asarray(TABLE, bf16), jnp.asarray(OWN_EDGES, bf16), blocks,
    )


def pack_kernel(pair_ref, lat_a_ref, lat_b_ref, next_ref, core_ref, swap_ref):
    f32 = jnp.float32
    lon_par = lax.axis_index("lon") & 1
    lane = lax.broadcasted_iota(jnp.int32, (MEMBERS, 2 * MEMBERS), 1)
    lat_a = lat_a_ref[...].astype(f32)
    lat_b = lat_b_ref[...].astype(f32)
    first = lane < MEMBERS
    zero = jnp.where(first, lat_a, pltpu.roll(lat_b, MEMBERS, 1))
    one = jnp.where(first, pltpu.roll(lat_a, MEMBERS, 1), lat_b)
    even = lon_par == 0
    tiles = (jnp.where(even, one, zero), jnp.where(even, zero, one))
    for ref, tile in zip((core_ref, swap_ref), tiles):
        ref[0:PAIR_ROWS] = pair_ref[...]
        ref[PAIR_ROWS : PAIR_ROWS + MEMBERS] = tile.astype(jnp.bfloat16)
        ref[PAIR_ROWS + MEMBERS :] = next_ref[...]


def pack_of(pairs, lat_a, lat_b, next_taper):
    shape = jax.ShapeDtypeStruct((MSG_ROWS, 2 * MEMBERS), jnp.bfloat16)
    return pl.pallas_call(
        pack_kernel,
        out_shape=(shape, shape),
        in_specs=[VMEM] * 4,
        out_specs=(VMEM, VMEM),
        name="pack",
    )(pairs, lat_a, lat_b, next_taper)


def spread(row, width):
    tile = jnp.broadcast_to(row, (COEF_ROWS, PATCH_CELLS))
    return jnp.concatenate([tile] * (width // PATCH_CELLS), axis=1)


def weighted_product(left_ref, weight_ref, count, perts):
    width = perts.shape[1]
    total = None
    for first in range(0, count, 4):
        parts = []
        for k in range(first, min(first + 4, count)):
            weight = weight_ref[k, :, 0:width]
            parts.append(perts * jnp.concatenate([weight] * (MEMBERS // COEF_ROWS), axis=0))
        part = lax.dot_general(
            left_ref[:, first * MEMBERS : min(first + 4, count) * MEMBERS],
            jnp.concatenate(parts, axis=0),
            (((1,), (0,)), ((), ())),
            preferred_element_type=jnp.float32,
        )
        total = part if total is None else total + part
    return total


OWN_TERMS = 10
SIDE_TERMS = 16
STEP = 8


def own_kernel(pair_ref, lat_a_ref, lat_b_ref, coef_ref, back_ref, sum_ref, edge_ref, left_ref, weight_ref):
    f32 = jnp.float32
    bf16 = jnp.bfloat16
    for tile in range(3):
        left_ref[:, tile * 128 : (tile + 1) * 128] = pair_ref[tile * MEMBERS : (tile + 1) * MEMBERS, :]
    left_ref[:, 384:512] = lat_a_ref[...]
    left_ref[:, 512:640] = lat_b_ref[...]
    coefs = coef_ref[...].astype(f32)
    for k in range(OWN_TERMS):
        weight_ref[k] = spread(coefs[k : k + 1], 2 * PATCH_CELLS).astype(bf16)
    lane = lax.broadcasted_iota(jnp.int32, (MEMBERS, PATCH_CELLS), 1)
    outer = jnp.logical_or(lane < CELLS_LAT, lane >= PATCH_CELLS - CELLS_LAT)

    def pair(first, count):
        perts = []
        means = []
        for f in range(count):
            state = back_ref[first + f].astype(f32)
            mean = jnp.sum(state, axis=0, keepdims=True) * (1.0 / MEMBERS)
            means.append(mean)
            perts.append((state - mean).astype(bf16))
        inner = pltpu.roll(perts[1].astype(f32), PATCH_CELLS // 2, 1) if count == 2 else 0.0
        edge_ref[first // 2] = jnp.where(outer, perts[0].astype(f32), inner).astype(bf16)
        both = jnp.concatenate(perts, axis=1) if count == 2 else perts[0]
        total = weighted_product(left_ref, weight_ref, OWN_TERMS, both)
        for f in range(count):
            sum_ref[first + f] = total[:, f * PATCH_CELLS : (f + 1) * PATCH_CELLS] + means[f]

    def step(index, carry):
        for at in range(0, STEP, 2):
            pair(index * STEP + at, 2)
        return carry

    whole = FIELDS // STEP
    lax.fori_loop(0, whole, step, 0)
    for first in range(whole * STEP, FIELDS, 2):
        pair(first, min(2, FIELDS - first))


def own_part(pairs, lat_a, lat_b, coefs, background):
    half = (FIELDS + 1) // 2
    return pl.pallas_call(
        own_kernel,
        out_shape=(
            jax.ShapeDtypeStruct((FIELDS, MEMBERS, PATCH_CELLS), jnp.float32),
            jax.ShapeDtypeStruct((half, MEMBERS, PATCH_CELLS), jnp.bfloat16),
        ),
        in_specs=[VMEM] * 5,
        out_specs=(VMEM, VMEM),
        scratch_shapes=[
            pltpu.VMEM((MEMBERS, OWN_TERMS * MEMBERS), jnp.bfloat16),
            pltpu.VMEM((OWN_TERMS, COEF_ROWS, 2 * PATCH_CELLS), jnp.bfloat16),
        ],
        cost_estimate=pl.CostEstimate(
            flops=2 * FIELDS * PATCH_CELLS * MEMBERS * MEMBERS * OWN_TERMS,
            bytes_accessed=FIELDS * MEMBERS * PATCH_CELLS * 8,
            transcendentals=0,
        ),
        compiler_params=pltpu.CompilerParams(vmem_limit_bytes=16 * MIB),
        name="own_part",
    )(pairs, lat_a, lat_b, coefs, background)


def side_kernel(core_ref, swap_ref, sides_ref, mask_ref, edge_ref, sum_ref, out_ref, left_ref, weight_ref):
    f32 = jnp.float32
    bf16 = jnp.bfloat16
    lat_par = lax.axis_index("lat") & 1
    lon_par = lax.axis_index("lon") & 1
    for source, ref in enumerate((core_ref, swap_ref)):
        for tile in range(4):
            at = (source * 4 + tile) * 128
            left_ref[:, at : at + 128] = ref[tile * MEMBERS : (tile + 1) * MEMBERS, :]
        tapers = ref[PAIR_ROWS + MEMBERS :, :].astype(f32) * mask_ref[lon_par, source].astype(f32)
        coefs = tapers + sides_ref[lat_par, lon_par, source].astype(f32)
        coefs = coefs + pltpu.roll(coefs, PATCH_CELLS // 2, 1)
        for k in range(8):
            weight_ref[source * 8 + k] = spread(coefs[k : k + 1], 2 * PATCH_CELLS).astype(bf16)
    lane = lax.broadcasted_iota(jnp.int32, (MEMBERS, PATCH_CELLS), 1)
    outer = jnp.logical_or(lane < CELLS_LAT, lane >= PATCH_CELLS - CELLS_LAT)

    def group(first, count):
        tiles = (count + 1) // 2
        edges = [edge_ref[first // 2 + t] for t in range(tiles)]
        both = jnp.concatenate(edges, axis=1) if tiles == 2 else edges[0]
        total = weighted_product(left_ref, weight_ref, SIDE_TERMS, both)
        for f in range(count):
            piece = total[:, f // 2 * PATCH_CELLS : (f // 2 + 1) * PATCH_CELLS]
            if f % 2:
                piece = pltpu.roll(piece, PATCH_CELLS // 2, 1)
            out_ref[first + f] = (sum_ref[first + f] + jnp.where(outer, piece, 0.0)).astype(bf16)

    def step(index, carry):
        for at in range(0, STEP, 4):
            group(index * STEP + at, 4)
        return carry

    whole = FIELDS // STEP
    lax.fori_loop(0, whole, step, 0)
    for first in range(whole * STEP, FIELDS, 4):
        group(first, min(4, FIELDS - first))


def side_part(from_core, from_swap, edges, sums):
    bf16 = jnp.bfloat16
    return pl.pallas_call(
        side_kernel,
        out_shape=jax.ShapeDtypeStruct((FIELDS, MEMBERS, PATCH_CELLS), bf16),
        in_specs=[VMEM] * 6,
        out_specs=VMEM,
        scratch_shapes=[
            pltpu.VMEM((MEMBERS, SIDE_TERMS * MEMBERS), bf16),
            pltpu.VMEM((SIDE_TERMS, COEF_ROWS, 2 * PATCH_CELLS), bf16),
        ],
        cost_estimate=pl.CostEstimate(
            flops=FIELDS * PATCH_CELLS * MEMBERS * MEMBERS * SIDE_TERMS,
            bytes_accessed=FIELDS * MEMBERS * PATCH_CELLS * 7,
            transcendentals=0,
        ),
        compiler_params=pltpu.CompilerParams(vmem_limit_bytes=16 * MIB),
        name="side_part",
    )(from_core, from_swap, jnp.asarray(SIDE_EDGES, bf16), jnp.asarray(MASKS, bf16), edges, sums)


def chip_transforms(depth, obs_ens, obs_value, obs_prec, slot_owner, counts, region_slots):
    send, keep = split_of(depth, slot_owner, obs_ens, obs_value, obs_prec)
    got = lax.ppermute(send, "lon", [(i, i ^ 1) for i in range(32)])
    both = merge_of(depth, slot_owner, keep, got)
    received = lax.all_to_all(both, "lon", 0, 0, axis_index_groups=SAME_CORE, tiled=True)
    blocks = received.reshape(CHIPS * depth, ROWS, OBS_BLOCK)
    return transforms_of(depth, slot_owner, counts, region_slots, blocks)


def shards(background, obs_ens, obs_value, obs_prec, obs_count, slot_owner, region_slots):
    chip = slot_owner >> 1
    most = jnp.max(jnp.sum((chip[:, None] == chip[None, :]).astype(jnp.int32), axis=1))
    operands = (
        obs_ens,
        obs_value,
        obs_prec,
        slot_owner,
        obs_count[:, 0, 0],
        jnp.transpose(region_slots, (0, 2, 1)),
    )
    branches = [functools.partial(chip_transforms, depth) for depth in (1, 2, SLOTS)]
    pairs, edge_a, edge_b, coefs, next_taper = lax.switch(
        jnp.minimum(most, 3) - 1, branches, *operands
    )

    pairs_a = [(i, i ^ 1) for i in range(8)]
    pairs_b = [(i, i + 1) for i in range(1, 7, 2)] + [(i + 1, i) for i in range(1, 7, 2)]
    lat_a = lax.ppermute(edge_a, "lat", pairs_a)
    lat_b = lax.ppermute(edge_b, "lat", pairs_b)
    to_core, to_swap = pack_of(pairs, lat_a, lat_b, next_taper)
    swap = [(i, (i + 1) % 32) for i in range(1, 32, 2)] + [((i + 1) % 32, i) for i in range(1, 32, 2)]
    from_swap = lax.ppermute(to_swap, "lon", swap)
    from_core = lax.ppermute(to_core, "lon", [(i, i ^ 1) for i in range(32)])
    state = background.reshape(FIELDS, MEMBERS, PATCH_CELLS)
    sums, edges = own_part(pairs, lat_a, lat_b, coefs, state)
    result = side_part(from_core, from_swap, edges, sums)
    return result.reshape(FIELDS, MEMBERS, 1, 1, PATCH_CELLS)


def solution(mesh):
    in_specs = (
        P(None, None, "lon", "lat", None),
        P(None, "lat", "lon", None, None, None),
        P(None, "lat", "lon", None, None),
        P(None, "lat", "lon", None, None),
        P(None, "lat", "lon"),
        P(),
        P("lon", "lat", None),
    )
    out_specs = P(None, None, "lon", "lat", None)
    return jax.shard_map(shards, mesh=mesh, in_specs=in_specs, out_specs=out_specs, check_vma=False)
```

```python
import functools
import math

import jax
import jax.numpy as jnp
from jax import lax
from jax.experimental import pallas as pl
from jax.experimental.pallas import tpu as pltpu
from jax.sharding import PartitionSpec as P

MEMBERS = 64
FIELDS = 69
CELLS_LAT = 32
CELLS_LON = 4
PATCH_CELLS = 128
SLOTS = 4
OBS_BLOCK = 128
NEWTON_STEPS = 3
LON_PAIRS = 2
LAT_PAIRS = 16
PAIRS = ((0, 1), (0, 2), (0, 3), (1, 2), (1, 3), (2, 3))
ROWS = 66
PAIR_ROWS = 192
COEF_ROWS = 16
MSG_ROWS = PAIR_ROWS + MEMBERS + COEF_ROWS
CHIPS = 16
SAME_CORE = [[j for j in range(32) if j % 2 == core] for core in range(2)]


def lon_weight(column, region):
    own = column >> 1
    outer = own + jnp.where((column & 1) == 1, 1, -1)
    return jnp.where(own == region, 0.75, jnp.where(outer == region, 0.25, 0.0))


def lat_weight(row, region):
    own = row >> 1
    outer = own + jnp.where((row & 1) == 1, 1, -1)
    return jnp.where(own == region, 0.75, jnp.where(outer == region, 0.25, 0.0))


def cell_lanes(rows):
    lane = lax.broadcasted_iota(jnp.int32, (rows, PATCH_CELLS), 1)
    return lane >> 5, lane & (CELLS_LAT - 1)


SMEM = pl.BlockSpec(memory_space=pltpu.SMEM)
VMEM = pl.BlockSpec(memory_space=pltpu.VMEM)
MIB = 1024 * 1024


def halves(array):
    high = array.astype(jnp.bfloat16)
    return high, (array - high.astype(jnp.float32)).astype(jnp.bfloat16)


def mm(left, right):
    def dot(x, y):
        return lax.dot_general(
            x, y, (((1,), (0,)), ((), ())), preferred_element_type=jnp.float32
        )

    left_high, left_low = halves(left)
    right_high, right_low = halves(right)
    return dot(left_high, right_high) + (dot(left_high, right_low) + dot(left_low, right_high))


def slot_ranks(owner_ref):
    owners = [owner_ref[s] for s in range(SLOTS)]
    ranks = []
    for s in range(SLOTS):
        rank = jnp.int32(0)
        for earlier in range(s):
            rank = rank + jnp.where((owners[earlier] >> 1) == (owners[s] >> 1), 1, 0)
        ranks.append(rank)
    return owners, ranks


def chosen_slot(owners, ranks, chip, q):
    slot = jnp.int32(0)
    owner = jnp.int32(0)
    for s in range(SLOTS):
        match = jnp.logical_and((owners[s] >> 1) == chip, ranks[s] == q)
        slot = jnp.where(match, s, slot)
        owner = jnp.where(match, owners[s], owner)
    return slot, owner


def split_kernel(places, owner_ref, ens_ref, value_ref, prec_ref, send_ref, keep_ref, held_ref, rows_ref, sems):
    f32 = jnp.float32
    me = lax.axis_index("lon")
    core = me & 1
    owners, ranks = slot_ranks(owner_ref)
    chosen = [chosen_slot(owners, ranks, me >> 1, q) for q in places]
    slots = [slot for slot, _ in chosen]
    for q, (_, owner) in enumerate(chosen):
        held_ref[q] = jnp.full((COEF_ROWS, OBS_BLOCK), jnp.where((owner & 1) == core, 1.0, 0.0), f32)
    targets = ((send_ref, 1 - core), (keep_ref, core))
    copies = []
    for q in range(len(places)):
        for k, (ref, side) in enumerate(targets):
            copy = pltpu.make_async_copy(
                ens_ref.at[slots[q], :, side], ref.at[:, q, pl.ds(0, MEMBERS)], sems.at[2 * q + k]
            )
            copy.start()
            copies.append(copy)
    for q in range(len(places)):
        rows_ref[0] = value_ref[slots[q]].astype(f32)
        rows_ref[1] = prec_ref[slots[q]].astype(f32)
        for ref, side in targets:
            value = rows_ref[0, pl.ds(side, CHIPS, stride=2), :]
            prec = rows_ref[1, pl.ds(side, CHIPS, stride=2), :]
            for i in range(CHIPS):
                both = jnp.concatenate([value[i : i + 1], prec[i : i + 1]], axis=0)
                ref[i, q, MEMBERS:ROWS, :] = both.astype(jnp.bfloat16)
    for copy in copies:
        copy.wait()


def split_of(places, slot_owner, obs_ens, obs_value, obs_prec):
    count = len(places)
    shape = jax.ShapeDtypeStruct((CHIPS, count, ROWS, OBS_BLOCK), jnp.bfloat16)
    return pl.pallas_call(
        functools.partial(split_kernel, places),
        out_shape=(shape, shape, jax.ShapeDtypeStruct((count, COEF_ROWS, OBS_BLOCK), jnp.float32)),
        in_specs=[SMEM, pl.BlockSpec(memory_space=pl.ANY), VMEM, VMEM],
        out_specs=(VMEM,) * 3,
        scratch_shapes=[
            pltpu.VMEM((2, 2 * CHIPS, OBS_BLOCK), jnp.float32),
            pltpu.SemaphoreType.DMA((2 * count,)),
        ],
        compiler_params=pltpu.CompilerParams(vmem_limit_bytes=16 * MIB),
        name="split",
    )(
        slot_owner,
        obs_ens.reshape(SLOTS, CHIPS, 2, MEMBERS, OBS_BLOCK),
        obs_value.reshape(SLOTS, 2 * CHIPS, OBS_BLOCK),
        obs_prec.reshape(SLOTS, 2 * CHIPS, OBS_BLOCK),
    )


def merge_kernel(held_ref, keep_ref, got_ref, out_ref):
    for q in range(held_ref.shape[0]):
        held = held_ref[q, 0:1, :]
        mine = held.astype(jnp.bfloat16)
        other = (1.0 - held).astype(jnp.bfloat16)
        out_ref[:, q] = keep_ref[:, q] * mine + got_ref[:, q] * other


def merge_of(held, keep, got):
    return pl.pallas_call(
        merge_kernel,
        out_shape=jax.ShapeDtypeStruct(keep.shape, keep.dtype),
        in_specs=[VMEM, VMEM, VMEM],
        out_specs=VMEM,
        compiler_params=pltpu.CompilerParams(vmem_limit_bytes=16 * MIB),
        name="merge",
    )(held, keep, got)


def transform_kernel(
    depth, owner_ref, count_ref, slots_ref, ids_ref, block_ref,
    core_ref, swap_ref, edge_a_ref, edge_b_ref, coef_ref, held_ref,
):
    lat_par = lax.axis_index("lat") & 1
    owners, ranks = slot_ranks(owner_ref)
    places = [(owners[s] >> 1) * depth + ranks[s] for s in range(SLOTS)]
    f32 = jnp.float32
    members = MEMBERS
    row_id = lax.broadcasted_iota(jnp.int32, (members, members), 0)
    col_id = lax.broadcasted_iota(jnp.int32, (members, members), 1)
    identity = jnp.where(row_id == col_id, 1.0, 0.0).astype(f32)
    position = lax.broadcasted_iota(jnp.int32, (1, OBS_BLOCK), 1)
    grams = []
    projs = []
    for slot in range(SLOTS):
        block = block_ref[places[slot]].astype(f32)
        ens = block[:members]
        value = block[members : members + 1]
        prec = block[members + 1 : members + 2]
        obs_mean = jnp.sum(ens, axis=0, keepdims=True) * (1.0 / members)
        pert = (ens - obs_mean).astype(jnp.bfloat16)
        weight = jnp.where(position < count_ref[slot], prec, 0.0)
        weighted = (pert.astype(f32) * weight).astype(jnp.bfloat16)
        grams.append(
            lax.dot_general(
                weighted, pert, (((1,), (1,)), ((), ())), preferred_element_type=f32
            )
        )
        innovation = value - obs_mean
        projs.append(jnp.sum(weighted.astype(f32) * innovation, axis=1, keepdims=True))
    inverses = []
    iterates = []
    scalings = []
    for first, second in PAIRS:
        matrix = grams[first] + grams[second] + (members - 1.0) * identity
        trace = jnp.sum(jnp.sum(matrix * identity, axis=1, keepdims=True), axis=0, keepdims=True)
        scaling = trace * (1.0 / members)
        scalings.append(scaling)
        iterate = matrix / scaling
        inverses.append(1.5 * identity - 0.5 * iterate)
        iterates.append(iterate)
    sums = [
        jnp.broadcast_to(projs[first] + projs[second], (members, members)) for first, second in PAIRS
    ]
    iterates = [mm(x, y) for x, y in zip(iterates, inverses)]
    for step in range(1, NEWTON_STEPS):
        last = step == NEWTON_STEPS - 1
        factors = [1.5 * identity - 0.5 * mm(y, x) for x, y in zip(iterates, inverses)]
        if last:
            sums = [mm(y, p) for y, p in zip(inverses, sums)]
            sums = [mm(f, p) for f, p in zip(factors, sums)]
        else:
            iterates = [mm(x, f) for x, f in zip(iterates, factors)]
        inverses = [mm(f, y) for f, y in zip(factors, inverses)]
    scales = [1.0 / jnp.sqrt(s) for s in scalings]
    roots = [y * s for y, s in zip(inverses, scales)]
    means = [mm(r, p * s) for r, p, s in zip(roots, sums, scales)]
    for pair in range(len(PAIRS)):
        transform = math.sqrt(members - 1.0) * roots[pair] + means[pair]
        turned = transform.T
        held_ref[pair] = turned
        half = pair % 2
        for ref in (core_ref, swap_ref):
            ref[pl.ds(pair // 2 * members, members), half * members : (half + 1) * members] = turned.astype(
                jnp.bfloat16
            )
    even = (lax.axis_index("lon") & 1) == 0
    for which, ref in enumerate((edge_a_ref, edge_b_ref)):
        row = jnp.where(lat_par == which, LAT_PAIRS - 1, 0)
        chosen = []
        for a in range(LON_PAIRS):
            one = slots_ref[a, 0, row]
            two = slots_ref[a, 1, row]
            low = jnp.minimum(one, two)
            high = jnp.maximum(one, two)
            chosen.append(held_ref[((low * (7 - low)) >> 1) + (high - low - 1)])
            ref[:, a * members : (a + 1) * members] = chosen[a].astype(jnp.bfloat16)
        lanes = slice(which * members, (which + 1) * members)
        rows = pl.ds(PAIR_ROWS, members)
        core_ref[rows, lanes] = jnp.where(even, chosen[1], chosen[0]).astype(jnp.bfloat16)
        swap_ref[rows, lanes] = jnp.where(even, chosen[0], chosen[1]).astype(jnp.bfloat16)
    tapers = jnp.zeros((COEF_ROWS, 2 * PATCH_CELLS), f32)
    pair_id = lax.broadcasted_iota(jnp.int32, (COEF_ROWS, LAT_PAIRS), 0)
    col, row = cell_lanes(LAT_PAIRS)
    lat_w = lat_weight(row, lax.broadcasted_iota(jnp.int32, (LAT_PAIRS, PATCH_CELLS), 0))
    for a in range(LON_PAIRS):
        one = ids_ref[a, 0:1, :]
        two = ids_ref[a, 1:2, :]
        low = jnp.minimum(one, two)
        high = jnp.maximum(one, two)
        ids = ((low * (7 - low)) >> 1) + (high - low - 1)
        hot = jnp.where(pair_id == ids, 1.0, 0.0).astype(jnp.bfloat16)
        outer = 0 if a == LON_PAIRS - 1 else CELLS_LON - 1
        table = jnp.concatenate(
            [lat_w * lon_weight(col, a), lat_w * jnp.where(col == outer, 0.25, 0.0)], axis=1
        )
        tapers = tapers + lax.dot_general(
            hot, table.astype(jnp.bfloat16), (((1,), (0,)), ((), ())), preferred_element_type=f32
        )
    coef_ref[...] = tapers[:, :PATCH_CELLS].astype(jnp.bfloat16)
    next_taper = tapers[:, PATCH_CELLS:].astype(jnp.bfloat16)
    core_ref[PAIR_ROWS + members :, :] = next_taper
    swap_ref[PAIR_ROWS + members :, :] = next_taper


def transforms_of(depth, slot_owner, counts, region_slots, blocks):
    bf16 = jnp.bfloat16
    wide = jax.ShapeDtypeStruct((MEMBERS, 2 * MEMBERS), bf16)
    coef = jax.ShapeDtypeStruct((COEF_ROWS, PATCH_CELLS), bf16)
    message = jax.ShapeDtypeStruct((MSG_ROWS, 2 * MEMBERS), bf16)
    return pl.pallas_call(
        functools.partial(transform_kernel, depth),
        out_shape=(message, message, wide, wide, coef),
        in_specs=[SMEM, SMEM, SMEM, VMEM, VMEM],
        out_specs=(VMEM,) * 5,
        scratch_shapes=[pltpu.VMEM((len(PAIRS), MEMBERS, MEMBERS), jnp.float32)],
        compiler_params=pltpu.CompilerParams(vmem_limit_bytes=16 * MIB),
        name="transforms",
    )(slot_owner, counts, region_slots, region_slots, blocks)


def pack_kernel(edge_a_ref, edge_b_ref, core_ref, swap_ref, out_a_ref, out_b_ref):
    f32 = jnp.float32
    even = (lax.axis_index("lon") & 1) == 0
    first = lax.broadcasted_iota(jnp.int32, (MEMBERS, 2 * MEMBERS), 1) < MEMBERS
    rows = pl.ds(PAIR_ROWS, MEMBERS)
    core = core_ref[rows, :].astype(f32)
    swap = swap_ref[rows, :].astype(f32)
    before = jnp.where(even, swap, core)
    after = jnp.where(even, core, swap)
    out_a_ref[0:MEMBERS] = edge_a_ref[...]
    out_b_ref[0:MEMBERS] = edge_b_ref[...]
    out_a_ref[MEMBERS:] = jnp.where(first, before, pltpu.roll(after, MEMBERS, 1)).astype(jnp.bfloat16)
    out_b_ref[MEMBERS:] = jnp.where(first, pltpu.roll(before, MEMBERS, 1), after).astype(jnp.bfloat16)


def pack_of(edge_a, edge_b, from_core, from_swap):
    shape = jax.ShapeDtypeStruct((2 * MEMBERS, 2 * MEMBERS), jnp.bfloat16)
    return pl.pallas_call(
        pack_kernel,
        out_shape=(shape, shape),
        in_specs=[VMEM] * 4,
        out_specs=(VMEM, VMEM),
        compiler_params=pltpu.CompilerParams(vmem_limit_bytes=4 * MIB),
        name="pack",
    )(edge_a, edge_b, from_core, from_swap)


def spread(row, width):
    tile = jnp.broadcast_to(row, (COEF_ROWS, PATCH_CELLS))
    return jnp.concatenate([tile] * (width // PATCH_CELLS), axis=1)


def weighted_product(left_ref, weight_ref, count, perts):
    width = perts.shape[1]
    total = None
    for first in range(0, count, 4):
        parts = []
        for k in range(first, min(first + 4, count)):
            weight = weight_ref[k, :, 0:width]
            parts.append(perts * jnp.concatenate([weight] * (MEMBERS // COEF_ROWS), axis=0))
        part = lax.dot_general(
            left_ref[:, first * MEMBERS : min(first + 4, count) * MEMBERS],
            jnp.concatenate(parts, axis=0),
            (((1,), (0,)), ((), ())),
            preferred_element_type=jnp.float32,
        )
        total = part if total is None else total + part
    return total


OWN_TERMS = 6
LAT_TERMS = 8
SIDE_TERMS = 12
CHUNK = 16
HALF = (FIELDS + 1) // 2
LAT_GROUP = 16
LAT_TILES = (FIELDS + LAT_GROUP - 1) // LAT_GROUP


def side_lanes():
    lane = lax.broadcasted_iota(jnp.int32, (MEMBERS, PATCH_CELLS), 1)
    return jnp.logical_or(lane < CELLS_LAT, lane >= PATCH_CELLS - CELLS_LAT)


def lat_lanes(field):
    lane = lax.broadcasted_iota(jnp.int32, (MEMBERS, PATCH_CELLS), 1)
    at = (lane - 2 * (field % LAT_GROUP)) & (CELLS_LAT - 1)
    return jnp.logical_or(at == 0, at == CELLS_LAT - 1)


def own_kernel(pair_ref, coef_ref, back_ref, sum_ref, edge_ref, rows_ref, left_ref, weight_ref):
    f32 = jnp.float32
    bf16 = jnp.bfloat16
    for tile in range(3):
        left_ref[:, tile * 128 : (tile + 1) * 128] = pair_ref[tile * MEMBERS : (tile + 1) * MEMBERS, :]
    coefs = coef_ref[...].astype(f32)
    for k in range(OWN_TERMS):
        weight_ref[k] = spread(coefs[k : k + 1], 2 * PATCH_CELLS).astype(bf16)
    outer = side_lanes()

    def pair(first, base, count, rows):
        perts = []
        means = []
        for f in range(count):
            state = back_ref[first + f].astype(f32)
            mean = jnp.sum(state, axis=0, keepdims=True) * (1.0 / MEMBERS)
            means.append(mean)
            perts.append((state - mean).astype(bf16))
        wide = [p.astype(f32) for p in perts]
        inner = pltpu.roll(wide[1], PATCH_CELLS // 2, 1) if count == 2 else 0.0
        edge_ref[first // 2] = jnp.where(outer, wide[0], inner).astype(bf16)
        for f in range(count):
            shift = 2 * ((base + f) % LAT_GROUP)
            moved = pltpu.roll(wide[f], shift, 1) if shift else wide[f]
            rows = jnp.where(lat_lanes(base + f), moved, rows)
        both = jnp.concatenate(perts, axis=1) if count == 2 else perts[0]
        total = weighted_product(left_ref, weight_ref, OWN_TERMS, both)
        for f in range(count):
            sum_ref[first + f] = total[:, f * PATCH_CELLS : (f + 1) * PATCH_CELLS] + means[f]
        return rows

    for tile in range(LAT_TILES):
        rows = jnp.zeros((MEMBERS, PATCH_CELLS), f32)
        last = min((tile + 1) * LAT_GROUP, FIELDS)
        for first in range(tile * LAT_GROUP, last, 2):
            rows = pair(first, first, min(2, last - first), rows)
        rows_ref[tile] = rows.astype(bf16)


def own_part(pairs, coefs, background):
    def tiles(count, kind):
        return jax.ShapeDtypeStruct((count, MEMBERS, PATCH_CELLS), kind)

    return pl.pallas_call(
        own_kernel,
        out_shape=(
            tiles(FIELDS, jnp.float32), tiles(HALF, jnp.bfloat16), tiles(LAT_TILES, jnp.bfloat16)
        ),
        in_specs=[VMEM] * 3,
        out_specs=(VMEM,) * 3,
        scratch_shapes=[
            pltpu.VMEM((MEMBERS, OWN_TERMS * MEMBERS), jnp.bfloat16),
            pltpu.VMEM((OWN_TERMS, COEF_ROWS, 2 * PATCH_CELLS), jnp.bfloat16),
        ],
        cost_estimate=pl.CostEstimate(
            flops=2 * FIELDS * PATCH_CELLS * MEMBERS * MEMBERS * OWN_TERMS,
            bytes_accessed=FIELDS * MEMBERS * PATCH_CELLS * 8,
            transcendentals=0,
        ),
        compiler_params=pltpu.CompilerParams(vmem_limit_bytes=16 * MIB),
        name="own_part",
    )(pairs, coefs, background)


def lat_kernel(
    lat_a_ref, lat_b_ref, rows_ref, sum_ref, final_ref, left_ref, weight_ref, out_ref, sems
):
    lat_par = lax.axis_index("lat") & 1
    for which, ref in enumerate((lat_a_ref, lat_b_ref)):
        for tile in range(2):
            at = (2 * which + tile) * 128
            left_ref[:, at : at + 128] = ref[tile * MEMBERS : (tile + 1) * MEMBERS, :]
    lane = lax.broadcasted_iota(jnp.int32, (COEF_ROWS, PATCH_CELLS), 1)
    group = lane >> 5
    last = (lane & 1) == 1
    before = jnp.logical_and(last, (lane & (CELLS_LAT - 1)) != CELLS_LAT - 1)
    col = jnp.where(before, (group + CELLS_LON - 1) & (CELLS_LON - 1), group)
    for which in range(2):
        edge = jnp.where(lat_par == which, 1, 0)
        for k, region in enumerate((0, 1, -1, LON_PAIRS)):
            weight = jnp.where((lane & 1) == edge, 0.25 * lon_weight(col, region), 0.0)
            weight = weight.astype(jnp.bfloat16)
            weight_ref[4 * which + k] = jnp.concatenate([weight, weight], axis=1)
    parts = []
    for tile in range(0, LAT_TILES, 2):
        some = [rows_ref[t] for t in range(tile, min(tile + 2, LAT_TILES))]
        both = jnp.concatenate(some, axis=1) if len(some) == 2 else some[0]
        total = weighted_product(left_ref, weight_ref, LAT_TERMS, both)
        for t in range(len(some)):
            parts.append(total[:, t * PATCH_CELLS : (t + 1) * PATCH_CELLS])
    edges = lat_lanes(0)
    copies = []
    for first in range(0, FIELDS, CHUNK):
        stop = min(first + CHUNK, FIELDS)
        for field in range(first, stop):
            shift = 2 * (field % LAT_GROUP)
            part = parts[field // LAT_GROUP]
            moved = pltpu.roll(part, PATCH_CELLS - shift, 1) if shift else part
            out_ref[field] = (sum_ref[field] + jnp.where(edges, moved, 0.0)).astype(jnp.bfloat16)
        span = pl.ds(first, stop - first)
        copy = pltpu.make_async_copy(out_ref.at[span], final_ref.at[span], sems.at[first // CHUNK])
        copy.start()
        copies.append(copy)
    for copy in copies:
        copy.wait()


def lat_part(lat_a, lat_b, rows, sums):
    return pl.pallas_call(
        lat_kernel,
        out_shape=jax.ShapeDtypeStruct(sums.shape, jnp.bfloat16),
        in_specs=[VMEM] * 4,
        out_specs=pl.BlockSpec(memory_space=pl.ANY),
        scratch_shapes=[
            pltpu.VMEM((MEMBERS, LAT_TERMS * MEMBERS), jnp.bfloat16),
            pltpu.VMEM((LAT_TERMS, COEF_ROWS, 2 * PATCH_CELLS), jnp.bfloat16),
            pltpu.VMEM((FIELDS, MEMBERS, PATCH_CELLS), jnp.bfloat16),
            pltpu.SemaphoreType.DMA(((FIELDS + CHUNK - 1) // CHUNK,)),
        ],
        compiler_params=pltpu.CompilerParams(vmem_limit_bytes=16 * MIB),
        name="lat_part",
    )(lat_a, lat_b, rows, sums)


def side_kernel(core_ref, swap_ref, edge_ref, sum_ref, out_ref, left_ref, weight_ref):
    f32 = jnp.float32
    bf16 = jnp.bfloat16
    lon_par = lax.axis_index("lon") & 1
    col = cell_lanes(COEF_ROWS)[0]
    for source, ref in enumerate((core_ref, swap_ref)):
        for tile in range(3):
            at = (source * 3 + tile) * 128
            left_ref[:, at : at + 128] = ref[tile * MEMBERS : (tile + 1) * MEMBERS, :]
        mine = col == jnp.where(lon_par == source, CELLS_LON - 1, 0)
        coefs = jnp.where(mine, ref[PAIR_ROWS + MEMBERS :, :].astype(f32), 0.0)
        coefs = coefs + pltpu.roll(coefs, PATCH_CELLS // 2, 1)
        for k in range(6):
            weight_ref[source * 6 + k] = spread(coefs[k : k + 1], 2 * PATCH_CELLS).astype(bf16)
    outer = side_lanes()

    def group(first, count):
        tiles = (count + 1) // 2
        edges = [edge_ref[first // 2 + t] for t in range(tiles)]
        both = jnp.concatenate(edges, axis=1) if tiles == 2 else edges[0]
        total = weighted_product(left_ref, weight_ref, SIDE_TERMS, both)
        for f in range(count):
            piece = total[:, f // 2 * PATCH_CELLS : (f // 2 + 1) * PATCH_CELLS]
            if f % 2:
                piece = pltpu.roll(piece, PATCH_CELLS // 2, 1)
            out_ref[first + f] = sum_ref[first + f] + jnp.where(outer, piece, 0.0)

    for first in range(0, FIELDS, 4):
        group(first, min(4, FIELDS - first))


def side_part(from_core, from_swap, edges, sums):
    bf16 = jnp.bfloat16
    return pl.pallas_call(
        side_kernel,
        out_shape=jax.ShapeDtypeStruct(sums.shape, sums.dtype),
        in_specs=[VMEM] * 4,
        out_specs=VMEM,
        scratch_shapes=[
            pltpu.VMEM((MEMBERS, SIDE_TERMS * MEMBERS), bf16),
            pltpu.VMEM((SIDE_TERMS, COEF_ROWS, 2 * PATCH_CELLS), bf16),
        ],
        cost_estimate=pl.CostEstimate(
            flops=FIELDS * PATCH_CELLS * MEMBERS * MEMBERS * SIDE_TERMS,
            bytes_accessed=FIELDS * MEMBERS * PATCH_CELLS * 7,
            transcendentals=0,
        ),
        compiler_params=pltpu.CompilerParams(vmem_limit_bytes=16 * MIB),
        name="side_part",
    )(from_core, from_swap, edges, sums)


CORES = [(i, i ^ 1) for i in range(32)]


def chip_transforms(depth, both, obs_ens, obs_value, obs_prec, slot_owner, counts, region_slots):
    if depth > 1:
        rest = tuple(range(1, depth))
        send, keep, held = split_of(rest, slot_owner, obs_ens, obs_value, obs_prec)
        got = lax.ppermute(send, "lon", CORES)
        both = jnp.concatenate([both, merge_of(held, keep, got)], axis=1)
    received = lax.all_to_all(both, "lon", 0, 0, axis_index_groups=SAME_CORE, tiled=True)
    blocks = received.reshape(CHIPS * depth, ROWS, OBS_BLOCK)
    return transforms_of(depth, slot_owner, counts, region_slots, blocks)


def shards(background, obs_ens, obs_value, obs_prec, obs_count, slot_owner, region_slots):
    send, keep, held = split_of((0,), slot_owner, obs_ens, obs_value, obs_prec)
    got = lax.ppermute(send, "lon", CORES)
    both = merge_of(held, keep, got)
    chip = slot_owner >> 1
    most = jnp.max(jnp.sum((chip[:, None] == chip[None, :]).astype(jnp.int32), axis=1))
    operands = (
        both,
        obs_ens,
        obs_value,
        obs_prec,
        slot_owner,
        obs_count[:, 0, 0],
        jnp.transpose(region_slots, (0, 2, 1)),
    )
    branches = [functools.partial(chip_transforms, depth) for depth in (1, 2, SLOTS)]
    to_core, to_swap, edge_a, edge_b, coefs = lax.switch(
        jnp.minimum(most, 3) - 1, branches, *operands
    )

    swap = [(i, (i + 1) % 32) for i in range(1, 32, 2)] + [((i + 1) % 32, i) for i in range(1, 32, 2)]
    from_swap = lax.ppermute(to_swap, "lon", swap)
    from_core = lax.ppermute(to_core, "lon", CORES)
    state = background.reshape(FIELDS, MEMBERS, PATCH_CELLS)
    sums, edges, rows = own_part(to_core, coefs, state)
    message_a, message_b = pack_of(edge_a, edge_b, from_core, from_swap)
    pairs_a = [(i, i ^ 1) for i in range(8)]
    pairs_b = [(i, i + 1) for i in range(1, 7, 2)] + [(i + 1, i) for i in range(1, 7, 2)]
    lat_b = lax.ppermute(message_b, "lat", pairs_b)
    lat_a = lax.ppermute(message_a, "lat", pairs_a)
    sums = side_part(from_core, from_swap, edges, sums)
    result = lat_part(lat_a, lat_b, rows, sums)
    return result.reshape(FIELDS, MEMBERS, 1, 1, PATCH_CELLS)


def solution(mesh):
    in_specs = (
        P(None, None, "lon", "lat", None),
        P(None, "lat", "lon", None, None, None),
        P(None, "lat", "lon", None, None),
        P(None, "lat", "lon", None, None),
        P(None, "lat", "lon"),
        P(),
        P("lon", "lat", None),
    )
    out_specs = P(None, None, "lon", "lat", None)
    return jax.shard_map(shards, mesh=mesh, in_specs=in_specs, out_specs=out_specs, check_vma=False)
```

```python
import functools
import math

import jax
import jax.numpy as jnp
from jax import lax
from jax.experimental import pallas as pl
from jax.experimental.pallas import tpu as pltpu
from jax.sharding import PartitionSpec as P

MEMBERS = 64
FIELDS = 69
CELLS_LAT = 32
CELLS_LON = 4
PATCH_CELLS = 128
SLOTS = 4
OBS_BLOCK = 128
NEWTON_STEPS = 3
LON_PAIRS = 2
LAT_PAIRS = 16
PAIRS = ((0, 1), (0, 2), (0, 3), (1, 2), (1, 3), (2, 3))
ROWS = 66
PAIR_ROWS = 192
COEF_ROWS = 16
MSG_ROWS = PAIR_ROWS + MEMBERS + COEF_ROWS
CHIPS = 16
N_LAT = 8
SAME_CORE = [[j for j in range(32) if j % 2 == core] for core in range(2)]


def lon_weight(column, region):
    own = column >> 1
    outer = own + jnp.where((column & 1) == 1, 1, -1)
    return jnp.where(own == region, 0.75, jnp.where(outer == region, 0.25, 0.0))


def lat_weight(row, region):
    own = row >> 1
    outer = own + jnp.where((row & 1) == 1, 1, -1)
    return jnp.where(own == region, 0.75, jnp.where(outer == region, 0.25, 0.0))


def cell_lanes(rows):
    lane = lax.broadcasted_iota(jnp.int32, (rows, PATCH_CELLS), 1)
    return lane >> 5, lane & (CELLS_LAT - 1)


SMEM = pl.BlockSpec(memory_space=pltpu.SMEM)
VMEM = pl.BlockSpec(memory_space=pltpu.VMEM)
MIB = 1024 * 1024


def halves(array):
    high = array.astype(jnp.bfloat16)
    return high, (array - high.astype(jnp.float32)).astype(jnp.bfloat16)


def mm(left, right):
    def dot(x, y):
        return lax.dot_general(
            x, y, (((1,), (0,)), ((), ())), preferred_element_type=jnp.float32
        )

    left_high, left_low = halves(left)
    right_high, right_low = halves(right)
    return dot(left_high, right_high) + (dot(left_high, right_low) + dot(left_low, right_high))


def slot_ranks(owner_ref):
    owners = [owner_ref[s] for s in range(SLOTS)]
    ranks = []
    for s in range(SLOTS):
        rank = jnp.int32(0)
        for earlier in range(s):
            rank = rank + jnp.where((owners[earlier] >> 1) == (owners[s] >> 1), 1, 0)
        ranks.append(rank)
    return owners, ranks


def chosen_slot(owners, ranks, chip, q):
    slot = jnp.int32(0)
    owner = jnp.int32(0)
    for s in range(SLOTS):
        match = jnp.logical_and((owners[s] >> 1) == chip, ranks[s] == q)
        slot = jnp.where(match, s, slot)
        owner = jnp.where(match, owners[s], owner)
    return slot, owner


def split_kernel(
    places, owner_ref, ens_ref, value_ref, prec_ref, send_ref, keep_ref, held_ref, info_ref, index_ref,
    rows_ref, small_ref, small_sems, sems,
):
    f32 = jnp.float32
    me = lax.axis_index("lon")
    core = me & 1
    owners, ranks = slot_ranks(owner_ref)
    chosen = [chosen_slot(owners, ranks, me >> 1, q) for q in places]
    slots = [slot for slot, _ in chosen]
    for q, (_, owner) in enumerate(chosen):
        held_ref[q] = jnp.full((COEF_ROWS, OBS_BLOCK), jnp.where((owner & 1) == core, 1.0, 0.0), f32)
    most = ranks[0]
    for s in range(1, SLOTS):
        most = jnp.maximum(most, ranks[s])
    index_ref[...] = jnp.full((8, OBS_BLOCK), jnp.minimum(most, 2), jnp.int32)
    for s in range(SLOTS):
        info_ref[s : s + 1, :] = jnp.full((1, OBS_BLOCK), (owners[s] >> 1).astype(f32), f32)
        info_ref[SLOTS + s : SLOTS + s + 1, :] = jnp.full((1, OBS_BLOCK), ranks[s].astype(f32), f32)
    targets = ((send_ref, 1 - core), (keep_ref, core))
    copies = []
    smalls = []
    for q in range(len(places)):
        for k, ref in enumerate((value_ref, prec_ref)):
            copy = pltpu.make_async_copy(
                ref.at[slots[q]], small_ref.at[2 * q + k], small_sems.at[2 * q + k]
            )
            copy.start()
            smalls.append(copy)
        for k, (ref, side) in enumerate(targets):
            copy = pltpu.make_async_copy(
                ens_ref.at[slots[q], :, side], ref.at[:, q, pl.ds(0, MEMBERS)], sems.at[2 * q + k]
            )
            copy.start()
            copies.append(copy)
    for copy in smalls:
        copy.wait()
    for q in range(len(places)):
        rows_ref[0] = small_ref[2 * q].astype(f32)
        rows_ref[1] = small_ref[2 * q + 1].astype(f32)
        for ref, side in targets:
            value = rows_ref[0, pl.ds(side, CHIPS, stride=2), :]
            prec = rows_ref[1, pl.ds(side, CHIPS, stride=2), :]
            for i in range(CHIPS):
                both = jnp.concatenate([value[i : i + 1], prec[i : i + 1]], axis=0)
                ref[i, q, MEMBERS:ROWS, :] = both.astype(jnp.bfloat16)
    for copy in copies:
        copy.wait()


def split_of(places, slot_owner, obs_ens, obs_value, obs_prec):
    count = len(places)
    shape = jax.ShapeDtypeStruct((CHIPS, count, ROWS, OBS_BLOCK), jnp.bfloat16)
    return pl.pallas_call(
        functools.partial(split_kernel, places),
        out_shape=(
            shape,
            shape,
            jax.ShapeDtypeStruct((count, COEF_ROWS, OBS_BLOCK), jnp.float32),
            jax.ShapeDtypeStruct((2 * SLOTS, OBS_BLOCK), jnp.float32),
            jax.ShapeDtypeStruct((8, OBS_BLOCK), jnp.int32),
        ),
        in_specs=[SMEM] + [pl.BlockSpec(memory_space=pl.ANY)] * 3,
        out_specs=(VMEM,) * 5,
        scratch_shapes=[
            pltpu.VMEM((2, 2 * CHIPS, OBS_BLOCK), jnp.float32),
            pltpu.VMEM((2 * count, 2 * CHIPS, OBS_BLOCK), jnp.bfloat16),
            pltpu.SemaphoreType.DMA((2 * count,)),
            pltpu.SemaphoreType.DMA((2 * count,)),
        ],
        compiler_params=pltpu.CompilerParams(vmem_limit_bytes=16 * MIB),
        name="split",
    )(
        slot_owner,
        obs_ens.reshape(SLOTS, CHIPS, 2, MEMBERS, OBS_BLOCK),
        obs_value.reshape(SLOTS, 2 * CHIPS, OBS_BLOCK),
        obs_prec.reshape(SLOTS, 2 * CHIPS, OBS_BLOCK),
    )


def blend(held, keep, got):
    mine = held.astype(jnp.bfloat16)
    other = (1.0 - held).astype(jnp.bfloat16)
    return keep * mine + got * other


def merge_kernel(held_ref, keep_ref, got_ref, out_ref):
    for q in range(held_ref.shape[0]):
        out_ref[:, q] = blend(held_ref[q, 0:1, :], keep_ref[:, q], got_ref[:, q])


def append_kernel(both_ref, held_ref, keep_ref, got_ref, out_ref):
    out_ref[:, 0] = both_ref[:, 0]
    for q in range(held_ref.shape[0]):
        out_ref[:, 1 + q] = blend(held_ref[q, 0:1, :], keep_ref[:, q], got_ref[:, q])


def merge_of(held, keep, got, both=None):
    count = keep.shape[1]
    operands = (held, keep, got)
    if both is not None:
        count = count + 1
        operands = (both,) + operands
    return pl.pallas_call(
        merge_kernel if both is None else append_kernel,
        out_shape=jax.ShapeDtypeStruct((CHIPS, count, ROWS, OBS_BLOCK), keep.dtype),
        in_specs=[VMEM] * len(operands),
        out_specs=VMEM,
        compiler_params=pltpu.CompilerParams(vmem_limit_bytes=16 * MIB),
        name="merge",
    )(*operands)


def entry(row, lane):
    at = lax.broadcasted_iota(jnp.int32, row.shape, 1)
    return jnp.sum(jnp.where(at == lane, row.astype(jnp.float32), 0.0), axis=1, keepdims=True)


def pair_ids(ids_ref, a):
    one = ids_ref[a, 0:1, :]
    two = ids_ref[a, 1:2, :]
    low = jnp.minimum(one, two)
    high = jnp.maximum(one, two)
    return ((low * (7 - low)) >> 1) + (high - low - 1)


def transform_kernel(
    depth, info_ref, count_ref, ids_ref, block_ref, core_ref, swap_ref, edge_a_ref, edge_b_ref, coef_ref
):
    f32 = jnp.float32
    bf16 = jnp.bfloat16
    members = MEMBERS
    lat_par = lax.axis_index("lat") & 1
    even = (lax.axis_index("lon") & 1) == 0
    row_id = lax.broadcasted_iota(jnp.int32, (members, members), 0)
    col_id = lax.broadcasted_iota(jnp.int32, (members, members), 1)
    identity = jnp.where(row_id == col_id, 1.0, 0.0).astype(f32)
    position = lax.broadcasted_iota(jnp.int32, (1, OBS_BLOCK), 1).astype(f32)
    grams = []
    projs = []
    for slot in range(SLOTS):
        place = info_ref[slot : slot + 1, :] * depth + info_ref[SLOTS + slot : SLOTS + slot + 1, :]
        block = None
        for k in range(CHIPS * depth):
            here = jnp.where(place == k, 1.0, 0.0).astype(bf16)
            part = block_ref[k] * here
            block = part if block is None else block + part
        block = block.astype(f32)
        ens = block[:members]
        value = block[members : members + 1]
        prec = block[members + 1 : members + 2]
        obs_mean = jnp.sum(ens, axis=0, keepdims=True) * (1.0 / members)
        pert = (ens - obs_mean).astype(bf16)
        weight = jnp.where(position < entry(count_ref[...], slot), prec, 0.0)
        weighted = (pert.astype(f32) * weight).astype(bf16)
        high, low = halves(value - obs_mean)
        rows = [jnp.broadcast_to(x, (COEF_ROWS, OBS_BLOCK)) for x in (high, low)]
        product = lax.dot_general(
            jnp.concatenate([pert] + rows, axis=0),
            weighted,
            (((1,), (1,)), ((), ())),
            preferred_element_type=f32,
        )
        grams.append(product[:members])
        projs.append(product[members : members + 8] + product[members + COEF_ROWS : members + COEF_ROWS + 8])
    iterates = []
    inverses = []
    scalings = []
    for first, second in PAIRS:
        matrix = grams[first] + grams[second] + (members - 1.0) * identity
        trace = jnp.sum(jnp.sum(matrix * identity, axis=1, keepdims=True), axis=0, keepdims=True)
        scaling = trace * (1.0 / members)
        scalings.append(scaling)
        iterate = matrix * (1.0 / scaling)
        iterates.append(iterate)
        inverses.append(1.5 * identity - 0.5 * iterate)
    sums = [projs[first] + projs[second] for first, second in PAIRS]
    iterates = [mm(x, y) for x, y in zip(iterates, inverses)]
    for step in range(1, NEWTON_STEPS):
        factors = [1.5 * identity - 0.5 * mm(y, x) for x, y in zip(iterates, inverses)]
        if step < NEWTON_STEPS - 1:
            both = [mm(jnp.concatenate([x, y], axis=0), f) for x, y, f in zip(iterates, inverses, factors)]
            iterates = [z[:members] for z in both]
            inverses = [z[members:] for z in both]
        else:
            sums = [mm(p, y) for p, y in zip(sums, inverses)]
            both = [mm(jnp.concatenate([y, p], axis=0), f) for y, p, f in zip(inverses, sums, factors)]
            inverses = [z[:members] for z in both]
            sums = [mm(z[members:], z[:members]) for z in both]
    turned = []
    for pair in range(len(PAIRS)):
        scale = 1.0 / scalings[pair]
        root = math.sqrt(members - 1.0) * jnp.sqrt(scale)
        turned.append(inverses[pair] * root + sums[pair][0:1] * scale)
        lanes = slice(pair % 2 * members, (pair % 2 + 1) * members)
        rows = pl.ds(pair // 2 * members, members)
        core_ref[rows, lanes] = turned[pair].astype(bf16)
        swap_ref[rows, lanes] = turned[pair].astype(bf16)
    ids = [pair_ids(ids_ref, a) for a in range(LON_PAIRS)]
    for which, ref in enumerate((edge_a_ref, edge_b_ref)):
        row = jnp.where(lat_par == which, LAT_PAIRS - 1, 0)
        chosen = []
        for a in range(LON_PAIRS):
            edge = entry(ids[a], row)
            one = turned[0]
            for pair in range(1, len(PAIRS)):
                one = jnp.where(edge == pair, turned[pair], one)
            chosen.append(one)
            ref[:, a * members : (a + 1) * members] = one.astype(bf16)
        lanes = slice(which * members, (which + 1) * members)
        rows = pl.ds(PAIR_ROWS, members)
        core_ref[rows, lanes] = jnp.where(even, chosen[1], chosen[0]).astype(bf16)
        swap_ref[rows, lanes] = jnp.where(even, chosen[0], chosen[1]).astype(bf16)
    tapers = jnp.zeros((COEF_ROWS, 2 * PATCH_CELLS), f32)
    pair_id = lax.broadcasted_iota(jnp.int32, (COEF_ROWS, LAT_PAIRS), 0)
    col, row = cell_lanes(LAT_PAIRS)
    lat_w = lat_weight(row, lax.broadcasted_iota(jnp.int32, (LAT_PAIRS, PATCH_CELLS), 0))
    for a in range(LON_PAIRS):
        hot = jnp.where(pair_id == ids[a], 1.0, 0.0).astype(bf16)
        outer = 0 if a == LON_PAIRS - 1 else CELLS_LON - 1
        table = jnp.concatenate(
            [lat_w * lon_weight(col, a), lat_w * jnp.where(col == outer, 0.25, 0.0)], axis=1
        )
        tapers = tapers + lax.dot_general(
            hot, table.astype(bf16), (((1,), (0,)), ((), ())), preferred_element_type=f32
        )
    coef_ref[...] = tapers[:, :PATCH_CELLS].astype(bf16)
    next_taper = tapers[:, PATCH_CELLS:].astype(bf16)
    core_ref[PAIR_ROWS + members :, :] = next_taper
    swap_ref[PAIR_ROWS + members :, :] = next_taper


def transforms_of(depth, info, counts, region_slots, blocks):
    bf16 = jnp.bfloat16
    wide = jax.ShapeDtypeStruct((MEMBERS, 2 * MEMBERS), bf16)
    coef = jax.ShapeDtypeStruct((COEF_ROWS, PATCH_CELLS), bf16)
    message = jax.ShapeDtypeStruct((MSG_ROWS, 2 * MEMBERS), bf16)
    return pl.pallas_call(
        functools.partial(transform_kernel, depth),
        out_shape=(message, message, wide, wide, coef),
        in_specs=[VMEM] * 4,
        out_specs=(VMEM,) * 5,
        compiler_params=pltpu.CompilerParams(vmem_limit_bytes=16 * MIB),
        name="transforms",
    )(info, counts.reshape(1, SLOTS), region_slots, blocks)


def pack_kernel(edge_a_ref, edge_b_ref, core_ref, swap_ref, out_a_ref, out_b_ref):
    f32 = jnp.float32
    even = (lax.axis_index("lon") & 1) == 0
    first = lax.broadcasted_iota(jnp.int32, (MEMBERS, 2 * MEMBERS), 1) < MEMBERS
    rows = pl.ds(PAIR_ROWS, MEMBERS)
    core = core_ref[rows, :].astype(f32)
    swap = swap_ref[rows, :].astype(f32)
    before = jnp.where(even, swap, core)
    after = jnp.where(even, core, swap)
    out_a_ref[0:MEMBERS] = edge_a_ref[...]
    out_b_ref[0:MEMBERS] = edge_b_ref[...]
    out_a_ref[MEMBERS:] = jnp.where(first, before, pltpu.roll(after, MEMBERS, 1)).astype(jnp.bfloat16)
    out_b_ref[MEMBERS:] = jnp.where(first, pltpu.roll(before, MEMBERS, 1), after).astype(jnp.bfloat16)


def pack_of(edge_a, edge_b, from_core, from_swap):
    shape = jax.ShapeDtypeStruct((2 * MEMBERS, 2 * MEMBERS), jnp.bfloat16)
    return pl.pallas_call(
        pack_kernel,
        out_shape=(shape, shape),
        in_specs=[VMEM] * 4,
        out_specs=(VMEM, VMEM),
        compiler_params=pltpu.CompilerParams(vmem_limit_bytes=4 * MIB),
        name="pack",
    )(edge_a, edge_b, from_core, from_swap)


def spread(row, width):
    tile = jnp.broadcast_to(row, (COEF_ROWS, PATCH_CELLS))
    return jnp.concatenate([tile] * (width // PATCH_CELLS), axis=1)


def weighted_product(left_ref, weight_ref, count, perts):
    width = perts.shape[1]
    total = None
    for first in range(0, count, 4):
        parts = []
        for k in range(first, min(first + 4, count)):
            weight = weight_ref[k, :, 0:width]
            parts.append(perts * jnp.concatenate([weight] * (MEMBERS // COEF_ROWS), axis=0))
        part = lax.dot_general(
            left_ref[:, first * MEMBERS : min(first + 4, count) * MEMBERS],
            jnp.concatenate(parts, axis=0),
            (((1,), (0,)), ((), ())),
            preferred_element_type=jnp.float32,
        )
        total = part if total is None else total + part
    return total


OWN_TERMS = 6
LAT_TERMS = 8
SIDE_TERMS = 12
CHUNK = 16
HALF = (FIELDS + 1) // 2
LAT_GROUP = 16
LAT_TILES = (FIELDS + LAT_GROUP - 1) // LAT_GROUP


def side_lanes():
    lane = lax.broadcasted_iota(jnp.int32, (MEMBERS, PATCH_CELLS), 1)
    return jnp.logical_or(lane < CELLS_LAT, lane >= PATCH_CELLS - CELLS_LAT)


def lat_lanes(field):
    lane = lax.broadcasted_iota(jnp.int32, (MEMBERS, PATCH_CELLS), 1)
    at = (lane - 2 * (field % LAT_GROUP)) & (CELLS_LAT - 1)
    return jnp.logical_or(at == 0, at == CELLS_LAT - 1)


def own_kernel(pair_ref, coef_ref, back_ref, sum_ref, edge_ref, rows_ref, left_ref, weight_ref):
    f32 = jnp.float32
    bf16 = jnp.bfloat16
    for tile in range(3):
        left_ref[:, tile * 128 : (tile + 1) * 128] = pair_ref[tile * MEMBERS : (tile + 1) * MEMBERS, :]
    coefs = coef_ref[...].astype(f32)
    for k in range(OWN_TERMS):
        weight_ref[k] = spread(coefs[k : k + 1], 2 * PATCH_CELLS).astype(bf16)
    outer = side_lanes()

    def pair(first, base, count, rows):
        perts = []
        means = []
        for f in range(count):
            state = back_ref[first + f].astype(f32)
            mean = jnp.sum(state, axis=0, keepdims=True) * (1.0 / MEMBERS)
            means.append(mean)
            perts.append((state - mean).astype(bf16))
        wide = [p.astype(f32) for p in perts]
        inner = pltpu.roll(wide[1], PATCH_CELLS // 2, 1) if count == 2 else 0.0
        edge_ref[first // 2] = jnp.where(outer, wide[0], inner).astype(bf16)
        for f in range(count):
            shift = 2 * ((base + f) % LAT_GROUP)
            moved = pltpu.roll(wide[f], shift, 1) if shift else wide[f]
            rows = jnp.where(lat_lanes(base + f), moved, rows)
        both = jnp.concatenate(perts, axis=1) if count == 2 else perts[0]
        total = weighted_product(left_ref, weight_ref, OWN_TERMS, both)
        for f in range(count):
            sum_ref[first + f] = total[:, f * PATCH_CELLS : (f + 1) * PATCH_CELLS] + means[f]
        return rows

    for tile in range(LAT_TILES):
        rows = jnp.zeros((MEMBERS, PATCH_CELLS), f32)
        last = min((tile + 1) * LAT_GROUP, FIELDS)
        for first in range(tile * LAT_GROUP, last, 2):
            rows = pair(first, first, min(2, last - first), rows)
        rows_ref[tile] = rows.astype(bf16)


def own_part(pairs, coefs, background):
    def tiles(count, kind):
        return jax.ShapeDtypeStruct((count, MEMBERS, PATCH_CELLS), kind)

    return pl.pallas_call(
        own_kernel,
        out_shape=(
            tiles(FIELDS, jnp.float32), tiles(HALF, jnp.bfloat16), tiles(LAT_TILES, jnp.bfloat16)
        ),
        in_specs=[VMEM] * 3,
        out_specs=(VMEM,) * 3,
        scratch_shapes=[
            pltpu.VMEM((MEMBERS, OWN_TERMS * MEMBERS), jnp.bfloat16),
            pltpu.VMEM((OWN_TERMS, COEF_ROWS, 2 * PATCH_CELLS), jnp.bfloat16),
        ],
        cost_estimate=pl.CostEstimate(
            flops=2 * FIELDS * PATCH_CELLS * MEMBERS * MEMBERS * OWN_TERMS,
            bytes_accessed=FIELDS * MEMBERS * PATCH_CELLS * 8,
            transcendentals=0,
        ),
        compiler_params=pltpu.CompilerParams(vmem_limit_bytes=16 * MIB),
        name="own_part",
    )(pairs, coefs, background)


def lat_kernel(
    lat_a_ref, lat_b_ref, rows_ref, sum_ref, final_ref, left_ref, weight_ref, out_ref, sems
):
    lat = lax.axis_index("lat")
    lat_par = lat & 1
    for which, ref in enumerate((lat_a_ref, lat_b_ref)):
        for tile in range(2):
            at = (2 * which + tile) * 128
            left_ref[:, at : at + 128] = ref[tile * MEMBERS : (tile + 1) * MEMBERS, :]
    lane = lax.broadcasted_iota(jnp.int32, (COEF_ROWS, PATCH_CELLS), 1)
    group = lane >> 5
    last = (lane & 1) == 1
    before = jnp.logical_and(last, (lane & (CELLS_LAT - 1)) != CELLS_LAT - 1)
    col = jnp.where(before, (group + CELLS_LON - 1) & (CELLS_LON - 1), group)
    for which in range(2):
        edge = jnp.where(lat_par == which, 1, 0)
        inside = jnp.where(lat_par == which, lat < N_LAT - 1, lat > 0)
        quarter = jnp.where(inside, 0.25, 0.0)
        for k, region in enumerate((0, 1, -1, LON_PAIRS)):
            weight = jnp.where((lane & 1) == edge, quarter * lon_weight(col, region), 0.0)
            weight = weight.astype(jnp.bfloat16)
            weight_ref[4 * which + k] = jnp.concatenate([weight, weight], axis=1)
    parts = []
    for tile in range(0, LAT_TILES, 2):
        some = [rows_ref[t] for t in range(tile, min(tile + 2, LAT_TILES))]
        both = jnp.concatenate(some, axis=1) if len(some) == 2 else some[0]
        total = weighted_product(left_ref, weight_ref, LAT_TERMS, both)
        for t in range(len(some)):
            parts.append(total[:, t * PATCH_CELLS : (t + 1) * PATCH_CELLS])
    edges = lat_lanes(0)
    copies = []
    for first in range(0, FIELDS, CHUNK):
        stop = min(first + CHUNK, FIELDS)
        for field in range(first, stop):
            shift = 2 * (field % LAT_GROUP)
            part = parts[field // LAT_GROUP]
            moved = pltpu.roll(part, PATCH_CELLS - shift, 1) if shift else part
            out_ref[field] = (sum_ref[field] + jnp.where(edges, moved, 0.0)).astype(jnp.bfloat16)
        span = pl.ds(first, stop - first)
        copy = pltpu.make_async_copy(out_ref.at[span], final_ref.at[span], sems.at[first // CHUNK])
        copy.start()
        copies.append(copy)
    for copy in copies:
        copy.wait()


def lat_part(lat_a, lat_b, rows, sums):
    return pl.pallas_call(
        lat_kernel,
        out_shape=jax.ShapeDtypeStruct(sums.shape, jnp.bfloat16),
        in_specs=[VMEM] * 4,
        out_specs=pl.BlockSpec(memory_space=pl.ANY),
        scratch_shapes=[
            pltpu.VMEM((MEMBERS, LAT_TERMS * MEMBERS), jnp.bfloat16),
            pltpu.VMEM((LAT_TERMS, COEF_ROWS, 2 * PATCH_CELLS), jnp.bfloat16),
            pltpu.VMEM((FIELDS, MEMBERS, PATCH_CELLS), jnp.bfloat16),
            pltpu.SemaphoreType.DMA(((FIELDS + CHUNK - 1) // CHUNK,)),
        ],
        compiler_params=pltpu.CompilerParams(vmem_limit_bytes=16 * MIB),
        name="lat_part",
    )(lat_a, lat_b, rows, sums)


def side_kernel(core_ref, swap_ref, edge_ref, sum_ref, out_ref, left_ref, weight_ref):
    f32 = jnp.float32
    bf16 = jnp.bfloat16
    lon_par = lax.axis_index("lon") & 1
    col = cell_lanes(COEF_ROWS)[0]
    for source, ref in enumerate((core_ref, swap_ref)):
        for tile in range(3):
            at = (source * 3 + tile) * 128
            left_ref[:, at : at + 128] = ref[tile * MEMBERS : (tile + 1) * MEMBERS, :]
        mine = col == jnp.where(lon_par == source, CELLS_LON - 1, 0)
        coefs = jnp.where(mine, ref[PAIR_ROWS + MEMBERS :, :].astype(f32), 0.0)
        coefs = coefs + pltpu.roll(coefs, PATCH_CELLS // 2, 1)
        for k in range(6):
            weight_ref[source * 6 + k] = spread(coefs[k : k + 1], 2 * PATCH_CELLS).astype(bf16)
    outer = side_lanes()

    def group(first, count):
        tiles = (count + 1) // 2
        edges = [edge_ref[first // 2 + t] for t in range(tiles)]
        both = jnp.concatenate(edges, axis=1) if tiles == 2 else edges[0]
        total = weighted_product(left_ref, weight_ref, SIDE_TERMS, both)
        for f in range(count):
            piece = total[:, f // 2 * PATCH_CELLS : (f // 2 + 1) * PATCH_CELLS]
            if f % 2:
                piece = pltpu.roll(piece, PATCH_CELLS // 2, 1)
            out_ref[first + f] = sum_ref[first + f] + jnp.where(outer, piece, 0.0)

    for first in range(0, FIELDS, 4):
        group(first, min(4, FIELDS - first))


def side_part(from_core, from_swap, edges, sums):
    bf16 = jnp.bfloat16
    return pl.pallas_call(
        side_kernel,
        out_shape=jax.ShapeDtypeStruct(sums.shape, sums.dtype),
        in_specs=[VMEM] * 4,
        out_specs=VMEM,
        scratch_shapes=[
            pltpu.VMEM((MEMBERS, SIDE_TERMS * MEMBERS), bf16),
            pltpu.VMEM((SIDE_TERMS, COEF_ROWS, 2 * PATCH_CELLS), bf16),
        ],
        cost_estimate=pl.CostEstimate(
            flops=FIELDS * PATCH_CELLS * MEMBERS * MEMBERS * SIDE_TERMS,
            bytes_accessed=FIELDS * MEMBERS * PATCH_CELLS * 7,
            transcendentals=0,
        ),
        compiler_params=pltpu.CompilerParams(vmem_limit_bytes=16 * MIB),
        name="side_part",
    )(from_core, from_swap, edges, sums)


CORES = [(i, i ^ 1) for i in range(32)]


def chip_transforms(
    depth, both, obs_ens, obs_value, obs_prec, slot_owner, info, counts, region_slots
):
    if depth > 1:
        rest = tuple(range(1, depth))
        send, keep, held, _, _ = split_of(rest, slot_owner, obs_ens, obs_value, obs_prec)
        got = lax.ppermute(send, "lon", CORES)
        both = merge_of(held, keep, got, both)
    received = lax.all_to_all(both, "lon", 0, 0, axis_index_groups=SAME_CORE, tiled=True)
    blocks = received.reshape(CHIPS * depth, ROWS, OBS_BLOCK)
    return transforms_of(depth, info, counts, region_slots, blocks)


def shards(background, obs_ens, obs_value, obs_prec, obs_count, slot_owner, region_slots):
    send, keep, held, info, index = split_of((0,), slot_owner, obs_ens, obs_value, obs_prec)
    got = lax.ppermute(send, "lon", CORES)
    both = merge_of(held, keep, got)
    operands = (
        both,
        obs_ens,
        obs_value,
        obs_prec,
        slot_owner,
        info,
        obs_count[:, 0, 0],
        jnp.transpose(region_slots, (0, 2, 1)),
    )
    branches = [functools.partial(chip_transforms, depth) for depth in (1, 2, SLOTS)]
    to_core, to_swap, edge_a, edge_b, coefs = lax.switch(
        index[0, 0], branches, *operands
    )

    swap = [(i, (i + 1) % 32) for i in range(1, 32, 2)] + [((i + 1) % 32, i) for i in range(1, 32, 2)]
    from_swap = lax.ppermute(to_swap, "lon", swap)
    from_core = lax.ppermute(to_core, "lon", CORES)
    state = background.reshape(FIELDS, MEMBERS, PATCH_CELLS)
    sums, edges, rows = own_part(to_core, coefs, state)
    message_a, message_b = pack_of(edge_a, edge_b, from_core, from_swap)
    pairs_a = [(i, i ^ 1) for i in range(8)]
    pairs_b = [(i, (i + 1) % 8) for i in range(1, 8, 2)] + [((i + 1) % 8, i) for i in range(1, 8, 2)]
    lat_b = lax.ppermute(message_b, "lat", pairs_b)
    lat_a = lax.ppermute(message_a, "lat", pairs_a)
    sums = side_part(from_core, from_swap, edges, sums)
    result = lat_part(lat_a, lat_b, rows, sums)
    return result.reshape(FIELDS, MEMBERS, 1, 1, PATCH_CELLS)


def solution(mesh):
    in_specs = (
        P(None, None, "lon", "lat", None),
        P(None, "lat", "lon", None, None, None),
        P(None, "lat", "lon", None, None),
        P(None, "lat", "lon", None, None),
        P(None, "lat", "lon"),
        P(),
        P("lon", "lat", None),
    )
    out_specs = P(None, None, "lon", "lat", None)
    return jax.shard_map(shards, mesh=mesh, in_specs=in_specs, out_specs=out_specs, check_vma=False)
```

```python
import functools
import math

import jax
import jax.numpy as jnp
from jax import lax
from jax.experimental import pallas as pl
from jax.experimental.pallas import tpu as pltpu
from jax.sharding import PartitionSpec as P

MEMBERS = 64
FIELDS = 69
CELLS_LAT = 32
CELLS_LON = 4
PATCH_CELLS = 128
SLOTS = 4
OBS_BLOCK = 128
NEWTON_STEPS = 3
LON_PAIRS = 2
LAT_PAIRS = 16
PAIRS = ((0, 1), (0, 2), (0, 3), (1, 2), (1, 3), (2, 3))
ROWS = 66
PAIR_ROWS = 192
COEF_ROWS = 16
MSG_ROWS = PAIR_ROWS + MEMBERS + COEF_ROWS
CHIPS = 16
N_LAT = 8
SAME_CORE = [[j for j in range(32) if j % 2 == core] for core in range(2)]


def lon_weight(column, region):
    own = column >> 1
    outer = own + jnp.where((column & 1) == 1, 1, -1)
    return jnp.where(own == region, 0.75, jnp.where(outer == region, 0.25, 0.0))


def lat_weight(row, region):
    own = row >> 1
    outer = own + jnp.where((row & 1) == 1, 1, -1)
    return jnp.where(own == region, 0.75, jnp.where(outer == region, 0.25, 0.0))


def cell_lanes(rows):
    lane = lax.broadcasted_iota(jnp.int32, (rows, PATCH_CELLS), 1)
    return lane >> 5, lane & (CELLS_LAT - 1)


SMEM = pl.BlockSpec(memory_space=pltpu.SMEM)
VMEM = pl.BlockSpec(memory_space=pltpu.VMEM)
MIB = 1024 * 1024


def halves(array):
    high = array.astype(jnp.bfloat16)
    return high, (array - high.astype(jnp.float32)).astype(jnp.bfloat16)


def mm(left, right):
    def dot(x, y):
        return lax.dot_general(
            x, y, (((1,), (0,)), ((), ())), preferred_element_type=jnp.float32
        )

    left_high, left_low = halves(left)
    right_high, right_low = halves(right)
    return dot(left_high, right_high) + (dot(left_high, right_low) + dot(left_low, right_high))


def slot_ranks(owner_ref):
    owners = [owner_ref[s] for s in range(SLOTS)]
    ranks = []
    for s in range(SLOTS):
        rank = jnp.int32(0)
        for earlier in range(s):
            rank = rank + jnp.where((owners[earlier] >> 1) == (owners[s] >> 1), 1, 0)
        ranks.append(rank)
    return owners, ranks


def chosen_slot(owners, ranks, chip, q):
    slot = jnp.int32(0)
    owner = jnp.int32(0)
    for s in range(SLOTS):
        match = jnp.logical_and((owners[s] >> 1) == chip, ranks[s] == q)
        slot = jnp.where(match, s, slot)
        owner = jnp.where(match, owners[s], owner)
    return slot, owner


def split_kernel(
    places, owner_ref, ens_ref, value_ref, prec_ref, send_ref, keep_ref, held_ref, info_ref, index_ref,
    rows_ref, small_ref, small_sems, sems,
):
    f32 = jnp.float32
    me = lax.axis_index("lon")
    core = me & 1
    owners, ranks = slot_ranks(owner_ref)
    chosen = [chosen_slot(owners, ranks, me >> 1, q) for q in places]
    slots = [slot for slot, _ in chosen]
    for q, (_, owner) in enumerate(chosen):
        held_ref[q] = jnp.full((COEF_ROWS, OBS_BLOCK), jnp.where((owner & 1) == core, 1.0, 0.0), f32)
    most = ranks[0]
    for s in range(1, SLOTS):
        most = jnp.maximum(most, ranks[s])
    index_ref[...] = jnp.full((8, OBS_BLOCK), jnp.minimum(most, 2), jnp.int32)
    for s in range(SLOTS):
        info_ref[s : s + 1, :] = jnp.full((1, OBS_BLOCK), (owners[s] >> 1).astype(f32), f32)
        info_ref[SLOTS + s : SLOTS + s + 1, :] = jnp.full((1, OBS_BLOCK), ranks[s].astype(f32), f32)
    targets = ((send_ref, 1 - core), (keep_ref, core))
    copies = []
    smalls = []
    for q in range(len(places)):
        for k, ref in enumerate((value_ref, prec_ref)):
            copy = pltpu.make_async_copy(
                ref.at[slots[q]], small_ref.at[2 * q + k], small_sems.at[2 * q + k]
            )
            copy.start()
            smalls.append(copy)
        for k, (ref, side) in enumerate(targets):
            copy = pltpu.make_async_copy(
                ens_ref.at[slots[q], :, side], ref.at[:, q, pl.ds(0, MEMBERS)], sems.at[2 * q + k]
            )
            copy.start()
            copies.append(copy)
    for copy in smalls:
        copy.wait()
    for q in range(len(places)):
        rows_ref[0] = small_ref[2 * q].astype(f32)
        rows_ref[1] = small_ref[2 * q + 1].astype(f32)
        for ref, side in targets:
            value = rows_ref[0, pl.ds(side, CHIPS, stride=2), :]
            prec = rows_ref[1, pl.ds(side, CHIPS, stride=2), :]
            for i in range(CHIPS):
                both = jnp.concatenate([value[i : i + 1], prec[i : i + 1]], axis=0)
                ref[i, q, MEMBERS:ROWS, :] = both.astype(jnp.bfloat16)
    for copy in copies:
        copy.wait()


def split_of(places, slot_owner, obs_ens, obs_value, obs_prec):
    count = len(places)
    shape = jax.ShapeDtypeStruct((CHIPS, count, ROWS, OBS_BLOCK), jnp.bfloat16)
    return pl.pallas_call(
        functools.partial(split_kernel, places),
        out_shape=(
            shape,
            shape,
            jax.ShapeDtypeStruct((count, COEF_ROWS, OBS_BLOCK), jnp.float32),
            jax.ShapeDtypeStruct((2 * SLOTS, OBS_BLOCK), jnp.float32),
            jax.ShapeDtypeStruct((8, OBS_BLOCK), jnp.int32),
        ),
        in_specs=[SMEM] + [pl.BlockSpec(memory_space=pl.ANY)] * 3,
        out_specs=(VMEM,) * 5,
        scratch_shapes=[
            pltpu.VMEM((2, 2 * CHIPS, OBS_BLOCK), jnp.float32),
            pltpu.VMEM((2 * count, 2 * CHIPS, OBS_BLOCK), jnp.bfloat16),
            pltpu.SemaphoreType.DMA((2 * count,)),
            pltpu.SemaphoreType.DMA((2 * count,)),
        ],
        compiler_params=pltpu.CompilerParams(vmem_limit_bytes=16 * MIB),
        name="split",
    )(
        slot_owner,
        obs_ens.reshape(SLOTS, CHIPS, 2, MEMBERS, OBS_BLOCK),
        obs_value.reshape(SLOTS, 2 * CHIPS, OBS_BLOCK),
        obs_prec.reshape(SLOTS, 2 * CHIPS, OBS_BLOCK),
    )


def blend(held, keep, got):
    mine = held.astype(jnp.bfloat16)
    other = (1.0 - held).astype(jnp.bfloat16)
    return keep * mine + got * other


def merge_kernel(held_ref, keep_ref, got_ref, out_ref):
    for q in range(held_ref.shape[0]):
        out_ref[:, q] = blend(held_ref[q, 0:1, :], keep_ref[:, q], got_ref[:, q])


def append_kernel(both_ref, held_ref, keep_ref, got_ref, out_ref):
    out_ref[:, 0] = both_ref[:, 0]
    for q in range(held_ref.shape[0]):
        out_ref[:, 1 + q] = blend(held_ref[q, 0:1, :], keep_ref[:, q], got_ref[:, q])


def merge_of(held, keep, got, both=None):
    count = keep.shape[1]
    operands = (held, keep, got)
    if both is not None:
        count = count + 1
        operands = (both,) + operands
    return pl.pallas_call(
        merge_kernel if both is None else append_kernel,
        out_shape=jax.ShapeDtypeStruct((CHIPS, count, ROWS, OBS_BLOCK), keep.dtype),
        in_specs=[VMEM] * len(operands),
        out_specs=VMEM,
        compiler_params=pltpu.CompilerParams(vmem_limit_bytes=16 * MIB),
        name="merge",
    )(*operands)


def entry(row, lane):
    at = lax.broadcasted_iota(jnp.int32, row.shape, 1)
    return jnp.sum(jnp.where(at == lane, row.astype(jnp.float32), 0.0), axis=1, keepdims=True)


def pair_ids(ids_ref, a):
    one = ids_ref[a, 0:1, :]
    two = ids_ref[a, 1:2, :]
    low = jnp.minimum(one, two)
    high = jnp.maximum(one, two)
    return ((low * (7 - low)) >> 1) + (high - low - 1)


def transform_kernel(
    depth, info_ref, count_ref, ids_ref, block_ref, core_ref, swap_ref, edge_a_ref, edge_b_ref, coef_ref
):
    f32 = jnp.float32
    bf16 = jnp.bfloat16
    members = MEMBERS
    lat_par = lax.axis_index("lat") & 1
    even = (lax.axis_index("lon") & 1) == 0
    row_id = lax.broadcasted_iota(jnp.int32, (members, members), 0)
    col_id = lax.broadcasted_iota(jnp.int32, (members, members), 1)
    identity = jnp.where(row_id == col_id, 1.0, 0.0).astype(f32)
    position = lax.broadcasted_iota(jnp.int32, (1, OBS_BLOCK), 1).astype(f32)
    grams = []
    projs = []
    traces = []
    for slot in range(SLOTS):
        place = info_ref[slot : slot + 1, :] * depth + info_ref[SLOTS + slot : SLOTS + slot + 1, :]
        block = None
        for k in range(CHIPS * depth):
            here = jnp.where(place == k, 1.0, 0.0).astype(bf16)
            part = block_ref[k] * here
            block = part if block is None else block + part
        block = block.astype(f32)
        ens = block[:members]
        value = block[members : members + 1]
        prec = block[members + 1 : members + 2]
        obs_mean = jnp.sum(ens, axis=0, keepdims=True) * (1.0 / members)
        pert = (ens - obs_mean).astype(bf16)
        weight = jnp.where(position < entry(count_ref[...], slot), prec, 0.0)
        weighted = (pert.astype(f32) * weight).astype(bf16)
        diagonal = jnp.sum(weighted.astype(f32) * pert.astype(f32), axis=0, keepdims=True)
        traces.append(jnp.sum(diagonal, axis=1, keepdims=True))
        high, low = halves(value - obs_mean)
        rows = [jnp.broadcast_to(x, (COEF_ROWS, OBS_BLOCK)) for x in (high, low)]
        product = lax.dot_general(
            jnp.concatenate([pert] + rows, axis=0),
            weighted,
            (((1,), (1,)), ((), ())),
            preferred_element_type=f32,
        )
        grams.append(product[:members])
        projs.append(product[members : members + 8] + product[members + COEF_ROWS : members + COEF_ROWS + 8])
    iterates = []
    inverses = []
    scalings = []
    for first, second in PAIRS:
        matrix = grams[first] + grams[second] + (members - 1.0) * identity
        scaling = (traces[first] + traces[second]) * (1.0 / members) + (members - 1.0)
        scalings.append(scaling)
        iterate = matrix * (1.0 / scaling)
        iterates.append(iterate)
        inverses.append(1.5 * identity - 0.5 * iterate)
    sums = [projs[first] + projs[second] for first, second in PAIRS]
    iterates = [mm(x, y) for x, y in zip(iterates, inverses)]
    for step in range(1, NEWTON_STEPS):
        factors = [1.5 * identity - 0.5 * mm(y, x) for x, y in zip(iterates, inverses)]
        if step < NEWTON_STEPS - 1:
            both = [mm(jnp.concatenate([x, y], axis=0), f) for x, y, f in zip(iterates, inverses, factors)]
            iterates = [z[:members] for z in both]
            inverses = [z[members:] for z in both]
        else:
            sums = [mm(p, y) for p, y in zip(sums, inverses)]
            both = [mm(jnp.concatenate([y, p], axis=0), f) for y, p, f in zip(inverses, sums, factors)]
            inverses = [z[:members] for z in both]
            sums = [mm(z[members:], z[:members]) for z in both]
    turned = []
    for pair in range(len(PAIRS)):
        scale = 1.0 / scalings[pair]
        root = math.sqrt(members - 1.0) * jnp.sqrt(scale)
        turned.append(inverses[pair] * root + sums[pair][0:1] * scale)
        lanes = slice(pair % 2 * members, (pair % 2 + 1) * members)
        rows = pl.ds(pair // 2 * members, members)
        core_ref[rows, lanes] = turned[pair].astype(bf16)
        swap_ref[rows, lanes] = turned[pair].astype(bf16)
    ids = [pair_ids(ids_ref, a) for a in range(LON_PAIRS)]
    for which, ref in enumerate((edge_a_ref, edge_b_ref)):
        row = jnp.where(lat_par == which, LAT_PAIRS - 1, 0)
        chosen = []
        for a in range(LON_PAIRS):
            edge = entry(ids[a], row)
            one = turned[0]
            for pair in range(1, len(PAIRS)):
                one = jnp.where(edge == pair, turned[pair], one)
            chosen.append(one)
            ref[:, a * members : (a + 1) * members] = one.astype(bf16)
        lanes = slice(which * members, (which + 1) * members)
        rows = pl.ds(PAIR_ROWS, members)
        core_ref[rows, lanes] = jnp.where(even, chosen[1], chosen[0]).astype(bf16)
        swap_ref[rows, lanes] = jnp.where(even, chosen[0], chosen[1]).astype(bf16)
    tapers = jnp.zeros((COEF_ROWS, 2 * PATCH_CELLS), f32)
    pair_id = lax.broadcasted_iota(jnp.int32, (COEF_ROWS, LAT_PAIRS), 0)
    col, row = cell_lanes(LAT_PAIRS)
    lat_w = lat_weight(row, lax.broadcasted_iota(jnp.int32, (LAT_PAIRS, PATCH_CELLS), 0))
    for a in range(LON_PAIRS):
        hot = jnp.where(pair_id == ids[a], 1.0, 0.0).astype(bf16)
        outer = 0 if a == LON_PAIRS - 1 else CELLS_LON - 1
        table = jnp.concatenate(
            [lat_w * lon_weight(col, a), lat_w * jnp.where(col == outer, 0.25, 0.0)], axis=1
        )
        tapers = tapers + lax.dot_general(
            hot, table.astype(bf16), (((1,), (0,)), ((), ())), preferred_element_type=f32
        )
    coef_ref[...] = tapers[:, :PATCH_CELLS].astype(bf16)
    next_taper = tapers[:, PATCH_CELLS:].astype(bf16)
    core_ref[PAIR_ROWS + members :, :] = next_taper
    swap_ref[PAIR_ROWS + members :, :] = next_taper


def transforms_of(depth, info, counts, region_slots, blocks):
    bf16 = jnp.bfloat16
    wide = jax.ShapeDtypeStruct((MEMBERS, 2 * MEMBERS), bf16)
    coef = jax.ShapeDtypeStruct((COEF_ROWS, PATCH_CELLS), bf16)
    message = jax.ShapeDtypeStruct((MSG_ROWS, 2 * MEMBERS), bf16)
    return pl.pallas_call(
        functools.partial(transform_kernel, depth),
        out_shape=(message, message, wide, wide, coef),
        in_specs=[VMEM] * 4,
        out_specs=(VMEM,) * 5,
        compiler_params=pltpu.CompilerParams(vmem_limit_bytes=16 * MIB),
        name="transforms",
    )(info, counts.reshape(1, SLOTS), region_slots, blocks)


def pack_kernel(edge_a_ref, edge_b_ref, core_ref, swap_ref, out_a_ref, out_b_ref):
    f32 = jnp.float32
    even = (lax.axis_index("lon") & 1) == 0
    first = lax.broadcasted_iota(jnp.int32, (MEMBERS, 2 * MEMBERS), 1) < MEMBERS
    rows = pl.ds(PAIR_ROWS, MEMBERS)
    core = core_ref[rows, :].astype(f32)
    swap = swap_ref[rows, :].astype(f32)
    before = jnp.where(even, swap, core)
    after = jnp.where(even, core, swap)
    out_a_ref[0:MEMBERS] = edge_a_ref[...]
    out_b_ref[0:MEMBERS] = edge_b_ref[...]
    out_a_ref[MEMBERS:] = jnp.where(first, before, pltpu.roll(after, MEMBERS, 1)).astype(jnp.bfloat16)
    out_b_ref[MEMBERS:] = jnp.where(first, pltpu.roll(before, MEMBERS, 1), after).astype(jnp.bfloat16)


def pack_of(edge_a, edge_b, from_core, from_swap):
    shape = jax.ShapeDtypeStruct((2 * MEMBERS, 2 * MEMBERS), jnp.bfloat16)
    return pl.pallas_call(
        pack_kernel,
        out_shape=(shape, shape),
        in_specs=[VMEM] * 4,
        out_specs=(VMEM, VMEM),
        compiler_params=pltpu.CompilerParams(vmem_limit_bytes=4 * MIB),
        name="pack",
    )(edge_a, edge_b, from_core, from_swap)


def spread(row, width):
    tile = jnp.broadcast_to(row, (COEF_ROWS, PATCH_CELLS))
    return jnp.concatenate([tile] * (width // PATCH_CELLS), axis=1)


def weighted_product(left_ref, weight_ref, count, perts):
    width = perts.shape[1]
    total = None
    for first in range(0, count, 4):
        parts = []
        for k in range(first, min(first + 4, count)):
            weight = weight_ref[k, :, 0:width]
            parts.append(perts * jnp.concatenate([weight] * (MEMBERS // COEF_ROWS), axis=0))
        part = lax.dot_general(
            left_ref[:, first * MEMBERS : min(first + 4, count) * MEMBERS],
            jnp.concatenate(parts, axis=0),
            (((1,), (0,)), ((), ())),
            preferred_element_type=jnp.float32,
        )
        total = part if total is None else total + part
    return total


OWN_TERMS = 6
LAT_TERMS = 8
SIDE_TERMS = 12
CHUNK = 16
HALF = (FIELDS + 1) // 2
LAT_GROUP = 16
LAT_TILES = (FIELDS + LAT_GROUP - 1) // LAT_GROUP


def side_lanes():
    lane = lax.broadcasted_iota(jnp.int32, (MEMBERS, PATCH_CELLS), 1)
    return jnp.logical_or(lane < CELLS_LAT, lane >= PATCH_CELLS - CELLS_LAT)


def lat_lanes(field):
    lane = lax.broadcasted_iota(jnp.int32, (MEMBERS, PATCH_CELLS), 1)
    at = (lane - 2 * (field % LAT_GROUP)) & (CELLS_LAT - 1)
    return jnp.logical_or(at == 0, at == CELLS_LAT - 1)


def own_kernel(
    pair_ref, coef_ref, back_ref, sum_ref, edge_ref, rows_ref, left_ref, weight_ref
):
    f32 = jnp.float32
    bf16 = jnp.bfloat16
    for tile in range(3):
        left_ref[:, tile * 128 : (tile + 1) * 128] = pair_ref[tile * MEMBERS : (tile + 1) * MEMBERS, :]
    coefs = coef_ref[...].astype(f32)
    for k in range(OWN_TERMS):
        weight_ref[k] = spread(coefs[k : k + 1], 2 * PATCH_CELLS).astype(bf16)
    outer = side_lanes()

    def pair(first, base, count, rows):
        perts = []
        means = []
        for f in range(count):
            state = back_ref[first + f].astype(f32)
            mean = jnp.sum(state, axis=0, keepdims=True) * (1.0 / MEMBERS)
            means.append(mean)
            perts.append((state - mean).astype(bf16))
        wide = [p.astype(f32) for p in perts]
        inner = pltpu.roll(wide[1], PATCH_CELLS // 2, 1) if count == 2 else 0.0
        edge_ref[first // 2] = jnp.where(outer, wide[0], inner).astype(bf16)
        for f in range(count):
            shift = 2 * ((base + f) % LAT_GROUP)
            moved = pltpu.roll(wide[f], shift, 1) if shift else wide[f]
            rows = jnp.where(lat_lanes(base + f), moved, rows)
        both = jnp.concatenate(perts, axis=1) if count == 2 else perts[0]
        total = weighted_product(left_ref, weight_ref, OWN_TERMS, both)
        for f in range(count):
            sum_ref[first + f] = total[:, f * PATCH_CELLS : (f + 1) * PATCH_CELLS] + means[f]
        return rows

    for tile in range(LAT_TILES):
        rows = jnp.zeros((MEMBERS, PATCH_CELLS), f32)
        last = min((tile + 1) * LAT_GROUP, FIELDS)
        for first in range(tile * LAT_GROUP, last, 2):
            rows = pair(first, first, min(2, last - first), rows)
        rows_ref[tile] = rows.astype(bf16)


def own_part(message, coefs, background):
    def tiles(count, kind):
        return jax.ShapeDtypeStruct((count, MEMBERS, PATCH_CELLS), kind)

    return pl.pallas_call(
        own_kernel,
        out_shape=(
            tiles(FIELDS, jnp.float32),
            tiles(HALF, jnp.bfloat16),
            tiles(LAT_TILES, jnp.bfloat16),
        ),
        in_specs=[VMEM] * 3,
        out_specs=(VMEM,) * 3,
        scratch_shapes=[
            pltpu.VMEM((MEMBERS, OWN_TERMS * MEMBERS), jnp.bfloat16),
            pltpu.VMEM((OWN_TERMS, COEF_ROWS, 2 * PATCH_CELLS), jnp.bfloat16),
        ],
        cost_estimate=pl.CostEstimate(
            flops=2 * FIELDS * PATCH_CELLS * MEMBERS * MEMBERS * OWN_TERMS,
            bytes_accessed=FIELDS * MEMBERS * PATCH_CELLS * 8,
            transcendentals=0,
        ),
        compiler_params=pltpu.CompilerParams(vmem_limit_bytes=16 * MIB),
        name="own_part",
    )(message, coefs, background)


def lat_weights():
    lat = lax.axis_index("lat")
    lat_par = lat & 1
    lane = lax.broadcasted_iota(jnp.int32, (COEF_ROWS, PATCH_CELLS), 1)
    group = lane >> 5
    last = (lane & 1) == 1
    before = jnp.logical_and(last, (lane & (CELLS_LAT - 1)) != CELLS_LAT - 1)
    col = jnp.where(before, (group + CELLS_LON - 1) & (CELLS_LON - 1), group)
    weights = []
    for which in range(2):
        edge = jnp.where(lat_par == which, 1, 0)
        inside = jnp.where(lat_par == which, lat < N_LAT - 1, lat > 0)
        quarter = jnp.where(inside, 0.25, 0.0)
        for region in (0, 1, -1, LON_PAIRS):
            weight = jnp.where((lane & 1) == edge, quarter * lon_weight(col, region), 0.0)
            weights.append(weight.astype(jnp.bfloat16))
    return weights


def lat_kernel(lat_a_ref, lat_b_ref, right_ref, sum_ref, final_ref, left_ref, out_ref, sems):
    for which, ref in enumerate((lat_a_ref, lat_b_ref)):
        for tile in range(2):
            at = (2 * which + tile) * 128
            left_ref[:, at : at + 128] = ref[tile * MEMBERS : (tile + 1) * MEMBERS, :]
    parts = []
    for tile in range(LAT_TILES):
        parts.append(
            lax.dot_general(
                left_ref[...],
                right_ref[tile],
                (((1,), (0,)), ((), ())),
                preferred_element_type=jnp.float32,
            )
        )
    edges = lat_lanes(0)
    copies = []
    for first in range(0, FIELDS, CHUNK):
        stop = min(first + CHUNK, FIELDS)
        for field in range(first, stop):
            shift = 2 * (field % LAT_GROUP)
            part = parts[field // LAT_GROUP]
            moved = pltpu.roll(part, PATCH_CELLS - shift, 1) if shift else part
            out_ref[field] = (sum_ref[field] + jnp.where(edges, moved, 0.0)).astype(jnp.bfloat16)
        span = pl.ds(first, stop - first)
        copy = pltpu.make_async_copy(out_ref.at[span], final_ref.at[span], sems.at[first // CHUNK])
        copy.start()
        copies.append(copy)
    for copy in copies:
        copy.wait()


def lat_part(lat_a, lat_b, right, sums):
    return pl.pallas_call(
        lat_kernel,
        out_shape=jax.ShapeDtypeStruct(sums.shape, jnp.bfloat16),
        in_specs=[VMEM] * 4,
        out_specs=pl.BlockSpec(memory_space=pl.ANY),
        scratch_shapes=[
            pltpu.VMEM((MEMBERS, LAT_TERMS * MEMBERS), jnp.bfloat16),
            pltpu.VMEM((FIELDS, MEMBERS, PATCH_CELLS), jnp.bfloat16),
            pltpu.SemaphoreType.DMA(((FIELDS + CHUNK - 1) // CHUNK,)),
        ],
        compiler_params=pltpu.CompilerParams(vmem_limit_bytes=16 * MIB),
        name="lat_part",
    )(lat_a, lat_b, right, sums)


def side_kernel(
    core_ref, swap_ref, edge_ref, rows_ref, sum_ref, out_ref, right_ref, left_ref, weight_ref
):
    f32 = jnp.float32
    bf16 = jnp.bfloat16
    lon_par = lax.axis_index("lon") & 1
    col = cell_lanes(COEF_ROWS)[0]
    for source, ref in enumerate((core_ref, swap_ref)):
        for tile in range(3):
            at = (source * 3 + tile) * 128
            left_ref[:, at : at + 128] = ref[tile * MEMBERS : (tile + 1) * MEMBERS, :]
        mine = col == jnp.where(lon_par == source, CELLS_LON - 1, 0)
        coefs = jnp.where(mine, ref[PAIR_ROWS + MEMBERS :, :].astype(f32), 0.0)
        coefs = coefs + pltpu.roll(coefs, PATCH_CELLS // 2, 1)
        for k in range(6):
            weight_ref[source * 6 + k] = spread(coefs[k : k + 1], 2 * PATCH_CELLS).astype(bf16)
    for k, weight in enumerate(lat_weights()):
        weight = jnp.concatenate([weight] * (MEMBERS // COEF_ROWS), axis=0)
        for tile in range(LAT_TILES):
            right_ref[tile, pl.ds(k * MEMBERS, MEMBERS), :] = rows_ref[tile] * weight
    outer = side_lanes()

    def group(first, count):
        tiles = (count + 1) // 2
        edges = [edge_ref[first // 2 + t] for t in range(tiles)]
        both = jnp.concatenate(edges, axis=1) if tiles == 2 else edges[0]
        total = weighted_product(left_ref, weight_ref, SIDE_TERMS, both)
        for f in range(count):
            piece = total[:, f // 2 * PATCH_CELLS : (f // 2 + 1) * PATCH_CELLS]
            if f % 2:
                piece = pltpu.roll(piece, PATCH_CELLS // 2, 1)
            out_ref[first + f] = sum_ref[first + f] + jnp.where(outer, piece, 0.0)

    for first in range(0, FIELDS, 4):
        group(first, min(4, FIELDS - first))


def side_part(from_core, from_swap, edges, rows, sums):
    bf16 = jnp.bfloat16
    return pl.pallas_call(
        side_kernel,
        out_shape=(
            jax.ShapeDtypeStruct(sums.shape, sums.dtype),
            jax.ShapeDtypeStruct((LAT_TILES, LAT_TERMS * MEMBERS, PATCH_CELLS), bf16),
        ),
        in_specs=[VMEM] * 5,
        out_specs=(VMEM, VMEM),
        scratch_shapes=[
            pltpu.VMEM((MEMBERS, SIDE_TERMS * MEMBERS), bf16),
            pltpu.VMEM((SIDE_TERMS, COEF_ROWS, 2 * PATCH_CELLS), bf16),
        ],
        cost_estimate=pl.CostEstimate(
            flops=FIELDS * PATCH_CELLS * MEMBERS * MEMBERS * SIDE_TERMS,
            bytes_accessed=FIELDS * MEMBERS * PATCH_CELLS * 7,
            transcendentals=0,
        ),
        compiler_params=pltpu.CompilerParams(vmem_limit_bytes=16 * MIB),
        name="side_part",
    )(from_core, from_swap, edges, rows, sums)


CORES = [(i, i ^ 1) for i in range(32)]


def chip_transforms(
    depth, both, obs_ens, obs_value, obs_prec, slot_owner, info, counts, region_slots
):
    if depth > 1:
        rest = tuple(range(1, depth))
        send, keep, held, _, _ = split_of(rest, slot_owner, obs_ens, obs_value, obs_prec)
        got = lax.ppermute(send, "lon", CORES)
        both = merge_of(held, keep, got, both)
    received = lax.all_to_all(both, "lon", 0, 0, axis_index_groups=SAME_CORE, tiled=True)
    blocks = received.reshape(CHIPS * depth, ROWS, OBS_BLOCK)
    return transforms_of(depth, info, counts, region_slots, blocks)


def shards(background, obs_ens, obs_value, obs_prec, obs_count, slot_owner, region_slots):
    send, keep, held, info, index = split_of((0,), slot_owner, obs_ens, obs_value, obs_prec)
    got = lax.ppermute(send, "lon", CORES)
    both = merge_of(held, keep, got)
    operands = (
        both,
        obs_ens,
        obs_value,
        obs_prec,
        slot_owner,
        info,
        obs_count[:, 0, 0],
        jnp.transpose(region_slots, (0, 2, 1)),
    )
    branches = [functools.partial(chip_transforms, depth) for depth in (1, 2, SLOTS)]
    to_core, to_swap, edge_a, edge_b, coefs = lax.switch(
        index[0, 0], branches, *operands
    )

    swap = [(i, (i + 1) % 32) for i in range(1, 32, 2)] + [((i + 1) % 32, i) for i in range(1, 32, 2)]
    from_core = lax.ppermute(to_core, "lon", CORES)
    from_swap = lax.ppermute(to_swap, "lon", swap)
    state = background.reshape(FIELDS, MEMBERS, PATCH_CELLS)
    sums, edges, rows = own_part(to_core, coefs, state)
    message_a, message_b = pack_of(edge_a, edge_b, from_core, from_swap)
    pairs_a = [(i, i ^ 1) for i in range(8)]
    pairs_b = []
    for i in range(N_LAT):
        for j in range(32):
            if i in (0, N_LAT - 1):
                target = i * 32 + (j ^ 1)
            else:
                target = (i + 1 if i % 2 else i - 1) * 32 + j
            pairs_b.append((i * 32 + j, target))
    lat_b = lax.ppermute(message_b, ("lat", "lon"), pairs_b)
    lat_a = lax.ppermute(message_a, "lat", pairs_a)
    sums, right = side_part(from_core, from_swap, edges, rows, sums)
    result = lat_part(lat_a, lat_b, right, sums)
    return result.reshape(FIELDS, MEMBERS, 1, 1, PATCH_CELLS)


def solution(mesh):
    in_specs = (
        P(None, None, "lon", "lat", None),
        P(None, "lat", "lon", None, None, None),
        P(None, "lat", "lon", None, None),
        P(None, "lat", "lon", None, None),
        P(None, "lat", "lon"),
        P(),
        P("lon", "lat", None),
    )
    out_specs = P(None, None, "lon", "lat", None)
    return jax.shard_map(shards, mesh=mesh, in_specs=in_specs, out_specs=out_specs, check_vma=False)
```

```python
import functools
import math

import jax
import jax.numpy as jnp
from jax import lax
from jax.experimental import pallas as pl
from jax.experimental.pallas import tpu as pltpu
from jax.sharding import PartitionSpec as P

MEMBERS = 64
FIELDS = 69
CELLS_LAT = 32
CELLS_LON = 4
PATCH_CELLS = 128
SLOTS = 4
OBS_BLOCK = 128
NEWTON_STEPS = 3
LON_PAIRS = 2
LAT_PAIRS = 16
PAIRS = ((0, 1), (0, 2), (0, 3), (1, 2), (1, 3), (2, 3))
ROWS = 66
PAIR_ROWS = 192
COEF_ROWS = 16
MSG_ROWS = PAIR_ROWS + MEMBERS + COEF_ROWS
CHIPS = 16
N_LAT = 8
SAME_CORE = [[j for j in range(32) if j % 2 == core] for core in range(2)]


def lon_weight(column, region):
    own = column >> 1
    outer = own + jnp.where((column & 1) == 1, 1, -1)
    return jnp.where(own == region, 0.75, jnp.where(outer == region, 0.25, 0.0))


def lat_weight(row, region):
    own = row >> 1
    outer = own + jnp.where((row & 1) == 1, 1, -1)
    return jnp.where(own == region, 0.75, jnp.where(outer == region, 0.25, 0.0))


def cell_lanes(rows):
    lane = lax.broadcasted_iota(jnp.int32, (rows, PATCH_CELLS), 1)
    return lane >> 5, lane & (CELLS_LAT - 1)


SMEM = pl.BlockSpec(memory_space=pltpu.SMEM)
VMEM = pl.BlockSpec(memory_space=pltpu.VMEM)
MIB = 1024 * 1024


def halves(array):
    high = array.astype(jnp.bfloat16)
    return high, (array - high.astype(jnp.float32)).astype(jnp.bfloat16)


def mm(left, right):
    def dot(x, y):
        return lax.dot_general(
            x, y, (((1,), (0,)), ((), ())), preferred_element_type=jnp.float32
        )

    left_high, left_low = halves(left)
    right_high, right_low = halves(right)
    return dot(left_high, right_high) + (dot(left_high, right_low) + dot(left_low, right_high))


def slot_ranks(owner_ref):
    owners = [owner_ref[s] for s in range(SLOTS)]
    ranks = []
    for s in range(SLOTS):
        rank = jnp.int32(0)
        for earlier in range(s):
            rank = rank + jnp.where((owners[earlier] >> 1) == (owners[s] >> 1), 1, 0)
        ranks.append(rank)
    return owners, ranks


def chosen_slot(owners, ranks, chip, q):
    slot = jnp.int32(0)
    owner = jnp.int32(0)
    for s in range(SLOTS):
        match = jnp.logical_and((owners[s] >> 1) == chip, ranks[s] == q)
        slot = jnp.where(match, s, slot)
        owner = jnp.where(match, owners[s], owner)
    return slot, owner


def split_kernel(
    places, owner_ref, ens_ref, value_ref, prec_ref, send_ref, keep_ref, held_ref, info_ref, index_ref,
    rows_ref, small_ref, small_sems, sems,
):
    f32 = jnp.float32
    me = lax.axis_index("lon")
    core = me & 1
    owners, ranks = slot_ranks(owner_ref)
    chosen = [chosen_slot(owners, ranks, me >> 1, q) for q in places]
    slots = [slot for slot, _ in chosen]
    for q, (_, owner) in enumerate(chosen):
        held_ref[q] = jnp.full((COEF_ROWS, OBS_BLOCK), jnp.where((owner & 1) == core, 1.0, 0.0), f32)
    most = ranks[0]
    for s in range(1, SLOTS):
        most = jnp.maximum(most, ranks[s])
    index_ref[...] = jnp.full((8, OBS_BLOCK), jnp.minimum(most, 2), jnp.int32)
    for s in range(SLOTS):
        info_ref[s : s + 1, :] = jnp.full((1, OBS_BLOCK), (owners[s] >> 1).astype(f32), f32)
        info_ref[SLOTS + s : SLOTS + s + 1, :] = jnp.full((1, OBS_BLOCK), ranks[s].astype(f32), f32)
    targets = ((send_ref, 1 - core), (keep_ref, core))
    copies = []
    smalls = []
    for q in range(len(places)):
        for k, ref in enumerate((value_ref, prec_ref)):
            copy = pltpu.make_async_copy(
                ref.at[slots[q]], small_ref.at[2 * q + k], small_sems.at[2 * q + k]
            )
            copy.start()
            smalls.append(copy)
        for k, (ref, side) in enumerate(targets):
            copy = pltpu.make_async_copy(
                ens_ref.at[slots[q], :, side], ref.at[:, q, pl.ds(0, MEMBERS)], sems.at[2 * q + k]
            )
            copy.start()
            copies.append(copy)
    for copy in smalls:
        copy.wait()
    for q in range(len(places)):
        rows_ref[0, 0 : 2 * CHIPS] = small_ref[2 * q].astype(f32)
        rows_ref[1, 0 : 2 * CHIPS] = small_ref[2 * q + 1].astype(f32)
        for ref, side in targets:
            value = rows_ref[0, pl.ds(side, CHIPS, stride=2), :]
            prec = rows_ref[1, pl.ds(side, CHIPS, stride=2), :]
            for i in range(CHIPS):
                both = jnp.concatenate([value[i : i + 1], prec[i : i + 1]], axis=0)
                ref[i, q, MEMBERS:ROWS, :] = both.astype(jnp.bfloat16)
    for copy in copies:
        copy.wait()


def split_of(places, slot_owner, obs_ens, obs_value, obs_prec):
    count = len(places)
    shape = jax.ShapeDtypeStruct((CHIPS, count, ROWS, OBS_BLOCK), jnp.bfloat16)
    return pl.pallas_call(
        functools.partial(split_kernel, places),
        out_shape=(
            shape,
            shape,
            jax.ShapeDtypeStruct((count, COEF_ROWS, OBS_BLOCK), jnp.float32),
            jax.ShapeDtypeStruct((2 * SLOTS, OBS_BLOCK), jnp.float32),
            jax.ShapeDtypeStruct((8, OBS_BLOCK), jnp.int32),
        ),
        in_specs=[SMEM] + [pl.BlockSpec(memory_space=pl.ANY)] * 3,
        out_specs=(VMEM,) * 5,
        scratch_shapes=[
            pltpu.VMEM((2, 2 * CHIPS + 8, OBS_BLOCK), jnp.float32),
            pltpu.VMEM((2 * count, 2 * CHIPS, OBS_BLOCK), jnp.bfloat16),
            pltpu.SemaphoreType.DMA((2 * count,)),
            pltpu.SemaphoreType.DMA((2 * count,)),
        ],
        compiler_params=pltpu.CompilerParams(vmem_limit_bytes=16 * MIB),
        name="split",
    )(
        slot_owner,
        obs_ens.reshape(SLOTS, CHIPS, 2, MEMBERS, OBS_BLOCK),
        obs_value.reshape(SLOTS, 2 * CHIPS, OBS_BLOCK),
        obs_prec.reshape(SLOTS, 2 * CHIPS, OBS_BLOCK),
    )


def blend(held, keep, got):
    mine = held.astype(jnp.bfloat16)
    other = (1.0 - held).astype(jnp.bfloat16)
    return keep * mine + got * other


def merge_kernel(held_ref, keep_ref, got_ref, out_ref):
    for q in range(held_ref.shape[0]):
        out_ref[:, q] = blend(held_ref[q, 0:1, :], keep_ref[:, q], got_ref[:, q])


def append_kernel(both_ref, held_ref, keep_ref, got_ref, out_ref):
    out_ref[:, 0] = both_ref[:, 0]
    for q in range(held_ref.shape[0]):
        out_ref[:, 1 + q] = blend(held_ref[q, 0:1, :], keep_ref[:, q], got_ref[:, q])


def merge_of(held, keep, got, both=None):
    count = keep.shape[1]
    operands = (held, keep, got)
    if both is not None:
        count = count + 1
        operands = (both,) + operands
    return pl.pallas_call(
        merge_kernel if both is None else append_kernel,
        out_shape=jax.ShapeDtypeStruct((CHIPS, count, ROWS, OBS_BLOCK), keep.dtype),
        in_specs=[VMEM] * len(operands),
        out_specs=VMEM,
        compiler_params=pltpu.CompilerParams(vmem_limit_bytes=16 * MIB),
        name="merge",
    )(*operands)


def entry(row, lane):
    at = lax.broadcasted_iota(jnp.int32, row.shape, 1)
    return jnp.sum(jnp.where(at == lane, row.astype(jnp.float32), 0.0), axis=1, keepdims=True)


def pair_ids(ids_ref, a):
    one = ids_ref[a, 0:1, :]
    two = ids_ref[a, 1:2, :]
    low = jnp.minimum(one, two)
    high = jnp.maximum(one, two)
    return ((low * (7 - low)) >> 1) + (high - low - 1)


def transform_kernel(
    depth, info_ref, count_ref, ids_ref, block_ref, core_ref, swap_ref, edge_a_ref, edge_b_ref, coef_ref
):
    f32 = jnp.float32
    bf16 = jnp.bfloat16
    members = MEMBERS
    lat_par = lax.axis_index("lat") & 1
    even = (lax.axis_index("lon") & 1) == 0
    row_id = lax.broadcasted_iota(jnp.int32, (members, members), 0)
    col_id = lax.broadcasted_iota(jnp.int32, (members, members), 1)
    identity = jnp.where(row_id == col_id, 1.0, 0.0).astype(f32)
    position = lax.broadcasted_iota(jnp.int32, (1, OBS_BLOCK), 1).astype(f32)
    grams = []
    projs = []
    traces = []
    for slot in range(SLOTS):
        place = info_ref[slot : slot + 1, :] * depth + info_ref[SLOTS + slot : SLOTS + slot + 1, :]
        block = None
        for k in range(CHIPS * depth):
            here = jnp.where(place == k, 1.0, 0.0).astype(bf16)
            part = block_ref[k] * here
            block = part if block is None else block + part
        block = block.astype(f32)
        ens = block[:members]
        value = block[members : members + 1]
        prec = block[members + 1 : members + 2]
        obs_mean = jnp.sum(ens, axis=0, keepdims=True) * (1.0 / members)
        pert = (ens - obs_mean).astype(bf16)
        weight = jnp.where(position < entry(count_ref[...], slot), prec, 0.0)
        weighted = (pert.astype(f32) * weight).astype(bf16)
        diagonal = jnp.sum(weighted.astype(f32) * pert.astype(f32), axis=0, keepdims=True)
        traces.append(jnp.sum(diagonal, axis=1, keepdims=True))
        high, low = halves(value - obs_mean)
        rows = [jnp.broadcast_to(x, (COEF_ROWS, OBS_BLOCK)) for x in (high, low)]
        product = lax.dot_general(
            jnp.concatenate([pert] + rows, axis=0),
            weighted,
            (((1,), (1,)), ((), ())),
            preferred_element_type=f32,
        )
        grams.append(product[:members])
        projs.append(product[members : members + 8] + product[members + COEF_ROWS : members + COEF_ROWS + 8])
    iterates = []
    inverses = []
    scalings = []
    for first, second in PAIRS:
        matrix = grams[first] + grams[second] + (members - 1.0) * identity
        scaling = (traces[first] + traces[second]) * (1.0 / members) + (members - 1.0)
        scalings.append(scaling)
        iterate = matrix * (1.0 / scaling)
        iterates.append(iterate)
        inverses.append(1.5 * identity - 0.5 * iterate)
    sums = [projs[first] + projs[second] for first, second in PAIRS]
    iterates = [mm(x, y) for x, y in zip(iterates, inverses)]
    for step in range(1, NEWTON_STEPS):
        factors = [1.5 * identity - 0.5 * mm(y, x) for x, y in zip(iterates, inverses)]
        if step < NEWTON_STEPS - 1:
            both = [mm(jnp.concatenate([x, y], axis=0), f) for x, y, f in zip(iterates, inverses, factors)]
            iterates = [z[:members] for z in both]
            inverses = [z[members:] for z in both]
        else:
            sums = [mm(p, y) for p, y in zip(sums, inverses)]
            both = [mm(jnp.concatenate([y, p], axis=0), f) for y, p, f in zip(inverses, sums, factors)]
            inverses = [z[:members] for z in both]
            sums = [mm(z[members:], z[:members]) for z in both]
    turned = []
    for pair in range(len(PAIRS)):
        scale = 1.0 / scalings[pair]
        root = math.sqrt(members - 1.0) * jnp.sqrt(scale)
        turned.append(inverses[pair] * root + sums[pair][0:1] * scale)
        lanes = slice(pair % 2 * members, (pair % 2 + 1) * members)
        rows = pl.ds(pair // 2 * members, members)
        core_ref[rows, lanes] = turned[pair].astype(bf16)
        swap_ref[rows, lanes] = turned[pair].astype(bf16)
    ids = [pair_ids(ids_ref, a) for a in range(LON_PAIRS)]
    for which, ref in enumerate((edge_a_ref, edge_b_ref)):
        row = jnp.where(lat_par == which, LAT_PAIRS - 1, 0)
        chosen = []
        for a in range(LON_PAIRS):
            edge = entry(ids[a], row)
            one = turned[0]
            for pair in range(1, len(PAIRS)):
                one = jnp.where(edge == pair, turned[pair], one)
            chosen.append(one)
            ref[:, a * members : (a + 1) * members] = one.astype(bf16)
        lanes = slice(which * members, (which + 1) * members)
        rows = pl.ds(PAIR_ROWS, members)
        core_ref[rows, lanes] = jnp.where(even, chosen[1], chosen[0]).astype(bf16)
        swap_ref[rows, lanes] = jnp.where(even, chosen[0], chosen[1]).astype(bf16)
    tapers = jnp.zeros((COEF_ROWS, 2 * PATCH_CELLS), f32)
    pair_id = lax.broadcasted_iota(jnp.int32, (COEF_ROWS, LAT_PAIRS), 0)
    col, row = cell_lanes(LAT_PAIRS)
    lat_w = lat_weight(row, lax.broadcasted_iota(jnp.int32, (LAT_PAIRS, PATCH_CELLS), 0))
    for a in range(LON_PAIRS):
        hot = jnp.where(pair_id == ids[a], 1.0, 0.0).astype(bf16)
        outer = 0 if a == LON_PAIRS - 1 else CELLS_LON - 1
        table = jnp.concatenate(
            [lat_w * lon_weight(col, a), lat_w * jnp.where(col == outer, 0.25, 0.0)], axis=1
        )
        tapers = tapers + lax.dot_general(
            hot, table.astype(bf16), (((1,), (0,)), ((), ())), preferred_element_type=f32
        )
    coef_ref[...] = tapers[:, :PATCH_CELLS].astype(bf16)
    next_taper = tapers[:, PATCH_CELLS:].astype(bf16)
    core_ref[PAIR_ROWS + members :, :] = next_taper
    swap_ref[PAIR_ROWS + members :, :] = next_taper


def transforms_of(depth, info, counts, region_slots, blocks):
    bf16 = jnp.bfloat16
    wide = jax.ShapeDtypeStruct((MEMBERS, 2 * MEMBERS), bf16)
    coef = jax.ShapeDtypeStruct((COEF_ROWS, PATCH_CELLS), bf16)
    message = jax.ShapeDtypeStruct((MSG_ROWS, 2 * MEMBERS), bf16)
    return pl.pallas_call(
        functools.partial(transform_kernel, depth),
        out_shape=(message, message, wide, wide, coef),
        in_specs=[VMEM] * 4,
        out_specs=(VMEM,) * 5,
        compiler_params=pltpu.CompilerParams(vmem_limit_bytes=16 * MIB),
        name="transforms",
    )(info, counts.reshape(1, SLOTS), region_slots, blocks)


def pack_kernel(edge_a_ref, edge_b_ref, core_ref, swap_ref, out_a_ref, out_b_ref):
    f32 = jnp.float32
    even = (lax.axis_index("lon") & 1) == 0
    first = lax.broadcasted_iota(jnp.int32, (MEMBERS, 2 * MEMBERS), 1) < MEMBERS
    rows = pl.ds(PAIR_ROWS, MEMBERS)
    core = core_ref[rows, :].astype(f32)
    swap = swap_ref[rows, :].astype(f32)
    before = jnp.where(even, swap, core)
    after = jnp.where(even, core, swap)
    out_a_ref[0:MEMBERS] = edge_a_ref[...]
    out_b_ref[0:MEMBERS] = edge_b_ref[...]
    out_a_ref[MEMBERS:] = jnp.where(first, before, pltpu.roll(after, MEMBERS, 1)).astype(jnp.bfloat16)
    out_b_ref[MEMBERS:] = jnp.where(first, pltpu.roll(before, MEMBERS, 1), after).astype(jnp.bfloat16)


def pack_of(edge_a, edge_b, from_core, from_swap):
    shape = jax.ShapeDtypeStruct((2 * MEMBERS, 2 * MEMBERS), jnp.bfloat16)
    return pl.pallas_call(
        pack_kernel,
        out_shape=(shape, shape),
        in_specs=[VMEM] * 4,
        out_specs=(VMEM, VMEM),
        compiler_params=pltpu.CompilerParams(vmem_limit_bytes=4 * MIB),
        name="pack",
    )(edge_a, edge_b, from_core, from_swap)


def spread(row, width):
    tile = jnp.broadcast_to(row, (COEF_ROWS, PATCH_CELLS))
    return jnp.concatenate([tile] * (width // PATCH_CELLS), axis=1)


def weighted_product(left_ref, weight_ref, count, perts):
    width = perts.shape[1]
    total = None
    for first in range(0, count, 4):
        parts = []
        for k in range(first, min(first + 4, count)):
            weight = weight_ref[k, :, 0:width]
            parts.append(perts * jnp.concatenate([weight] * (MEMBERS // COEF_ROWS), axis=0))
        part = lax.dot_general(
            left_ref[:, first * MEMBERS : min(first + 4, count) * MEMBERS],
            jnp.concatenate(parts, axis=0),
            (((1,), (0,)), ((), ())),
            preferred_element_type=jnp.float32,
        )
        total = part if total is None else total + part
    return total


OWN_TERMS = 6
LAT_TERMS = 8
SIDE_TERMS = 12
CHUNK = 16
HALF = (FIELDS + 1) // 2
LAT_GROUP = 16
LAT_TILES = (FIELDS + LAT_GROUP - 1) // LAT_GROUP


def side_lanes():
    lane = lax.broadcasted_iota(jnp.int32, (MEMBERS, PATCH_CELLS), 1)
    return jnp.logical_or(lane < CELLS_LAT, lane >= PATCH_CELLS - CELLS_LAT)


def lat_lanes(field):
    lane = lax.broadcasted_iota(jnp.int32, (MEMBERS, PATCH_CELLS), 1)
    at = (lane - 2 * (field % LAT_GROUP)) & (CELLS_LAT - 1)
    return jnp.logical_or(at == 0, at == CELLS_LAT - 1)


def own_kernel(
    pair_ref, coef_ref, back_ref, sum_ref, edge_ref, rows_ref, left_ref, weight_ref
):
    f32 = jnp.float32
    bf16 = jnp.bfloat16
    for tile in range(3):
        left_ref[:, tile * 128 : (tile + 1) * 128] = pair_ref[tile * MEMBERS : (tile + 1) * MEMBERS, :]
    coefs = coef_ref[...].astype(f32)
    for k in range(OWN_TERMS):
        weight_ref[k] = spread(coefs[k : k + 1], 2 * PATCH_CELLS).astype(bf16)
    outer = side_lanes()

    def pair(first, base, count, rows):
        perts = []
        means = []
        for f in range(count):
            state = back_ref[first + f].astype(f32)
            mean = jnp.sum(state, axis=0, keepdims=True) * (1.0 / MEMBERS)
            means.append(mean)
            perts.append((state - mean).astype(bf16))
        wide = [p.astype(f32) for p in perts]
        inner = pltpu.roll(wide[1], PATCH_CELLS // 2, 1) if count == 2 else 0.0
        edge_ref[first // 2] = jnp.where(outer, wide[0], inner).astype(bf16)
        for f in range(count):
            shift = 2 * ((base + f) % LAT_GROUP)
            moved = pltpu.roll(wide[f], shift, 1) if shift else wide[f]
            rows = jnp.where(lat_lanes(base + f), moved, rows)
        both = jnp.concatenate(perts, axis=1) if count == 2 else perts[0]
        total = weighted_product(left_ref, weight_ref, OWN_TERMS, both)
        for f in range(count):
            sum_ref[first + f] = total[:, f * PATCH_CELLS : (f + 1) * PATCH_CELLS] + means[f]
        return rows

    for tile in range(LAT_TILES):
        rows = jnp.zeros((MEMBERS, PATCH_CELLS), f32)
        last = min((tile + 1) * LAT_GROUP, FIELDS)
        for first in range(tile * LAT_GROUP, last, 2):
            rows = pair(first, first, min(2, last - first), rows)
        rows_ref[tile] = rows.astype(bf16)


def own_part(message, coefs, background):
    def tiles(count, kind):
        return jax.ShapeDtypeStruct((count, MEMBERS, PATCH_CELLS), kind)

    return pl.pallas_call(
        own_kernel,
        out_shape=(
            tiles(FIELDS, jnp.float32),
            tiles(HALF, jnp.bfloat16),
            tiles(LAT_TILES, jnp.bfloat16),
        ),
        in_specs=[VMEM] * 3,
        out_specs=(VMEM,) * 3,
        scratch_shapes=[
            pltpu.VMEM((MEMBERS, OWN_TERMS * MEMBERS), jnp.bfloat16),
            pltpu.VMEM((OWN_TERMS, COEF_ROWS, 2 * PATCH_CELLS), jnp.bfloat16),
        ],
        cost_estimate=pl.CostEstimate(
            flops=2 * FIELDS * PATCH_CELLS * MEMBERS * MEMBERS * OWN_TERMS,
            bytes_accessed=FIELDS * MEMBERS * PATCH_CELLS * 8,
            transcendentals=0,
        ),
        compiler_params=pltpu.CompilerParams(vmem_limit_bytes=16 * MIB),
        name="own_part",
    )(message, coefs, background)


def lat_weights():
    lat = lax.axis_index("lat")
    lat_par = lat & 1
    lane = lax.broadcasted_iota(jnp.int32, (COEF_ROWS, PATCH_CELLS), 1)
    group = lane >> 5
    last = (lane & 1) == 1
    before = jnp.logical_and(last, (lane & (CELLS_LAT - 1)) != CELLS_LAT - 1)
    col = jnp.where(before, (group + CELLS_LON - 1) & (CELLS_LON - 1), group)
    weights = []
    for which in range(2):
        edge = jnp.where(lat_par == which, 1, 0)
        inside = jnp.where(lat_par == which, lat < N_LAT - 1, lat > 0)
        quarter = jnp.where(inside, 0.25, 0.0)
        for region in (0, 1, -1, LON_PAIRS):
            weight = jnp.where((lane & 1) == edge, quarter * lon_weight(col, region), 0.0)
            weights.append(weight.astype(jnp.bfloat16))
    return weights


def lat_kernel(lat_a_ref, lat_b_ref, right_ref, sum_ref, final_ref, left_ref, out_ref, sems):
    for which, ref in enumerate((lat_a_ref, lat_b_ref)):
        for tile in range(2):
            at = (2 * which + tile) * 128
            left_ref[:, at : at + 128] = ref[tile * MEMBERS : (tile + 1) * MEMBERS, :]
    parts = []
    for tile in range(LAT_TILES):
        parts.append(
            lax.dot_general(
                left_ref[...],
                right_ref[tile],
                (((1,), (0,)), ((), ())),
                preferred_element_type=jnp.float32,
            )
        )
    edges = lat_lanes(0)
    copies = []
    for first in range(0, FIELDS, CHUNK):
        stop = min(first + CHUNK, FIELDS)
        for field in range(first, stop):
            shift = 2 * (field % LAT_GROUP)
            part = parts[field // LAT_GROUP]
            moved = pltpu.roll(part, PATCH_CELLS - shift, 1) if shift else part
            out_ref[field] = (sum_ref[field] + jnp.where(edges, moved, 0.0)).astype(jnp.bfloat16)
        span = pl.ds(first, stop - first)
        copy = pltpu.make_async_copy(out_ref.at[span], final_ref.at[span], sems.at[first // CHUNK])
        copy.start()
        copies.append(copy)
    for copy in copies:
        copy.wait()


def lat_part(lat_a, lat_b, right, sums):
    return pl.pallas_call(
        lat_kernel,
        out_shape=jax.ShapeDtypeStruct(sums.shape, jnp.bfloat16),
        in_specs=[VMEM] * 4,
        out_specs=pl.BlockSpec(memory_space=pl.ANY),
        scratch_shapes=[
            pltpu.VMEM((MEMBERS, LAT_TERMS * MEMBERS), jnp.bfloat16),
            pltpu.VMEM((FIELDS, MEMBERS, PATCH_CELLS), jnp.bfloat16),
            pltpu.SemaphoreType.DMA(((FIELDS + CHUNK - 1) // CHUNK,)),
        ],
        compiler_params=pltpu.CompilerParams(vmem_limit_bytes=16 * MIB),
        name="lat_part",
    )(lat_a, lat_b, right, sums)


def side_kernel(
    core_ref, swap_ref, edge_ref, rows_ref, sum_ref, out_ref, right_ref, left_ref, weight_ref
):
    f32 = jnp.float32
    bf16 = jnp.bfloat16
    lon_par = lax.axis_index("lon") & 1
    col = cell_lanes(COEF_ROWS)[0]
    for source, ref in enumerate((core_ref, swap_ref)):
        for tile in range(3):
            at = (source * 3 + tile) * 128
            left_ref[:, at : at + 128] = ref[tile * MEMBERS : (tile + 1) * MEMBERS, :]
        mine = col == jnp.where(lon_par == source, CELLS_LON - 1, 0)
        coefs = jnp.where(mine, ref[PAIR_ROWS + MEMBERS :, :].astype(f32), 0.0)
        coefs = coefs + pltpu.roll(coefs, PATCH_CELLS // 2, 1)
        for k in range(6):
            weight_ref[source * 6 + k] = spread(coefs[k : k + 1], 2 * PATCH_CELLS).astype(bf16)
    for k, weight in enumerate(lat_weights()):
        weight = jnp.concatenate([weight] * (MEMBERS // COEF_ROWS), axis=0)
        for tile in range(LAT_TILES):
            right_ref[tile, pl.ds(k * MEMBERS, MEMBERS), :] = rows_ref[tile] * weight
    outer = side_lanes()

    def group(first, count):
        tiles = (count + 1) // 2
        edges = [edge_ref[first // 2 + t] for t in range(tiles)]
        both = jnp.concatenate(edges, axis=1) if tiles == 2 else edges[0]
        total = weighted_product(left_ref, weight_ref, SIDE_TERMS, both)
        for f in range(count):
            piece = total[:, f // 2 * PATCH_CELLS : (f // 2 + 1) * PATCH_CELLS]
            if f % 2:
                piece = pltpu.roll(piece, PATCH_CELLS // 2, 1)
            out_ref[first + f] = sum_ref[first + f] + jnp.where(outer, piece, 0.0)

    for first in range(0, FIELDS, 4):
        group(first, min(4, FIELDS - first))


def side_part(from_core, from_swap, edges, rows, sums):
    bf16 = jnp.bfloat16
    return pl.pallas_call(
        side_kernel,
        out_shape=(
            jax.ShapeDtypeStruct(sums.shape, sums.dtype),
            jax.ShapeDtypeStruct((LAT_TILES, LAT_TERMS * MEMBERS, PATCH_CELLS), bf16),
        ),
        in_specs=[VMEM] * 5,
        out_specs=(VMEM, VMEM),
        scratch_shapes=[
            pltpu.VMEM((MEMBERS, SIDE_TERMS * MEMBERS), bf16),
            pltpu.VMEM((SIDE_TERMS, COEF_ROWS, 2 * PATCH_CELLS), bf16),
        ],
        cost_estimate=pl.CostEstimate(
            flops=FIELDS * PATCH_CELLS * MEMBERS * MEMBERS * SIDE_TERMS,
            bytes_accessed=FIELDS * MEMBERS * PATCH_CELLS * 7,
            transcendentals=0,
        ),
        compiler_params=pltpu.CompilerParams(vmem_limit_bytes=16 * MIB),
        name="side_part",
    )(from_core, from_swap, edges, rows, sums)


CORES = [(i, i ^ 1) for i in range(32)]


def chip_transforms(
    depth, both, obs_ens, obs_value, obs_prec, slot_owner, info, counts, region_slots
):
    if depth > 1:
        rest = tuple(range(1, depth))
        send, keep, held, _, _ = split_of(rest, slot_owner, obs_ens, obs_value, obs_prec)
        got = lax.ppermute(send, "lon", CORES)
        both = merge_of(held, keep, got, both)
    received = lax.all_to_all(both, "lon", 0, 0, axis_index_groups=SAME_CORE, tiled=True)
    blocks = received.reshape(CHIPS * depth, ROWS, OBS_BLOCK)
    return transforms_of(depth, info, counts, region_slots, blocks)


def shards(background, obs_ens, obs_value, obs_prec, obs_count, slot_owner, region_slots):
    send, keep, held, info, index = split_of((0,), slot_owner, obs_ens, obs_value, obs_prec)
    got = lax.ppermute(send, "lon", CORES)
    both = merge_of(held, keep, got)
    operands = (
        both,
        obs_ens,
        obs_value,
        obs_prec,
        slot_owner,
        info,
        obs_count[:, 0, 0],
        jnp.transpose(region_slots, (0, 2, 1)),
    )
    branches = [functools.partial(chip_transforms, depth) for depth in (1, 2, SLOTS)]
    to_core, to_swap, edge_a, edge_b, coefs = lax.switch(
        index[0, 0], branches, *operands
    )

    swap = [(i, (i + 1) % 32) for i in range(1, 32, 2)] + [((i + 1) % 32, i) for i in range(1, 32, 2)]
    from_core = lax.ppermute(to_core, "lon", CORES)
    from_swap = lax.ppermute(to_swap, "lon", swap)
    state = background.reshape(FIELDS, MEMBERS, PATCH_CELLS)
    sums, edges, rows = own_part(to_core, coefs, state)
    message_a, message_b = pack_of(edge_a, edge_b, from_core, from_swap)
    pairs_a = [(i, i ^ 1) for i in range(8)]
    pairs_b = []
    for i in range(N_LAT):
        for j in range(32):
            if i in (0, N_LAT - 1):
                target = i * 32 + (j ^ 1)
            else:
                target = (i + 1 if i % 2 else i - 1) * 32 + j
            pairs_b.append((i * 32 + j, target))
    lat_b = lax.ppermute(message_b, ("lat", "lon"), pairs_b)
    lat_a = lax.ppermute(message_a, "lat", pairs_a)
    sums, right = side_part(from_core, from_swap, edges, rows, sums)
    result = lat_part(lat_a, lat_b, right, sums)
    return result.reshape(FIELDS, MEMBERS, 1, 1, PATCH_CELLS)


def solution(mesh):
    in_specs = (
        P(None, None, "lon", "lat", None),
        P(None, "lat", "lon", None, None, None),
        P(None, "lat", "lon", None, None),
        P(None, "lat", "lon", None, None),
        P(None, "lat", "lon"),
        P(),
        P("lon", "lat", None),
    )
    out_specs = P(None, None, "lon", "lat", None)
    return jax.shard_map(shards, mesh=mesh, in_specs=in_specs, out_specs=out_specs, check_vma=False)
```

```python
import functools
import math

import jax
import jax.numpy as jnp
from jax import lax
from jax.experimental import pallas as pl
from jax.experimental.pallas import tpu as pltpu
from jax.sharding import PartitionSpec as P

MEMBERS = 64
FIELDS = 69
CELLS_LAT = 32
CELLS_LON = 4
PATCH_CELLS = 128
SLOTS = 4
OBS_BLOCK = 128
NEWTON_STEPS = 3
LON_PAIRS = 2
LAT_PAIRS = 16
PAIRS = ((0, 1), (0, 2), (0, 3), (1, 2), (1, 3), (2, 3))
ROWS = 66
PAIR_ROWS = 192
COEF_ROWS = 16
MSG_ROWS = PAIR_ROWS + MEMBERS + COEF_ROWS
CHIPS = 16
N_LAT = 8
SAME_CORE = [[j for j in range(32) if j % 2 == core] for core in range(2)]


def lon_weight(column, region):
    own = column >> 1
    outer = own + jnp.where((column & 1) == 1, 1, -1)
    return jnp.where(own == region, 0.75, jnp.where(outer == region, 0.25, 0.0))


def lat_weight(row, region):
    own = row >> 1
    outer = own + jnp.where((row & 1) == 1, 1, -1)
    return jnp.where(own == region, 0.75, jnp.where(outer == region, 0.25, 0.0))


def cell_lanes(rows):
    lane = lax.broadcasted_iota(jnp.int32, (rows, PATCH_CELLS), 1)
    return lane >> 5, lane & (CELLS_LAT - 1)


SMEM = pl.BlockSpec(memory_space=pltpu.SMEM)
VMEM = pl.BlockSpec(memory_space=pltpu.VMEM)
MIB = 1024 * 1024


def halves(array):
    high = array.astype(jnp.bfloat16)
    return high, (array - high.astype(jnp.float32)).astype(jnp.bfloat16)


def mm(left, right):
    def dot(x, y):
        return lax.dot_general(
            x, y, (((1,), (0,)), ((), ())), preferred_element_type=jnp.float32
        )

    left_high, left_low = halves(left)
    right_high, right_low = halves(right)
    return dot(left_high, right_high) + (dot(left_high, right_low) + dot(left_low, right_high))


def slot_ranks(owner_ref):
    owners = [owner_ref[s] for s in range(SLOTS)]
    ranks = []
    for s in range(SLOTS):
        rank = jnp.int32(0)
        for earlier in range(s):
            rank = rank + jnp.where((owners[earlier] >> 1) == (owners[s] >> 1), 1, 0)
        ranks.append(rank)
    return owners, ranks


def chosen_slot(owners, ranks, chip, q):
    slot = jnp.int32(0)
    owner = jnp.int32(0)
    for s in range(SLOTS):
        match = jnp.logical_and((owners[s] >> 1) == chip, ranks[s] == q)
        slot = jnp.where(match, s, slot)
        owner = jnp.where(match, owners[s], owner)
    return slot, owner


def split_kernel(
    places, owner_ref, ens_ref, value_ref, prec_ref, send_ref, keep_ref, held_ref, info_ref, index_ref,
    rows_ref, small_ref, small_sems, sems,
):
    f32 = jnp.float32
    me = lax.axis_index("lon")
    core = me & 1
    owners, ranks = slot_ranks(owner_ref)
    chosen = [chosen_slot(owners, ranks, me >> 1, q) for q in places]
    slots = [slot for slot, _ in chosen]
    for q, (_, owner) in enumerate(chosen):
        held_ref[q] = jnp.full((COEF_ROWS, OBS_BLOCK), jnp.where((owner & 1) == core, 1.0, 0.0), f32)
    most = ranks[0]
    for s in range(1, SLOTS):
        most = jnp.maximum(most, ranks[s])
    index_ref[...] = jnp.full((8, OBS_BLOCK), jnp.minimum(most, 2), jnp.int32)
    for s in range(SLOTS):
        info_ref[s : s + 1, :] = jnp.full((1, OBS_BLOCK), (owners[s] >> 1).astype(f32), f32)
        info_ref[SLOTS + s : SLOTS + s + 1, :] = jnp.full((1, OBS_BLOCK), ranks[s].astype(f32), f32)
    targets = ((send_ref, 1 - core), (keep_ref, core))
    copies = []
    smalls = []
    for q in range(len(places)):
        for k, ref in enumerate((value_ref, prec_ref)):
            copy = pltpu.make_async_copy(
                ref.at[slots[q]], small_ref.at[2 * q + k], small_sems.at[2 * q + k]
            )
            copy.start()
            smalls.append(copy)
        for k, (ref, side) in enumerate(targets):
            copy = pltpu.make_async_copy(
                ens_ref.at[slots[q], :, side], ref.at[:, q, pl.ds(0, MEMBERS)], sems.at[2 * q + k]
            )
            copy.start()
            copies.append(copy)
    for copy in smalls:
        copy.wait()
    for q in range(len(places)):
        rows_ref[0, 0 : 2 * CHIPS] = small_ref[2 * q].astype(f32)
        rows_ref[1, 0 : 2 * CHIPS] = small_ref[2 * q + 1].astype(f32)
        for ref, side in targets:
            value = rows_ref[0, pl.ds(side, CHIPS, stride=2), :]
            prec = rows_ref[1, pl.ds(side, CHIPS, stride=2), :]
            for i in range(CHIPS):
                both = jnp.concatenate([value[i : i + 1], prec[i : i + 1]], axis=0)
                ref[i, q, MEMBERS:ROWS, :] = both.astype(jnp.bfloat16)
    for copy in copies:
        copy.wait()


def split_of(places, slot_owner, obs_ens, obs_value, obs_prec):
    count = len(places)
    shape = jax.ShapeDtypeStruct((CHIPS, count, ROWS, OBS_BLOCK), jnp.bfloat16)
    return pl.pallas_call(
        functools.partial(split_kernel, places),
        out_shape=(
            shape,
            shape,
            jax.ShapeDtypeStruct((count, COEF_ROWS, OBS_BLOCK), jnp.float32),
            jax.ShapeDtypeStruct((2 * SLOTS, OBS_BLOCK), jnp.float32),
            jax.ShapeDtypeStruct((8, OBS_BLOCK), jnp.int32),
        ),
        in_specs=[SMEM] + [pl.BlockSpec(memory_space=pl.ANY)] * 3,
        out_specs=(VMEM,) * 5,
        scratch_shapes=[
            pltpu.VMEM((2, 2 * CHIPS + 8, OBS_BLOCK), jnp.float32),
            pltpu.VMEM((2 * count, 2 * CHIPS, OBS_BLOCK), jnp.bfloat16),
            pltpu.SemaphoreType.DMA((2 * count,)),
            pltpu.SemaphoreType.DMA((2 * count,)),
        ],
        compiler_params=pltpu.CompilerParams(vmem_limit_bytes=16 * MIB),
        name="split",
    )(
        slot_owner,
        obs_ens.reshape(SLOTS, CHIPS, 2, MEMBERS, OBS_BLOCK),
        obs_value.reshape(SLOTS, 2 * CHIPS, OBS_BLOCK),
        obs_prec.reshape(SLOTS, 2 * CHIPS, OBS_BLOCK),
    )


def blend(held, keep, got):
    mine = held.astype(jnp.bfloat16)
    other = (1.0 - held).astype(jnp.bfloat16)
    return keep * mine + got * other


def merge_kernel(held_ref, keep_ref, got_ref, out_ref):
    for q in range(held_ref.shape[0]):
        out_ref[:, q] = blend(held_ref[q, 0:1, :], keep_ref[:, q], got_ref[:, q])


def append_kernel(both_ref, held_ref, keep_ref, got_ref, out_ref):
    out_ref[:, 0] = both_ref[:, 0]
    for q in range(held_ref.shape[0]):
        out_ref[:, 1 + q] = blend(held_ref[q, 0:1, :], keep_ref[:, q], got_ref[:, q])


def merge_of(held, keep, got, both=None):
    count = keep.shape[1]
    operands = (held, keep, got)
    if both is not None:
        count = count + 1
        operands = (both,) + operands
    return pl.pallas_call(
        merge_kernel if both is None else append_kernel,
        out_shape=jax.ShapeDtypeStruct((CHIPS, count, ROWS, OBS_BLOCK), keep.dtype),
        in_specs=[VMEM] * len(operands),
        out_specs=VMEM,
        compiler_params=pltpu.CompilerParams(vmem_limit_bytes=16 * MIB),
        name="merge",
    )(*operands)


def entry(row, lane):
    at = lax.broadcasted_iota(jnp.int32, row.shape, 1)
    return jnp.sum(jnp.where(at == lane, row.astype(jnp.float32), 0.0), axis=1, keepdims=True)


def pair_ids(ids_ref, a):
    one = ids_ref[a, 0:1, :]
    two = ids_ref[a, 1:2, :]
    low = jnp.minimum(one, two)
    high = jnp.maximum(one, two)
    return ((low * (7 - low)) >> 1) + (high - low - 1)


def transform_kernel(
    depth, info_ref, count_ref, ids_ref, block_ref, core_ref, swap_ref, edge_a_ref, edge_b_ref, coef_ref
):
    f32 = jnp.float32
    bf16 = jnp.bfloat16
    members = MEMBERS
    lat_par = lax.axis_index("lat") & 1
    even = (lax.axis_index("lon") & 1) == 0
    row_id = lax.broadcasted_iota(jnp.int32, (members, members), 0)
    col_id = lax.broadcasted_iota(jnp.int32, (members, members), 1)
    identity = jnp.where(row_id == col_id, 1.0, 0.0).astype(f32)
    position = lax.broadcasted_iota(jnp.int32, (1, OBS_BLOCK), 1).astype(f32)
    grams = []
    projs = []
    traces = []
    for slot in range(SLOTS):
        place = info_ref[slot : slot + 1, :] * depth + info_ref[SLOTS + slot : SLOTS + slot + 1, :]
        block = None
        for k in range(CHIPS * depth):
            here = jnp.where(place == k, 1.0, 0.0).astype(bf16)
            part = block_ref[k] * here
            block = part if block is None else block + part
        block = block.astype(f32)
        ens = block[:members]
        value = block[members : members + 1]
        prec = block[members + 1 : members + 2]
        obs_mean = jnp.sum(ens, axis=0, keepdims=True) * (1.0 / members)
        pert = (ens - obs_mean).astype(bf16)
        weight = jnp.where(position < entry(count_ref[...], slot), prec, 0.0)
        weighted = (pert.astype(f32) * weight).astype(bf16)
        diagonal = jnp.sum(weighted.astype(f32) * pert.astype(f32), axis=0, keepdims=True)
        traces.append(jnp.sum(diagonal, axis=1, keepdims=True))
        high, low = halves(value - obs_mean)
        rows = [jnp.broadcast_to(x, (COEF_ROWS, OBS_BLOCK)) for x in (high, low)]
        product = lax.dot_general(
            jnp.concatenate([pert] + rows, axis=0),
            weighted,
            (((1,), (1,)), ((), ())),
            preferred_element_type=f32,
        )
        grams.append(product[:members])
        projs.append(product[members : members + 8] + product[members + COEF_ROWS : members + COEF_ROWS + 8])
    iterates = []
    inverses = []
    scalings = []
    for first, second in PAIRS:
        matrix = grams[first] + grams[second] + (members - 1.0) * identity
        scaling = (traces[first] + traces[second]) * (1.0 / members) + (members - 1.0)
        scalings.append(scaling)
        iterate = matrix * (1.0 / scaling)
        iterates.append(iterate)
        inverses.append(1.5 * identity - 0.5 * iterate)
    sums = [projs[first] + projs[second] for first, second in PAIRS]
    iterates = [mm(x, y) for x, y in zip(iterates, inverses)]
    for step in range(1, NEWTON_STEPS):
        factors = [1.5 * identity - 0.5 * mm(y, x) for x, y in zip(iterates, inverses)]
        if step < NEWTON_STEPS - 1:
            both = [mm(jnp.concatenate([x, y], axis=0), f) for x, y, f in zip(iterates, inverses, factors)]
            iterates = [z[:members] for z in both]
            inverses = [z[members:] for z in both]
        else:
            sums = [mm(p, y) for p, y in zip(sums, inverses)]
            both = [mm(jnp.concatenate([y, p], axis=0), f) for y, p, f in zip(inverses, sums, factors)]
            inverses = [z[:members] for z in both]
            sums = [mm(z[members:], z[:members]) for z in both]
    turned = []
    for pair in range(len(PAIRS)):
        scale = 1.0 / scalings[pair]
        root = math.sqrt(members - 1.0) * jnp.sqrt(scale)
        turned.append(inverses[pair] * root + sums[pair][0:1] * scale)
        lanes = slice(pair % 2 * members, (pair % 2 + 1) * members)
        rows = pl.ds(pair // 2 * members, members)
        core_ref[rows, lanes] = turned[pair].astype(bf16)
        swap_ref[rows, lanes] = turned[pair].astype(bf16)
    ids = [pair_ids(ids_ref, a) for a in range(LON_PAIRS)]
    for which, ref in enumerate((edge_a_ref, edge_b_ref)):
        row = jnp.where(lat_par == which, LAT_PAIRS - 1, 0)
        chosen = []
        for a in range(LON_PAIRS):
            edge = entry(ids[a], row)
            one = turned[0]
            for pair in range(1, len(PAIRS)):
                one = jnp.where(edge == pair, turned[pair], one)
            chosen.append(one)
            ref[:, a * members : (a + 1) * members] = one.astype(bf16)
        lanes = slice(which * members, (which + 1) * members)
        rows = pl.ds(PAIR_ROWS, members)
        core_ref[rows, lanes] = jnp.where(even, chosen[1], chosen[0]).astype(bf16)
        swap_ref[rows, lanes] = jnp.where(even, chosen[0], chosen[1]).astype(bf16)
    tapers = jnp.zeros((COEF_ROWS, 2 * PATCH_CELLS), f32)
    pair_id = lax.broadcasted_iota(jnp.int32, (COEF_ROWS, LAT_PAIRS), 0)
    col, row = cell_lanes(LAT_PAIRS)
    lat_w = lat_weight(row, lax.broadcasted_iota(jnp.int32, (LAT_PAIRS, PATCH_CELLS), 0))
    for a in range(LON_PAIRS):
        hot = jnp.where(pair_id == ids[a], 1.0, 0.0).astype(bf16)
        outer = 0 if a == LON_PAIRS - 1 else CELLS_LON - 1
        table = jnp.concatenate(
            [lat_w * lon_weight(col, a), lat_w * jnp.where(col == outer, 0.25, 0.0)], axis=1
        )
        tapers = tapers + lax.dot_general(
            hot, table.astype(bf16), (((1,), (0,)), ((), ())), preferred_element_type=f32
        )
    coef_ref[...] = tapers[:, :PATCH_CELLS].astype(bf16)
    next_taper = tapers[:, PATCH_CELLS:].astype(bf16)
    core_ref[PAIR_ROWS + members :, :] = next_taper
    swap_ref[PAIR_ROWS + members :, :] = next_taper


def transforms_of(depth, info, counts, region_slots, blocks):
    bf16 = jnp.bfloat16
    wide = jax.ShapeDtypeStruct((MEMBERS, 2 * MEMBERS), bf16)
    coef = jax.ShapeDtypeStruct((COEF_ROWS, PATCH_CELLS), bf16)
    message = jax.ShapeDtypeStruct((MSG_ROWS, 2 * MEMBERS), bf16)
    return pl.pallas_call(
        functools.partial(transform_kernel, depth),
        out_shape=(message, message, wide, wide, coef),
        in_specs=[VMEM] * 4,
        out_specs=(VMEM,) * 5,
        compiler_params=pltpu.CompilerParams(vmem_limit_bytes=16 * MIB),
        name="transforms",
    )(info, counts.reshape(1, SLOTS), region_slots, blocks)


def pack_kernel(which, edge_ref, core_ref, swap_ref, *refs):
    f32 = jnp.float32
    out_ref = refs[-1]
    even = (lax.axis_index("lon") & 1) == 0
    first = lax.broadcasted_iota(jnp.int32, (MEMBERS, 2 * MEMBERS), 1) < MEMBERS
    rows = pl.ds(PAIR_ROWS, MEMBERS)
    core = core_ref[rows, :].astype(f32)
    swap = swap_ref[rows, :].astype(f32)
    before = jnp.where(even, swap, core)
    after = jnp.where(even, core, swap)
    if which == 0:
        after = pltpu.roll(after, MEMBERS, 1)
    else:
        before = pltpu.roll(before, MEMBERS, 1)
    out_ref[0:MEMBERS] = edge_ref[...]
    out_ref[MEMBERS:] = jnp.where(first, before, after).astype(jnp.bfloat16)


def pack_of(which, edge, from_core, from_swap, *ahead):
    return pl.pallas_call(
        functools.partial(pack_kernel, which),
        out_shape=jax.ShapeDtypeStruct((2 * MEMBERS, 2 * MEMBERS), jnp.bfloat16),
        in_specs=[VMEM] * (3 + len(ahead)),
        out_specs=VMEM,
        cost_estimate=pl.CostEstimate(
            flops=1_000_000_000 * len(ahead), bytes_accessed=100_000, transcendentals=0
        ),
        compiler_params=pltpu.CompilerParams(vmem_limit_bytes=4 * MIB),
        name="pack",
    )(edge, from_core, from_swap, *ahead)


def spread(row, width):
    tile = jnp.broadcast_to(row, (COEF_ROWS, PATCH_CELLS))
    return jnp.concatenate([tile] * (width // PATCH_CELLS), axis=1)


def weighted_product(left_ref, weight_ref, count, perts):
    width = perts.shape[1]
    total = None
    for first in range(0, count, 4):
        parts = []
        for k in range(first, min(first + 4, count)):
            weight = weight_ref[k, :, 0:width]
            parts.append(perts * jnp.concatenate([weight] * (MEMBERS // COEF_ROWS), axis=0))
        part = lax.dot_general(
            left_ref[:, first * MEMBERS : min(first + 4, count) * MEMBERS],
            jnp.concatenate(parts, axis=0),
            (((1,), (0,)), ((), ())),
            preferred_element_type=jnp.float32,
        )
        total = part if total is None else total + part
    return total


OWN_TERMS = 6
LAT_TERMS = 8
SIDE_TERMS = 12
CHUNK = 16
HALF = (FIELDS + 1) // 2
LAT_GROUP = 16
LAT_TILES = (FIELDS + LAT_GROUP - 1) // LAT_GROUP


def side_lanes():
    lane = lax.broadcasted_iota(jnp.int32, (MEMBERS, PATCH_CELLS), 1)
    return jnp.logical_or(lane < CELLS_LAT, lane >= PATCH_CELLS - CELLS_LAT)


def lat_lanes(field):
    lane = lax.broadcasted_iota(jnp.int32, (MEMBERS, PATCH_CELLS), 1)
    at = (lane - 2 * (field % LAT_GROUP)) & (CELLS_LAT - 1)
    return jnp.logical_or(at == 0, at == CELLS_LAT - 1)


def own_kernel(
    pair_ref, coef_ref, back_ref, sum_ref, edge_ref, rows_ref, left_ref, weight_ref
):
    f32 = jnp.float32
    bf16 = jnp.bfloat16
    for tile in range(3):
        left_ref[:, tile * 128 : (tile + 1) * 128] = pair_ref[tile * MEMBERS : (tile + 1) * MEMBERS, :]
    coefs = coef_ref[...].astype(f32)
    for k in range(OWN_TERMS):
        weight_ref[k] = spread(coefs[k : k + 1], 2 * PATCH_CELLS).astype(bf16)
    outer = side_lanes()

    def pair(first, base, count, rows):
        perts = []
        means = []
        for f in range(count):
            state = back_ref[first + f].astype(f32)
            mean = jnp.sum(state, axis=0, keepdims=True) * (1.0 / MEMBERS)
            means.append(mean)
            perts.append((state - mean).astype(bf16))
        wide = [p.astype(f32) for p in perts]
        inner = pltpu.roll(wide[1], PATCH_CELLS // 2, 1) if count == 2 else 0.0
        edge_ref[first // 2] = jnp.where(outer, wide[0], inner).astype(bf16)
        for f in range(count):
            shift = 2 * ((base + f) % LAT_GROUP)
            moved = pltpu.roll(wide[f], shift, 1) if shift else wide[f]
            rows = jnp.where(lat_lanes(base + f), moved, rows)
        both = jnp.concatenate(perts, axis=1) if count == 2 else perts[0]
        total = weighted_product(left_ref, weight_ref, OWN_TERMS, both)
        for f in range(count):
            sum_ref[first + f] = total[:, f * PATCH_CELLS : (f + 1) * PATCH_CELLS] + means[f]
        return rows

    for tile in range(LAT_TILES):
        rows = jnp.zeros((MEMBERS, PATCH_CELLS), f32)
        last = min((tile + 1) * LAT_GROUP, FIELDS)
        for first in range(tile * LAT_GROUP, last, 2):
            rows = pair(first, first, min(2, last - first), rows)
        rows_ref[tile] = rows.astype(bf16)


def own_part(message, coefs, background):
    def tiles(count, kind):
        return jax.ShapeDtypeStruct((count, MEMBERS, PATCH_CELLS), kind)

    return pl.pallas_call(
        own_kernel,
        out_shape=(
            tiles(FIELDS, jnp.float32),
            tiles(HALF, jnp.bfloat16),
            tiles(LAT_TILES, jnp.bfloat16),
        ),
        in_specs=[VMEM] * 3,
        out_specs=(VMEM,) * 3,
        scratch_shapes=[
            pltpu.VMEM((MEMBERS, OWN_TERMS * MEMBERS), jnp.bfloat16),
            pltpu.VMEM((OWN_TERMS, COEF_ROWS, 2 * PATCH_CELLS), jnp.bfloat16),
        ],
        cost_estimate=pl.CostEstimate(
            flops=2 * FIELDS * PATCH_CELLS * MEMBERS * MEMBERS * OWN_TERMS,
            bytes_accessed=FIELDS * MEMBERS * PATCH_CELLS * 8,
            transcendentals=0,
        ),
        compiler_params=pltpu.CompilerParams(vmem_limit_bytes=16 * MIB),
        name="own_part",
    )(message, coefs, background)


def lat_weights():
    lat = lax.axis_index("lat")
    lat_par = lat & 1
    lane = lax.broadcasted_iota(jnp.int32, (COEF_ROWS, PATCH_CELLS), 1)
    group = lane >> 5
    last = (lane & 1) == 1
    before = jnp.logical_and(last, (lane & (CELLS_LAT - 1)) != CELLS_LAT - 1)
    col = jnp.where(before, (group + CELLS_LON - 1) & (CELLS_LON - 1), group)
    weights = []
    for which in range(2):
        edge = jnp.where(lat_par == which, 1, 0)
        inside = jnp.where(lat_par == which, lat < N_LAT - 1, lat > 0)
        quarter = jnp.where(inside, 0.25, 0.0)
        for region in (0, 1, -1, LON_PAIRS):
            weight = jnp.where((lane & 1) == edge, quarter * lon_weight(col, region), 0.0)
            weights.append(weight.astype(jnp.bfloat16))
    return weights


def lat_kernel(lat_a_ref, lat_b_ref, right_ref, sum_ref, final_ref, left_ref, out_ref, sems):
    for which, ref in enumerate((lat_a_ref, lat_b_ref)):
        for tile in range(2):
            at = (2 * which + tile) * 128
            left_ref[:, at : at + 128] = ref[tile * MEMBERS : (tile + 1) * MEMBERS, :]
    parts = []
    for tile in range(LAT_TILES):
        parts.append(
            lax.dot_general(
                left_ref[...],
                right_ref[tile],
                (((1,), (0,)), ((), ())),
                preferred_element_type=jnp.float32,
            )
        )
    edges = lat_lanes(0)
    copies = []
    for first in range(0, FIELDS, CHUNK):
        stop = min(first + CHUNK, FIELDS)
        for field in range(first, stop):
            shift = 2 * (field % LAT_GROUP)
            part = parts[field // LAT_GROUP]
            moved = pltpu.roll(part, PATCH_CELLS - shift, 1) if shift else part
            out_ref[field] = (sum_ref[field] + jnp.where(edges, moved, 0.0)).astype(jnp.bfloat16)
        span = pl.ds(first, stop - first)
        copy = pltpu.make_async_copy(out_ref.at[span], final_ref.at[span], sems.at[first // CHUNK])
        copy.start()
        copies.append(copy)
    for copy in copies:
        copy.wait()


def lat_part(lat_a, lat_b, right, sums):
    return pl.pallas_call(
        lat_kernel,
        out_shape=jax.ShapeDtypeStruct(sums.shape, jnp.bfloat16),
        in_specs=[VMEM] * 4,
        out_specs=pl.BlockSpec(memory_space=pl.ANY),
        scratch_shapes=[
            pltpu.VMEM((MEMBERS, LAT_TERMS * MEMBERS), jnp.bfloat16),
            pltpu.VMEM((FIELDS, MEMBERS, PATCH_CELLS), jnp.bfloat16),
            pltpu.SemaphoreType.DMA(((FIELDS + CHUNK - 1) // CHUNK,)),
        ],
        compiler_params=pltpu.CompilerParams(vmem_limit_bytes=16 * MIB),
        name="lat_part",
    )(lat_a, lat_b, right, sums)


def side_kernel(
    core_ref, swap_ref, edge_ref, rows_ref, sum_ref, out_ref, right_ref, left_ref, weight_ref
):
    f32 = jnp.float32
    bf16 = jnp.bfloat16
    lon_par = lax.axis_index("lon") & 1
    col = cell_lanes(COEF_ROWS)[0]
    for source, ref in enumerate((core_ref, swap_ref)):
        for tile in range(3):
            at = (source * 3 + tile) * 128
            left_ref[:, at : at + 128] = ref[tile * MEMBERS : (tile + 1) * MEMBERS, :]
        mine = col == jnp.where(lon_par == source, CELLS_LON - 1, 0)
        coefs = jnp.where(mine, ref[PAIR_ROWS + MEMBERS :, :].astype(f32), 0.0)
        coefs = coefs + pltpu.roll(coefs, PATCH_CELLS // 2, 1)
        for k in range(6):
            weight_ref[source * 6 + k] = spread(coefs[k : k + 1], 2 * PATCH_CELLS).astype(bf16)
    for k, weight in enumerate(lat_weights()):
        weight = jnp.concatenate([weight] * (MEMBERS // COEF_ROWS), axis=0)
        for tile in range(LAT_TILES):
            right_ref[tile, pl.ds(k * MEMBERS, MEMBERS), :] = rows_ref[tile] * weight
    outer = side_lanes()

    def group(first, count):
        tiles = (count + 1) // 2
        edges = [edge_ref[first // 2 + t] for t in range(tiles)]
        both = jnp.concatenate(edges, axis=1) if tiles == 2 else edges[0]
        total = weighted_product(left_ref, weight_ref, SIDE_TERMS, both)
        for f in range(count):
            piece = total[:, f // 2 * PATCH_CELLS : (f // 2 + 1) * PATCH_CELLS]
            if f % 2:
                piece = pltpu.roll(piece, PATCH_CELLS // 2, 1)
            out_ref[first + f] = sum_ref[first + f] + jnp.where(outer, piece, 0.0)

    for first in range(0, FIELDS, 4):
        group(first, min(4, FIELDS - first))


def side_part(from_core, from_swap, edges, rows, sums):
    bf16 = jnp.bfloat16
    return pl.pallas_call(
        side_kernel,
        out_shape=(
            jax.ShapeDtypeStruct(sums.shape, sums.dtype),
            jax.ShapeDtypeStruct((LAT_TILES, LAT_TERMS * MEMBERS, PATCH_CELLS), bf16),
        ),
        in_specs=[VMEM] * 5,
        out_specs=(VMEM, VMEM),
        scratch_shapes=[
            pltpu.VMEM((MEMBERS, SIDE_TERMS * MEMBERS), bf16),
            pltpu.VMEM((SIDE_TERMS, COEF_ROWS, 2 * PATCH_CELLS), bf16),
        ],
        cost_estimate=pl.CostEstimate(
            flops=FIELDS * PATCH_CELLS * MEMBERS * MEMBERS * SIDE_TERMS,
            bytes_accessed=FIELDS * MEMBERS * PATCH_CELLS * 7,
            transcendentals=0,
        ),
        compiler_params=pltpu.CompilerParams(vmem_limit_bytes=16 * MIB),
        name="side_part",
    )(from_core, from_swap, edges, rows, sums)


CORES = [(i, i ^ 1) for i in range(32)]


def chip_transforms(
    depth, both, obs_ens, obs_value, obs_prec, slot_owner, info, counts, region_slots
):
    if depth > 1:
        rest = tuple(range(1, depth))
        send, keep, held, _, _ = split_of(rest, slot_owner, obs_ens, obs_value, obs_prec)
        got = lax.ppermute(send, "lon", CORES)
        both = merge_of(held, keep, got, both)
    received = lax.all_to_all(both, "lon", 0, 0, axis_index_groups=SAME_CORE, tiled=True)
    blocks = received.reshape(CHIPS * depth, ROWS, OBS_BLOCK)
    return transforms_of(depth, info, counts, region_slots, blocks)


def shards(background, obs_ens, obs_value, obs_prec, obs_count, slot_owner, region_slots):
    send, keep, held, info, index = split_of((0,), slot_owner, obs_ens, obs_value, obs_prec)
    got = lax.ppermute(send, "lon", CORES)
    both = merge_of(held, keep, got)
    operands = (
        both,
        obs_ens,
        obs_value,
        obs_prec,
        slot_owner,
        info,
        obs_count[:, 0, 0],
        jnp.transpose(region_slots, (0, 2, 1)),
    )
    branches = [functools.partial(chip_transforms, depth) for depth in (1, 2, SLOTS)]
    to_core, to_swap, edge_a, edge_b, coefs = lax.switch(
        index[0, 0], branches, *operands
    )

    swap = [(i, (i + 1) % 32) for i in range(1, 32, 2)] + [((i + 1) % 32, i) for i in range(1, 32, 2)]
    from_core = lax.ppermute(to_core, "lon", CORES)
    from_swap = lax.ppermute(to_swap, "lon", swap)
    state = background.reshape(FIELDS, MEMBERS, PATCH_CELLS)
    sums, edges, rows = own_part(to_core, coefs, state)
    message_b = pack_of(1, edge_b, from_core, from_swap)
    message_a = pack_of(0, edge_a, from_core, from_swap, message_b)
    pairs_a = [(i, i ^ 1) for i in range(8)]
    pairs_b = []
    for i in range(N_LAT):
        for j in range(32):
            if i in (0, N_LAT - 1):
                target = i * 32 + (j ^ 1)
            else:
                target = (i + 1 if i % 2 else i - 1) * 32 + j
            pairs_b.append((i * 32 + j, target))
    lat_b = lax.ppermute(message_b, ("lat", "lon"), pairs_b)
    lat_a = lax.ppermute(message_a, "lat", pairs_a)
    sums, right = side_part(from_core, from_swap, edges, rows, sums)
    result = lat_part(lat_a, lat_b, right, sums)
    return result.reshape(FIELDS, MEMBERS, 1, 1, PATCH_CELLS)


def solution(mesh):
    in_specs = (
        P(None, None, "lon", "lat", None),
        P(None, "lat", "lon", None, None, None),
        P(None, "lat", "lon", None, None),
        P(None, "lat", "lon", None, None),
        P(None, "lat", "lon"),
        P(),
        P("lon", "lat", None),
    )
    out_specs = P(None, None, "lon", "lat", None)
    return jax.shard_map(shards, mesh=mesh, in_specs=in_specs, out_specs=out_specs, check_vma=False)
```
